32 devices in a mesh: dp: 4 (over z), row: 4 (over y, x), col: 2 (over core).
Axes of the slice: x: 2, y: 2, z: 4, core: 2. Of those that a mesh axis runs over, the one named last changes fastest.
Arguments:
- hidden: bfloat16 [16, 1024, 2048], P('dp', 'row', 'col'), may hold values from -6 to 6
- targets: bfloat16 [16, 1024, 2048], P('dp', 'row', 'col'), may hold values from -6 to 6
- lengths: int32 [16], replicated, may hold values from 256 to 1024, as said below
- dest_group: int32 [16], P('dp'), may hold values from 0 to 3, as said below
- norm_gain: float32 [2048], P('col'), may hold values from 0.1 to 1.9
- gate_input_weight: bfloat16 [2048, 64, 128], P('col', 'row'), may hold values from -0.125 to 0.125
- auxiliary_weight: bfloat16 [2048, 320], P('col'), may hold values from -0.125 to 0.125
- conv_x: float32 [4, 64, 64], P(None, 'row'), may hold values from -0.5 to 0.5
- conv_x_bias: float32 [64, 64], P('row'), may hold values from -0.5 to 0.5
- conv_bc: float32 [4, 256], replicated, may hold values from -0.5 to 0.5
- conv_bc_bias: float32 [256], replicated, may hold values from -0.5 to 0.5
- dt_bias: float32 [64], P('row'), may hold values from -6 to -2.5
- a_log: float32 [64], P('row'), may hold values from 0 to 2.77
- d_skip: float32 [64], P('row'), may hold values from 0.5 to 1.5
- out_gain: float32 [64, 64], P('row'), may hold values from 0.1 to 1.9
- output_weight: bfloat16 [64, 64, 2048], P('row', None, 'col'), may hold values from -0.09375 to 0.09375
Outputs:
- loss: float32 [], replicated
- output: bfloat16 [16, 1024, 2048], P('dp', 'row', 'col')
- hidden_grad: bfloat16 [16, 1024, 2048], P('dp', 'row', 'col')
- norm_gain_grad: float32 [2048], P('col')
- w_zx_grad: float32 [2048, 64, 128], P('col', 'row')
- w_aux_grad: float32 [2048, 320], P('col')
- conv_x_grad: float32 [4, 64, 64], P(None, 'row')
- conv_x_bias_grad: float32 [64, 64], P('row')
- conv_bc_grad: float32 [4, 256], replicated
- conv_bc_bias_grad: float32 [256], replicated
- dt_bias_grad: float32 [64], P('row')
- a_log_grad: float32 [64], P('row')
- d_skip_grad: float32 [64], P('row')
- out_gain_grad: float32 [64, 64], P('row')
- w_out_grad: float32 [64, 64, 2048], P('row', None, 'col')
The draws below stay inside these ranges and needn't reach their ends.
Inputs may be any that keep to these rules, and one draw needn't show every extreme that they name: `lengths`: in every block of 4 dealt sequences (one data group) one sequence has length 1024 and one has length 256. `dest_group`: in every block of 4 consecutive sequences of the given order every group number occurs exactly once.
All inputs are finite; a program needn't handle non-finite values.
Results may differ from the reference program's by a relative error of at most 0.0091.
Values may be sent and summed in bfloat16 or wider, within the bound.
No kernel may reach another device: no remote copies, remote signals or barrier semaphores. Data moves between devices by JAX's collectives and lax.ppermute only.
A program may use at most 320 MiB of HBM per device.

```python
import math
import jax
import jax.numpy as jnp
from jax import lax

D = 2048
H = 64
P_SIZE = 64
N = 128
CONVK = 4
CH = 256
LEN = 1024
SEQ_GRP = 4
SEQS = 16
TOKENS = 16384
N_ROW = 4


def shuffle_block(subkey):
    return jax.random.permutation(subkey, SEQ_GRP)


def draw_lengths(key, part):
    key = jax.random.fold_in(key, 11)
    first_key, second_key = jax.random.split(key, 2)
    group_count = SEQS // SEQ_GRP
    values = jax.random.randint(first_key, (group_count, SEQ_GRP), LEN // 4, LEN + 1)
    orders = jax.vmap(shuffle_block)(jax.random.split(second_key, group_count))
    slots = jnp.arange(SEQ_GRP, dtype=jnp.int32)[None, :]
    longest = slots == orders[:, 0:1]
    shortest = slots == orders[:, 1:2]
    values = jnp.where(longest, LEN, jnp.where(shortest, LEN // 4, values))
    return values.reshape(SEQS).astype(jnp.int32)


def draw_dest_group(key, part):
    key = jax.random.fold_in(key, 23)
    group_count = SEQS // SEQ_GRP
    orders = jax.vmap(shuffle_block)(jax.random.split(key, group_count))
    return orders.reshape(SEQS).astype(jnp.int32)


def block_levels(own_key, dims, shards, least, high):
    gain, own = 1.0, jax.random.fold_in(own_key, 6)
    for dim, parts in shards:
        draws = jnp.exp(jax.random.uniform(jax.random.fold_in(own, dim), (parts,), jnp.float32, least / len(shards), high / len(shards)))
        gain = gain * jnp.repeat(draws, dims[dim] // parts).reshape([-1 if axis == dim else 1 for axis in range(len(dims))])
    return gain


def bell_draw(key, shape, deviation, bound, cuts=(), held_as=jnp.bfloat16):
    array = deviation * jax.random.normal(key, shape, jnp.float32)
    if cuts:
        array = array * block_levels(key, shape, cuts, -0.22, 0.18)
    return jnp.clip(array, -bound, bound).astype(held_as)


def setup_inputs(seed: int = 0) -> dict:
    key_of = jax.random.split(jax.random.key(seed), 17)
    return {
        "hidden": bell_draw(key_of[0], (SEQS, LEN, D), 1.0, 6.0, ((0, 4), (1, 4), (2, 2))),
        "targets": bell_draw(key_of[1], (SEQS, LEN, D), 1.0, 6.0, ((0, 4), (1, 4), (2, 2))),
        "lengths": draw_lengths(jax.random.fold_in(key_of[16], 71), 0),
        "dest_group": draw_dest_group(jax.random.fold_in(key_of[16], 71), 0),
        "norm_gain": jnp.clip(1.0 + 0.18 * jax.random.normal(key_of[4], (D,), jnp.float32), 0.1, 1.9),
        "gate_input_weight": bell_draw(key_of[5], (D, H, 2 * P_SIZE), D ** -0.5, 0.125, ((0, 2), (1, 4))),
        "auxiliary_weight": bell_draw(key_of[6], (D, 2 * N + H), D ** -0.5, 0.125, ((0, 2),)),
        "conv_x": jnp.clip(jax.random.uniform(key_of[7], (CONVK, H, P_SIZE), jnp.float32, -0.5, 0.5) * block_levels(key_of[7], (CONVK, H, P_SIZE), ((1, 4),), -0.4, 0.0), -0.5, 0.5),
        "conv_x_bias": jnp.clip(jax.random.uniform(key_of[8], (H, P_SIZE), jnp.float32, -0.5, 0.5) * block_levels(key_of[8], (H, P_SIZE), ((0, 4),), -0.4, 0.0), -0.5, 0.5),
        "conv_bc": jnp.clip(jax.random.uniform(key_of[9], (CONVK, 2 * N), jnp.float32, -0.5, 0.5), -0.5, 0.5),
        "conv_bc_bias": jnp.clip(jax.random.uniform(key_of[10], (2 * N,), jnp.float32, -0.5, 0.5), -0.5, 0.5),
        "dt_bias": jnp.clip(-6.0 + 3.5 * jax.random.uniform(key_of[11], (H,), jnp.float32) ** block_levels(key_of[11], (H,), ((0, 4),), -0.2, 0.2), -6.0, -2.5),
        "a_log": jnp.clip(2.77 * jax.random.uniform(key_of[12], (H,), jnp.float32) ** block_levels(key_of[12], (H,), ((0, 4),), -0.2, 0.2), 0.0, 2.77),
        "d_skip": jnp.clip(0.5 + 1.0 * jax.random.uniform(key_of[13], (H,), jnp.float32) ** block_levels(key_of[13], (H,), ((0, 4),), -0.2, 0.2), 0.5, 1.5),
        "out_gain": jnp.clip(1.0 + 0.18 * jax.random.normal(key_of[14], (H, P_SIZE), jnp.float32), 0.1, 1.9),
        "output_weight": bell_draw(key_of[15], (H, P_SIZE, D), (H * P_SIZE) ** -0.5, 0.09375, ((0, 4), (2, 2))),
    }


EPSILON = 1e-05
HIGHEST = lax.Precision.HIGHEST

@jax.custom_vjp
def low(v):
    return lax.optimization_barrier(v.astype(jnp.bfloat16)).astype(jnp.float32)

@jax.custom_vjp
def low_back(v):
    return v

def low_keep(v):
    return (low(v), None)

def low_pass(kept, grad):
    return (grad,)

def back_keep(v):
    return (v, None)

def back_low(kept, grad):
    return (low(grad),)
low.defvjp(low_keep, low_pass)
low_back.defvjp(back_keep, back_low)

def silu_fn(values):
    return values * jax.nn.sigmoid(values)

def causal_conv(values, kernel, offset):
    tap_count = kernel.shape[0]
    seq_length = values.shape[0]
    padded = jnp.pad(values, ((tap_count - 1, 0), (0, 0)))
    summed = jnp.zeros_like(values) + offset[None, :]
    for tap_index in range(tap_count):
        summed = summed + kernel[tap_index][None, :] * padded[tap_index:tap_index + seq_length]
    return summed

def ssd_sequence(x_conv, b_conv, c_conv, step_size, a_negative, skip_gain, span_len):
    seq_length, head_count, head_dim = x_conv.shape
    state_dim = b_conv.shape[1]
    block_count = seq_length // span_len
    x_blocks = x_conv.reshape(block_count, span_len, head_count, head_dim)
    b_blocks = b_conv.reshape(block_count, span_len, state_dim)
    c_blocks = c_conv.reshape(block_count, span_len, state_dim)
    step_blocks = step_size.reshape(block_count, span_len, head_count)
    causal = (jnp.arange(span_len)[:, None] >= jnp.arange(span_len)[None, :])[:, :, None]

    def block_step(carried, pieces):
        x_blk, b_blk, c_blk, step_blk = pieces
        log_decay = jnp.cumsum(step_blk * a_negative[None, :], axis=0)
        log_gaps = jnp.where(causal, log_decay[:, None, :] - log_decay[None, :, :], 0.0)
        decays = jnp.where(causal, jnp.exp(log_gaps), 0.0)
        scores = jnp.dot(c_blk, b_blk.T, precision=HIGHEST)
        mixing = decays * scores[:, :, None] * step_blk[None, :, :]
        y_inner = jnp.einsum('tsh,shp->thp', mixing, x_blk, precision=HIGHEST)
        y_carry = jnp.einsum('tn,hpn->thp', c_blk, carried, precision=HIGHEST) * jnp.exp(log_decay)[:, :, None]
        tail_scale = jnp.exp(log_decay[-1][None, :] - log_decay) * step_blk
        new_state = carried * jnp.exp(log_decay[-1])[:, None, None] + jnp.einsum('sh,shp,sn->hpn', tail_scale, x_blk, b_blk, precision=HIGHEST)
        return (new_state, y_inner + y_carry)
    initial = jnp.zeros((head_count, head_dim, state_dim), jnp.float32)
    last_state, y_blocks = lax.scan(jax.checkpoint(block_step), initial, (x_blocks, b_blocks, c_blocks, step_blocks))
    return y_blocks.reshape(seq_length, head_count, head_dim) + skip_gain[None, :, None] * x_conv

def mixer_sequence(zx_seq, aux_seq, kernel_x, bias_x, kernel_bc, bias_bc, step_bias, decay_log, skip_gain, head_start, span_len):
    seq_length, head_count, pair_dim = zx_seq.shape
    head_dim = pair_dim // 2
    tap_count = kernel_x.shape[0]
    state_dim = kernel_bc.shape[1] // 2
    gate_vals = zx_seq[:, :, :head_dim]
    x_vals = zx_seq[:, :, head_dim:].reshape(seq_length, head_count * head_dim)
    x_conv = silu_fn(causal_conv(x_vals, kernel_x.reshape(tap_count, head_count * head_dim), bias_x.reshape(head_count * head_dim)))
    bc_conv = silu_fn(causal_conv(aux_seq[:, :2 * state_dim], kernel_bc, bias_bc))
    step_raw = lax.dynamic_slice_in_dim(aux_seq, 2 * state_dim + head_start, head_count, 1)
    step_size = jax.nn.softplus(step_raw + step_bias[None, :])
    y_vals = ssd_sequence(x_conv.reshape(seq_length, head_count, head_dim), bc_conv[:, :state_dim], bc_conv[:, state_dim:], step_size, -jnp.exp(decay_log), skip_gain, span_len)
    return y_vals * silu_fn(gate_vals)

def run_group(zx_vals, aux_vals, kernel_x, bias_x, kernel_bc, bias_bc, step_bias, decay_log, skip_gain, head_start):

    def one_sequence(zx_seq, aux_seq):
        return mixer_sequence(zx_seq, aux_seq, kernel_x, bias_x, kernel_bc, bias_bc, step_bias, decay_log, skip_gain, head_start, CH)
    return jax.vmap(one_sequence)(zx_vals, aux_vals)

def block_forward(param_set, block_data):
    norm_gain, gate_input_weight, auxiliary_weight, conv_x, conv_x_bias, conv_bc, conv_bc_bias, dt_bias, a_log, d_skip, out_gain, output_weight = param_set
    inputs, target_vals, valid_mask = block_data
    mean_square = lax.optimization_barrier(jnp.mean(inputs * inputs, axis=-1, keepdims=True))
    rescaled = low(inputs * lax.rsqrt(mean_square + EPSILON) * norm_gain)
    zx_all = low_back(jnp.einsum('bld,dhe->blhe', rescaled, gate_input_weight, precision=HIGHEST))
    aux_all = jnp.einsum('bld,dk->blk', rescaled, auxiliary_weight, precision=HIGHEST)
    group_heads = H // N_ROW
    pieces = []
    for group_idx in range(N_ROW):
        head_first = group_idx * group_heads
        head_last = head_first + group_heads
        aux_copy = low_back(aux_all)
        pieces.append(run_group(zx_all[:, :, head_first:head_last], aux_copy, conv_x[:, head_first:head_last], conv_x_bias[head_first:head_last], conv_bc, conv_bc_bias, dt_bias[head_first:head_last], a_log[head_first:head_last], d_skip[head_first:head_last], head_first))
    gated = jnp.concatenate(pieces, axis=2)
    gate_mean = lax.optimization_barrier(jnp.mean(gated * gated, axis=(2, 3), keepdims=True))
    normed = low(gated * lax.rsqrt(gate_mean + EPSILON) * out_gain)
    branch = low_back(jnp.einsum('blhp,hpd->bld', normed, output_weight, precision=HIGHEST))
    result = inputs + branch
    difference = (result - target_vals) * valid_mask[:, :, None]
    return (result, jnp.sum(difference * difference))

def reference(hidden, targets, lengths, dest_group, norm_gain, gate_input_weight, auxiliary_weight, conv_x, conv_x_bias, conv_bc, conv_bc_bias, dt_bias, a_log, d_skip, out_gain, output_weight):
    wide_type = jnp.float32
    block_seqs = math.gcd(SEQS, max(1, 4096 // LEN))
    block_count = SEQS // block_seqs
    positions = jnp.arange(LEN, dtype=jnp.int32)
    valid_mask = (positions[None, :] < lengths[:, None]).astype(wide_type)
    valid_count = jnp.sum(lengths).astype(wide_type)
    hidden_wide = hidden.astype(wide_type)
    target_wide = targets.astype(wide_type)
    params = (norm_gain, gate_input_weight.astype(wide_type), auxiliary_weight.astype(wide_type), conv_x, conv_x_bias, conv_bc, conv_bc_bias, dt_bias, a_log, d_skip, out_gain, output_weight.astype(wide_type))

    def total_loss(param_set, inputs):
        blocks = (inputs.reshape(block_count, block_seqs, LEN, D), target_wide.reshape(block_count, block_seqs, LEN, D), valid_mask.reshape(block_count, block_seqs, LEN))

        def scan_step(running, block_data):
            result, loss_part = block_forward(param_set, block_data)
            return (running + loss_part, result)
        loss_sum, results = lax.scan(jax.checkpoint(scan_step), jnp.zeros((), wide_type), blocks)
        return (loss_sum * 0.5 / valid_count, results.reshape(SEQS, LEN, D))
    (loss_value, results), pullback = jax.vjp(total_loss, params, hidden_wide)
    seed_grad = jnp.ones((), wide_type) * TOKENS
    param_grads, input_grad = pullback((seed_grad, jnp.zeros_like(results)))
    source = dest_group * SEQ_GRP + jnp.arange(SEQS, dtype=jnp.int32) // SEQ_GRP
    output = jnp.take(results, source, axis=0).astype(jnp.bfloat16)
    hidden_grad = jnp.take(input_grad, source, axis=0).astype(jnp.bfloat16)
    g_norm, g_zx, g_aux, g_conv_x, g_conv_x_bias, g_conv_bc, g_conv_bc_bias, g_dt_bias, g_a_log, g_d_skip, g_out_gain, g_out = param_grads
    return (loss_value, output, hidden_grad, g_norm, g_zx, g_aux, g_conv_x, g_conv_x_bias, g_conv_bc, g_conv_bc_bias, g_dt_bias, g_a_log, g_d_skip, g_out_gain, g_out)
```

```python
import functools
import jax
import jax.numpy as jnp
from jax import lax
from jax.experimental import pallas as pl
from jax.experimental.pallas import tpu as pltpu
from jax.sharding import PartitionSpec as P

BF = jnp.bfloat16
F32 = jnp.float32
SPAN = 512
EDGE = 128
EPSILON = 1e-05


def nn(a, b):
    return lax.dot_general(a, b, (((1,), (0,)), ((), ())), preferred_element_type=F32)


def nt(a, b):
    return lax.dot_general(a, b, (((1,), (1,)), ((), ())), preferred_element_type=F32)


def tn(a, b):
    return lax.dot_general(a, b, (((0,), (0,)), ((), ())), preferred_element_type=F32)


def exact(a, b):
    return lax.dot_general(
        a, b, (((1,), (0,)), ((), ())), precision=lax.Precision.HIGHEST, preferred_element_type=F32
    )


def sigmoid(v):
    return 0.5 * jnp.tanh(0.5 * v) + 0.5


def softplus(v):
    return jnp.maximum(v, 0.0) + jnp.log1p(jnp.exp(-jnp.abs(v)))


def shifted(before, now):
    joined = jnp.concatenate([before, now], axis=1)
    return [now] + [pltpu.roll(joined, k, 1)[:, EDGE:] for k in (1, 2, 3)]


def ahead(now, after):
    joined = jnp.concatenate([now, after], axis=1)
    size = joined.shape[1]
    return [now] + [pltpu.roll(joined, size - k, 1)[:, : now.shape[1]] for k in (1, 2, 3)]


def conv_of(shifts, taps):
    total = taps[:, 4:5] + taps[:, 3:4] * shifts[0]
    for k in (1, 2, 3):
        total = total + taps[:, 3 - k : 4 - k] * shifts[k]
    return total


def span_common(bc_before, bc_now, dt_raw, bc_taps, dt_par):
    shifts = shifted(bc_before, bc_now)
    pre = conv_of(shifts, bc_taps)
    sig = sigmoid(pre)
    act = pre * sig
    half = act.shape[0] // 2
    b_t = act[:half].astype(BF)
    c_t = act[half:].astype(BF)
    span = bc_now.shape[1]
    rows = lax.broadcasted_iota(jnp.int32, (span, span), 0)
    cols = lax.broadcasted_iota(jnp.int32, (span, span), 1)
    causal = rows <= cols
    steps = softplus(dt_raw + dt_par[:, 0:1])
    rate = -jnp.exp(dt_par[:, 1:2])
    decay = exact(steps * rate, causal.astype(F32))
    return shifts, pre, sig, b_t, c_t, causal, steps, rate, decay


def forward_kernel(
    heads, zx_ref, bc_ref, dt_ref, taps_ref, bc_taps_ref, dt_par_ref,
    gated_ref, square_ref, enter_ref,
    state, x_tail, bc_tail, carry, tailed,
):
    span = zx_ref.shape[1]
    size = zx_ref.shape[0] // heads // 2

    @pl.when(pl.program_id(0) == 0)
    def _():
        state[...] = jnp.zeros_like(state)
        x_tail[...] = jnp.zeros_like(x_tail)
        bc_tail[...] = jnp.zeros_like(bc_tail)

    bc_now = bc_ref[...]
    _, _, _, b_t, c_t, causal, steps, rate, decay = span_common(
        bc_tail[...], bc_now, dt_ref[...], bc_taps_ref[...], dt_par_ref[...]
    )
    bc_tail[...] = bc_now[:, span - EDGE :]
    b_n = b_t.astype(F32).T.astype(BF)
    scores = jnp.where(causal, nn(b_n, c_t), 0.0)
    decay_n = decay.T
    grown = jnp.exp(decay)
    last = decay[:, span - 1 : span]
    left = jnp.exp(last - decay)
    kept = jnp.exp(last)
    entering = state[...].astype(BF)
    enter_ref[...] = entering
    carry[...] = nn(entering, c_t)
    square = jnp.zeros((size, span), F32)
    for h in range(heads):
        at = slice(h * size, (h + 1) * size)
        z = zx_ref[2 * h * size : (2 * h + 1) * size, :]
        x_raw = zx_ref[(2 * h + 1) * size : (2 * h + 2) * size, :]
        taps = taps_ref[at, :]
        pre = conv_of(shifted(x_tail[at, :], x_raw), taps)
        x_tail[at, :] = x_raw[:, span - EDGE :]
        x = pre * sigmoid(pre)
        xd = x * steps[h : h + 1, :]
        mixing = scores * jnp.exp(jnp.minimum(decay[h : h + 1, :] - decay_n[:, h : h + 1], 0.0))
        y = nn(xd.astype(BF), mixing.astype(BF)) + carry[at, :] * grown[h : h + 1, :] + taps[:, 5:6] * x
        tailed[at, :] = (xd * left[h : h + 1, :]).astype(BF)
        gated = y * (z * sigmoid(z))
        square = square + gated * gated
        gated_ref[at, :] = (gated * taps[:, 6:7]).astype(BF)
        state[at, :] = state[at, :] * kept[h : h + 1, :]
    square_ref[...] = jnp.sum(square, axis=0, keepdims=True)
    state[...] = state[...] + nn(tailed[...], b_n)


def backward_kernel(
    heads, zx_ref, zx_before_ref, bc_ref, bc_before_ref, dt_ref, enter_ref, gn_ref, coef_ref,
    taps_ref, bc_taps_ref, dt_par_ref,
    gzx_ref, gx_sum_ref, gbc_sum_ref, gdt_sum_ref,
    dstate, x_head, bc_head, carry, from_state, grown_g, tailed, x_acc, bc_acc, dt_acc, rsum, dsum,
):
    span = zx_ref.shape[1]
    size = zx_ref.shape[0] // heads // 2
    half = bc_ref.shape[0] // 2
    wide = zx_ref.shape[0]
    step = pl.program_id(0)
    count = pl.num_programs(0)
    first = step == count - 1

    @pl.when(step == 0)
    def _():
        dstate[...] = jnp.zeros_like(dstate)
        x_head[...] = jnp.zeros_like(x_head)
        bc_head[...] = jnp.zeros_like(bc_head)
        x_acc[...] = jnp.zeros_like(x_acc)
        bc_acc[...] = jnp.zeros_like(bc_acc)
        dt_acc[...] = jnp.zeros_like(dt_acc)
        rsum[...] = jnp.zeros_like(rsum)
        dsum[...] = jnp.zeros_like(dsum)

    live = jnp.where(first, 0.0, 1.0)
    bc_taps = bc_taps_ref[...]
    dt_raw = dt_ref[...]
    bc_shifts, bc_pre, bc_sig, b_t, c_t, causal, steps, rate, decay = span_common(
        bc_before_ref[...] * live, bc_ref[...], dt_raw, bc_taps, dt_par_ref[...]
    )
    b_n = b_t.astype(F32).T.astype(BF)
    scores = jnp.where(causal, nn(b_n, c_t), 0.0)
    decay_n = decay.T
    grown = jnp.exp(decay)
    last = decay[:, span - 1 : span]
    left = jnp.exp(last - decay)
    kept = jnp.exp(last)
    entering = enter_ref[...]
    leaving = dstate[...].astype(BF)
    carry[...] = nn(entering, c_t)
    from_state[...] = nn(leaving, b_t)
    coef = coef_ref[...]
    dscores = jnp.zeros((span, span), F32)
    def fold(v):
        total = v[:, :EDGE]
        for k in range(1, span // EDGE):
            total = total + v[:, k * EDGE : (k + 1) * EDGE]
        return total
    for h in range(heads):
        at = slice(h * size, (h + 1) * size)
        z = zx_ref[2 * h * size : (2 * h + 1) * size, :]
        x_raw = zx_ref[(2 * h + 1) * size : (2 * h + 2) * size, :]
        x_before = zx_before_ref[(2 * h + 1) * size : (2 * h + 2) * size, :] * live
        taps = taps_ref[at, :]
        shifts = shifted(x_before, x_raw)
        pre = conv_of(shifts, taps)
        sig = sigmoid(pre)
        x = pre * sig
        steps_h = steps[h : h + 1, :]
        grown_h = grown[h : h + 1, :]
        left_h = left[h : h + 1, :]
        xd = x * steps_h
        xd_low = xd.astype(BF)
        ratio = jnp.exp(jnp.minimum(decay[h : h + 1, :] - decay_n[:, h : h + 1], 0.0))
        mixing = (scores * ratio).astype(BF)
        skip = taps[:, 5:6]
        y_scan = nn(xd_low, mixing) + carry[at, :] * grown_h
        y = y_scan + skip * x
        zsig = sigmoid(z)
        silu_z = z * zsig
        gated = y * silu_z
        gn = gn_ref[at, :].astype(F32)
        g_gated = taps[:, 6:7] * gn - gated * coef
        gy = g_gated * silu_z
        gzx_ref[2 * h * size : (2 * h + 1) * size, :] = (
            g_gated * y * (zsig + silu_z * (1.0 - zsig))
        ).astype(BF)
        gy_low = gy.astype(BF)
        gy_wide = gy_low.astype(F32)
        grown_g[at, :] = (gy * grown_h).astype(BF)
        tailed[at, :] = (xd * left_h).astype(BF)
        dx_state = from_state[at, :] * left_h
        dxd = nt(gy_low, mixing) + dx_state
        xd_wide = xd_low.astype(F32)
        rsum[h : h + 1, :] = jnp.sum(gy_wide * y_scan - xd_wide * dxd, axis=0, keepdims=True)
        dsum[h : h + 1, :] = jnp.sum(x * dxd, axis=0, keepdims=True)
        held = jnp.sum(xd_wide * dx_state, axis=0, keepdims=True)
        held = jnp.sum(held, axis=1, keepdims=True)
        flow = jnp.sum(dstate[at, :] * entering[at, :].astype(F32), axis=0, keepdims=True)
        flow = jnp.sum(flow, axis=1, keepdims=True) * kept[h : h + 1, :]
        dt_acc[h : h + 1, 0:1] = held + flow
        dscores = dscores + tn(xd_low, gy_low) * ratio
        dx = dxd * steps_h + skip * gy
        gpre = dx * (sig + x * (1.0 - sig))
        later = ahead(gpre, x_head[at, :])
        x_head[at, :] = gpre[:, :EDGE]
        g_raw = taps[:, 3:4] * later[0]
        for k in (1, 2, 3):
            g_raw = g_raw + taps[:, 3 - k : 4 - k] * later[k]
        gzx_ref[(2 * h + 1) * size : (2 * h + 2) * size, :] = g_raw.astype(BF)
        for k in range(4):
            x_acc[3 - k, at, :] = x_acc[3 - k, at, :] + fold(gpre * shifts[k])
        x_acc[4, at, :] = x_acc[4, at, :] + fold(gpre)
        x_acc[5, at, :] = x_acc[5, at, :] + fold(gy * x)
        x_acc[6, at, :] = x_acc[6, at, :] + fold(gn * gated)
    dscores = jnp.where(causal, dscores, 0.0).astype(BF)
    dc = nn(b_t, dscores) + tn(entering, grown_g[...])
    db = nt(c_t, dscores) + tn(leaving, tailed[...])
    dstate[...] = nt(grown_g[...], c_t)  + dstate[...] * jnp.concatenate(
        [jnp.broadcast_to(kept[h : h + 1, :], (size, dstate.shape[1])) for h in range(heads)], axis=0
    )
    gbc = jnp.concatenate([db, dc], axis=0) * (bc_sig + bc_pre * bc_sig * (1.0 - bc_sig))
    later = ahead(gbc, bc_head[...])
    bc_head[...] = gbc[:, :EDGE]
    g_raw = bc_taps[:, 3:4] * later[0]
    for k in (1, 2, 3):
        g_raw = g_raw + bc_taps[:, 3 - k : 4 - k] * later[k]
    gzx_ref[wide : wide + 2 * half, :] = g_raw.astype(BF)
    for k in range(4):
        bc_acc[3 - k] = bc_acc[3 - k] + fold(gbc * bc_shifts[k])
    bc_acc[4] = bc_acc[4] + fold(gbc)
    rows = lax.broadcasted_iota(jnp.int32, (span, span), 0)
    cols = lax.broadcasted_iota(jnp.int32, (span, span), 1)
    da = exact(rsum[...], (rows >= cols).astype(F32)) + dt_acc[:, 0:1]
    g_steps = dsum[...] + rate * da
    g_dt = g_steps * sigmoid(dt_raw + dt_par_ref[:, 0:1])
    gzx_ref[wide + 2 * half :, :] = g_dt.astype(BF)
    dt_acc[:, 1:2] = dt_acc[:, 1:2] + jnp.sum(g_dt, axis=1, keepdims=True)
    dt_acc[:, 2:3] = dt_acc[:, 2:3] + jnp.sum(da * steps * rate, axis=1, keepdims=True)

    @pl.when(first)
    def _():
        for k in range(7):
            gx_sum_ref[:, k : k + 1] = jnp.sum(x_acc[k], axis=1, keepdims=True)
        for k in range(5):
            gbc_sum_ref[:, k : k + 1] = jnp.sum(bc_acc[k], axis=1, keepdims=True)
        gdt_sum_ref[...] = dt_acc[...]


def scan_forward(zx, taps, bc_taps, dt_par, heads, span=SPAN):
    inner = taps.shape[0]
    length = zx.shape[1]
    aux = bc_taps.shape[0]
    steps = dt_par.shape[0]
    states = aux // 2
    body = functools.partial(forward_kernel, heads)
    whole = lambda r, c: pl.BlockSpec((r, c), lambda i: (0, 0))
    return pl.pallas_call(
        body,
        grid=(length // span,),
        in_specs=[
            pl.BlockSpec((2 * inner, span), lambda i: (0, i)),
            pl.BlockSpec((aux, span), lambda i: (2 * inner // aux, i)),
            pl.BlockSpec((steps, span), lambda i: ((2 * inner + aux) // steps, i)),
            whole(inner, 8), whole(aux, 8), whole(steps, 8),
        ],
        out_specs=[
            pl.BlockSpec((inner, span), lambda i: (0, i)),
            pl.BlockSpec((1, span), lambda i: (0, i)),
            pl.BlockSpec((inner, states), lambda i: (i, 0)),
        ],
        out_shape=[
            jax.ShapeDtypeStruct((inner, length), BF),
            jax.ShapeDtypeStruct((1, length), F32),
            jax.ShapeDtypeStruct((length // span * inner, states), BF),
        ],
        scratch_shapes=[
            pltpu.VMEM((inner, states), F32),
            pltpu.VMEM((inner, EDGE), F32),
            pltpu.VMEM((aux, EDGE), F32),
            pltpu.VMEM((inner, span), F32),
            pltpu.VMEM((inner, span), BF),
        ],
        compiler_params=pltpu.CompilerParams(vmem_limit_bytes=48 * 2**20),
        name="scan_forward",
    )(zx, zx, zx, taps, bc_taps, dt_par)


def scan_backward(zx, entering, gn, coef, taps, bc_taps, dt_par, heads, span=SPAN):
    inner = taps.shape[0]
    length = zx.shape[1]
    aux = bc_taps.shape[0]
    steps = dt_par.shape[0]
    states = aux // 2
    count = length // span
    ratio = span // EDGE
    body = functools.partial(backward_kernel, heads)
    whole = lambda r, c: pl.BlockSpec((r, c), lambda i: (0, 0))
    rev = lambda i: count - 1 - i
    before = lambda i: jnp.maximum((count - 1 - i) * ratio - 1, 0)
    return pl.pallas_call(
        body,
        grid=(count,),
        in_specs=[
            pl.BlockSpec((2 * inner, span), lambda i: (0, rev(i))),
            pl.BlockSpec((2 * inner, EDGE), lambda i: (0, before(i))),
            pl.BlockSpec((aux, span), lambda i: (2 * inner // aux, rev(i))),
            pl.BlockSpec((aux, EDGE), lambda i: (2 * inner // aux, before(i))),
            pl.BlockSpec((steps, span), lambda i: ((2 * inner + aux) // steps, rev(i))),
            pl.BlockSpec((inner, states), lambda i: (rev(i), 0)),
            pl.BlockSpec((inner, span), lambda i: (0, rev(i))),
            pl.BlockSpec((1, span), lambda i: (0, rev(i))),
            whole(inner, 8), whole(aux, 8), whole(steps, 8),
        ],
        out_specs=[
            pl.BlockSpec((2 * inner + aux + steps, span), lambda i: (0, rev(i))),
            whole(inner, 8), whole(aux, 8), whole(steps, EDGE),
        ],
        out_shape=[
            jax.ShapeDtypeStruct((2 * inner + aux + steps, length), BF),
            jax.ShapeDtypeStruct((inner, 8), F32),
            jax.ShapeDtypeStruct((aux, 8), F32),
            jax.ShapeDtypeStruct((steps, EDGE), F32),
        ],
        scratch_shapes=[
            pltpu.VMEM((inner, states), F32),
            pltpu.VMEM((inner, EDGE), F32),
            pltpu.VMEM((aux, EDGE), F32),
            pltpu.VMEM((inner, span), F32),
            pltpu.VMEM((inner, span), F32),
            pltpu.VMEM((inner, span), BF),
            pltpu.VMEM((inner, span), BF),
            pltpu.VMEM((7, inner, EDGE), F32),
            pltpu.VMEM((5, aux, EDGE), F32),
            pltpu.VMEM((steps, EDGE), F32),
            pltpu.VMEM((steps, span), F32),
            pltpu.VMEM((steps, span), F32),
        ],
        compiler_params=pltpu.CompilerParams(vmem_limit_bytes=56 * 2**20),
        name="scan_backward",
    )(zx, zx, zx, zx, zx, entering, gn, coef, taps, bc_taps, dt_par)


def gather_row(x):
    count = lax.axis_size("row")
    if count != 4:
        return lax.all_gather(x, "row", axis=0, tiled=True)
    me = lax.axis_index("row")
    size = x.shape[0]
    flip = lambda v, bit: lax.ppermute(v, "row", [(i, i ^ bit) for i in range(4)])
    from_x = flip(x, 1)
    from_y = flip(x, 2)
    cross_a = flip(from_y[: size // 2], 1)
    cross_b = flip(from_x[size // 2 :], 2)
    out = jnp.zeros((4 * size, x.shape[1]), x.dtype)
    put = lambda o, v, bit, off: lax.dynamic_update_slice(o, v, ((me ^ bit) * size + off, 0))
    out = put(out, x, 0, 0)
    out = put(out, from_x, 1, 0)
    out = put(out, from_y, 2, 0)
    out = put(out, cross_a, 3, 0)
    return put(out, cross_b, 3, size // 2)


def scatter_row(x):
    count = lax.axis_size("row")
    if count != 4:
        return lax.psum_scatter(x, "row", scatter_dimension=0, tiled=True).astype(F32)
    me = lax.axis_index("row")
    size, width = x.shape[0] // 4, x.shape[1]
    half = width // 2
    my_y, my_x = me // 2, me % 2
    blocks = x.reshape(2, 2, size, width)
    flip = lambda v, bit: lax.ppermute(v, "row", [(i, i ^ bit) for i in range(4)])
    at_x = lambda i: lax.dynamic_slice(blocks, (0, i, 0, 0), (2, 1, size, half))[:, 0]
    at_y = lambda i: lax.dynamic_slice(blocks, (i, 0, 0, half), (1, 2, size, half))[0]
    got_x = flip(at_x(1 - my_x), 1)
    got_y = flip(at_y(1 - my_y), 2)
    pick = lambda v, i: lax.dynamic_index_in_dim(v, i, 0, keepdims=False).astype(F32)
    keep_x, keep_y = at_x(my_x), at_y(my_y)
    pass_x = (pick(keep_x, 1 - my_y) + pick(got_x, 1 - my_y)).astype(BF)
    pass_y = (pick(keep_y, 1 - my_x) + pick(got_y, 1 - my_x)).astype(BF)
    end_x = flip(pass_x, 2)
    end_y = flip(pass_y, 1)
    left = pick(keep_x, my_y) + pick(got_x, my_y) + end_x.astype(F32)
    right = pick(keep_y, my_x) + pick(got_y, my_x) + end_y.astype(F32)
    return jnp.concatenate([left, right], axis=1)


def butterfly(v, axis):
    count = lax.axis_size(axis)
    bit = 1
    while bit < count:
        v = v + lax.ppermute(v, axis, [(i, i ^ bit) for i in range(count)])
        bit *= 2
    return v


def other_col(v):
    return lax.ppermute(v, "col", [(0, 1), (1, 0)])


def deal_back(rows, dest_group):
    groups = lax.axis_size("dp")
    me = lax.axis_index("dp")
    col = lax.axis_index("col")
    half = rows[0].shape[1] // 2
    own = jnp.stack([r[:, :half] for r in rows])
    got = other_col(jnp.stack([r[:, half:] for r in rows]))
    first = jnp.where(col == 0, own, got)
    second = jnp.where(col == 0, got, own)
    dealt = jnp.concatenate([first, second], axis=0)
    parts = []
    for hop in range(groups):
        piece = lax.dynamic_index_in_dim(dealt, (me + hop) % groups, 0, keepdims=False)
        if hop:
            piece = lax.ppermute(piece, "dp", [(i, (i + hop) % groups) for i in range(groups)])
        parts.append(piece)
    hops = ((me - dest_group) % groups)[:, None, None]
    out = jnp.where(hops == 0, parts[0][None], jnp.zeros((), BF))
    for hop in range(1, groups):
        out = jnp.where(hops == hop, parts[hop][None], out)
    return out


def per_device(
    hidden, targets, lengths, dest_group, norm_gain, gate_input_weight, auxiliary_weight,
    conv_x, conv_x_bias, conv_bc, conv_bc_bias, dt_bias, a_log, d_skip, out_gain, output_weight,
):
    row_count = lax.axis_size("row")
    col_count = lax.axis_size("col")
    row_index = lax.axis_index("row")
    col_index = lax.axis_index("col")
    group_index = lax.axis_index("dp")
    seq_group, local_len, width_col = hidden.shape
    heads = gate_input_weight.shape[1]
    pair = gate_input_weight.shape[2]
    head_dim = pair // 2
    inner = heads * head_dim
    wide = heads * pair
    aux = conv_bc.shape[1]
    head_total = auxiliary_weight.shape[1] - aux
    steps = -(-heads // 16) * 16
    seq_col = seq_group // col_count
    model_width = width_col * col_count
    inner_width = inner * row_count
    all_tokens = lengths.shape[0] * local_len * row_count
    valid_count = jnp.sum(lengths).astype(F32)
    group_lengths = lax.dynamic_slice_in_dim(lengths, group_index * seq_group, seq_group, 0)
    own_lengths = lax.dynamic_slice_in_dim(group_lengths, col_index * seq_col, seq_col, 0)

    def widened(v):
        mine = lax.dynamic_slice_in_dim(v, col_index * seq_col, seq_col, 0)
        theirs = lax.dynamic_slice_in_dim(v, (1 - col_index) * seq_col, seq_col, 0)
        return jnp.concatenate([mine, other_col(theirs)], axis=2)

    u_low = widened(hidden)
    gain = jnp.concatenate([norm_gain, other_col(norm_gain)])
    in_own = jnp.concatenate(
        [
            gate_input_weight.reshape(width_col, wide),
            auxiliary_weight[:, :aux],
            lax.dynamic_slice_in_dim(auxiliary_weight, aux + row_index * heads, heads, 1),
            jnp.zeros((width_col, steps - heads), BF),
        ],
        axis=1,
    )
    in_weight = jnp.concatenate([in_own, other_col(in_own)], axis=0)
    out_own = output_weight.reshape(inner, width_col)
    out_weight = jnp.concatenate([out_own, other_col(out_own)], axis=1)

    u = [u_low[k].astype(F32) for k in range(seq_col)]
    inv_rms = [lax.rsqrt(jnp.mean(v * v, axis=1, keepdims=True) + EPSILON) for v in u]
    scaled = [
        gather_row((v * r * gain[None, :]).astype(BF)) for v, r in zip(u, inv_rms, strict=True)
    ]

    column = lambda v: v.reshape(-1, 1)
    taps = jnp.concatenate(
        [
            conv_x.reshape(-1, inner).T,
            column(conv_x_bias),
            column(jnp.repeat(d_skip, head_dim)),
            column(out_gain),
            jnp.zeros((inner, 1), F32),
        ],
        axis=1,
    )
    bc_taps = jnp.concatenate([conv_bc.T, column(conv_bc_bias), jnp.zeros((aux, 3), F32)], axis=1)
    dt_par = jnp.pad(jnp.stack([dt_bias, a_log], axis=1), ((0, steps - heads), (0, 6)))

    zx, gated, square, entering = [], [], [], []
    for k in range(seq_col):
        projected = lax.dot_general(
            in_weight, scaled[k], (((0,), (1,)), ((), ())), preferred_element_type=F32
        )
        zx.append(projected)
        g, s, e = scan_forward(projected, taps, bc_taps, dt_par, heads)
        gated.append(g)
        square.append(s)
        entering.append(e)

    targets_own = widened(targets)
    positions = row_index * local_len + jnp.arange(local_len, dtype=jnp.int32)
    result, g_result, g_rows, coef = [], [], [], []
    loss_part = jnp.zeros((), F32)
    for k in range(seq_col):
        part = lax.dot_general(
            gated[k], out_weight, (((0,), (0,)), ((), ())), preferred_element_type=F32
        ).astype(BF)
        total_square = butterfly(square[k], "row")[0]
        mine = lax.dynamic_slice_in_dim(total_square, row_index * local_len, local_len, 0)
        gate_inv = lax.rsqrt(mine / inner_width + EPSILON)[:, None]
        branch = scatter_row(part) * gate_inv
        full = u[k] + branch
        valid = (positions < own_lengths[k]).astype(F32)[:, None]
        difference = (full - targets_own[k].astype(F32)) * valid
        loss_part = loss_part + jnp.sum(difference * difference)
        grad = difference * (all_tokens / valid_count)
        result.append(full.astype(BF))
        g_result.append(grad)
        share = gate_inv[:, 0] * gate_inv[:, 0] * jnp.sum(grad * branch, axis=1) / inner_width
        placed = lax.dynamic_update_slice_in_dim(
            jnp.zeros((local_len * row_count,), F32), share, row_index * local_len, 0
        )
        coef.append(butterfly(placed[None, :], "row"))
        g_rows.append(gather_row((grad * gate_inv).astype(BF)))

    output = deal_back(result, dest_group)

    w_out_part = 0.0
    g_in = []
    sums = [0.0, 0.0, 0.0]
    for k in range(seq_col):
        gn = lax.dot_general(
            out_weight, g_rows[k], (((1,), (1,)), ((), ())), preferred_element_type=F32
        )
        g, gx, gbc, gdt = scan_backward(
            zx[k], entering[k], gn, coef[k], taps, bc_taps, dt_par, heads
        )
        g_in.append(g)
        sums = [a + b for a, b in zip(sums, (gx, gbc, gdt), strict=True)]
        w_out_part = w_out_part + lax.dot_general(
            gated[k], g_rows[k], (((1,), (0,)), ((), ())), preferred_element_type=F32
        )
    w_out_half = w_out_part[:, :width_col] + other_col(
        w_out_part[:, width_col:].astype(BF)
    ).astype(F32)
    w_out_sum = lax.psum(w_out_half.astype(BF), "dp")

    in_part = 0.0
    gain_part = jnp.zeros((model_width,), F32)
    g_u = []
    for k in range(seq_col):
        part = lax.dot_general(
            g_in[k], in_weight, (((0,), (1,)), ((), ())), preferred_element_type=F32
        ).astype(BF)
        g_scaled = scatter_row(part)
        gain_part = gain_part + jnp.sum(g_scaled * u[k] * inv_rms[k], axis=0)
        weighted = g_scaled * gain[None, :]
        dot = jnp.sum(weighted * u[k], axis=1, keepdims=True) / model_width
        cube = inv_rms[k] * inv_rms[k] * inv_rms[k]
        g_u.append((g_result[k] + inv_rms[k] * weighted - u[k] * (cube * dot)).astype(BF))
        in_part = in_part + lax.dot_general(
            scaled[k], g_in[k], (((0,), (1,)), ((), ())), preferred_element_type=F32
        )
    in_half = in_part[:width_col] + other_col(in_part[width_col:].astype(BF)).astype(F32)
    aux_half = jnp.concatenate(
        [
            in_half[:, wide : wide + aux],
            lax.dynamic_update_slice_in_dim(
                jnp.zeros((width_col, head_total), F32),
                in_half[:, wide + aux : wide + aux + heads],
                row_index * heads,
                1,
            ),
        ],
        axis=1,
    )
    w_aux = lax.psum(butterfly(aux_half.astype(BF), "row"), "dp")
    w_zx = lax.psum(in_half[:, :wide].astype(BF), "dp")
    hidden_grad = deal_back(g_u, dest_group)

    gx, gbc, gdt = sums
    own = butterfly(
        butterfly(jnp.concatenate([gx.reshape(-1), gdt[:, 1:3].reshape(-1)]), "col"), "dp"
    )
    shared = jnp.concatenate([gbc.reshape(-1), loss_part[None]])
    shared = butterfly(butterfly(butterfly(shared, "col"), "row"), "dp")
    gain_half = gain_part[:width_col] + other_col(gain_part[width_col:])
    gain_sum = butterfly(butterfly(gain_half, "row"), "dp")

    gx = own[: inner * 8].reshape(inner, 8)
    gdt = own[inner * 8 :].reshape(steps, 2)
    gbc = shared[: aux * 8].reshape(aux, 8)
    loss = shared[aux * 8] * 0.5 / valid_count
    return (
        loss,
        output,
        hidden_grad,
        gain_sum,
        w_zx.astype(F32).reshape(width_col, heads, pair),
        w_aux.astype(F32),
        gx[:, :4].T.reshape(4, heads, head_dim),
        gx[:, 4].reshape(heads, head_dim),
        gbc[:, :4].T,
        gbc[:, 4],
        gdt[:heads, 0],
        gdt[:heads, 1],
        gx[:, 5].reshape(heads, head_dim).sum(axis=1),
        gx[:, 6].reshape(heads, head_dim),
        w_out_sum.astype(F32).reshape(heads, head_dim, width_col),
    )


def solution(mesh):
    placed = (
        P("dp", "row", "col"),
        P("dp", "row", "col"),
        P(),
        P("dp"),
        P("col"),
        P("col", "row", None),
        P("col", None),
        P(None, "row", None),
        P("row", None),
        P(),
        P(),
        P("row"),
        P("row"),
        P("row"),
        P("row", None),
        P("row", None, "col"),
    )
    return jax.shard_map(
        per_device,
        mesh=mesh,
        in_specs=placed,
        out_specs=(
            P(),
            P("dp", "row", "col"),
            P("dp", "row", "col"),
            P("col"),
            P("col", "row", None),
            P("col", None),
            P(None, "row", None),
            P("row", None),
            P(),
            P(),
            P("row"),
            P("row"),
            P("row"),
            P("row", None),
            P("row", None, "col"),
        ),
        check_vma=False,
    )
```

```python
import functools
import jax
import jax.numpy as jnp
from jax import lax
from jax.experimental import pallas as pl
from jax.experimental.pallas import tpu as pltpu
from jax.sharding import PartitionSpec as P

BF = jnp.bfloat16
F32 = jnp.float32
SPAN = 512
EDGE = 128
EPSILON = 1e-05


def nn(a, b):
    return lax.dot_general(a, b, (((1,), (0,)), ((), ())), preferred_element_type=F32)


def nt(a, b):
    return lax.dot_general(a, b, (((1,), (1,)), ((), ())), preferred_element_type=F32)


def tn(a, b):
    return lax.dot_general(a, b, (((0,), (0,)), ((), ())), preferred_element_type=F32)


def exact(a, b):
    return lax.dot_general(
        a, b, (((1,), (0,)), ((), ())), precision=lax.Precision.HIGHEST, preferred_element_type=F32
    )


def sigmoid(v):
    return 0.5 * jnp.tanh(0.5 * v) + 0.5


def softplus(v):
    return jnp.maximum(v, 0.0) + jnp.log1p(jnp.exp(-jnp.abs(v)))


def shifted(before, now):
    joined = jnp.concatenate([before, now], axis=1)
    return [now] + [pltpu.roll(joined, k, 1)[:, EDGE:] for k in (1, 2, 3)]


def ahead(now, after):
    joined = jnp.concatenate([now, after], axis=1)
    size = joined.shape[1]
    return [now] + [pltpu.roll(joined, size - k, 1)[:, : now.shape[1]] for k in (1, 2, 3)]


def conv_of(shifts, taps):
    total = taps[:, 4:5] + taps[:, 3:4] * shifts[0]
    for k in (1, 2, 3):
        total = total + taps[:, 3 - k : 4 - k] * shifts[k]
    return total


def span_common(bc_before, bc_now, dt_raw, bc_taps, dt_par):
    shifts = shifted(bc_before, bc_now)
    pre = conv_of(shifts, bc_taps)
    sig = sigmoid(pre)
    act = pre * sig
    half = act.shape[0] // 2
    b_t = act[:half].astype(BF)
    c_t = act[half:].astype(BF)
    span = bc_now.shape[1]
    rows = lax.broadcasted_iota(jnp.int32, (span, span), 0)
    cols = lax.broadcasted_iota(jnp.int32, (span, span), 1)
    causal = rows <= cols
    steps = softplus(dt_raw + dt_par[:, 0:1])
    rate = -jnp.exp(dt_par[:, 1:2])
    decay = exact(steps * rate, causal.astype(F32))
    return shifts, pre, sig, b_t, c_t, causal, steps, rate, decay


def forward_kernel(
    heads, zx_ref, bc_ref, dt_ref, taps_ref, bc_taps_ref, dt_par_ref,
    gated_ref, square_ref, enter_ref,
    state, x_tail, bc_tail, carry, tailed,
):
    span = zx_ref.shape[1]
    size = zx_ref.shape[0] // heads // 2

    @pl.when(pl.program_id(0) == 0)
    def _():
        state[...] = jnp.zeros_like(state)
        x_tail[...] = jnp.zeros_like(x_tail)
        bc_tail[...] = jnp.zeros_like(bc_tail)

    bc_now = bc_ref[...]
    _, _, _, b_t, c_t, causal, steps, rate, decay = span_common(
        bc_tail[...], bc_now, dt_ref[...], bc_taps_ref[...], dt_par_ref[...]
    )
    bc_tail[...] = bc_now[:, span - EDGE :]
    b_n = b_t.astype(F32).T.astype(BF)
    scores = jnp.where(causal, nn(b_n, c_t), 0.0)
    decay_n = decay.T
    grown = jnp.exp(decay)
    last = decay[:, span - 1 : span]
    left = jnp.exp(last - decay)
    kept = jnp.exp(last)
    entering = state[...].astype(BF)
    enter_ref[...] = entering
    carry[...] = nn(entering, c_t)
    square = jnp.zeros((size, span), F32)
    for h in range(heads):
        at = slice(h * size, (h + 1) * size)
        z = zx_ref[2 * h * size : (2 * h + 1) * size, :]
        x_raw = zx_ref[(2 * h + 1) * size : (2 * h + 2) * size, :]
        taps = taps_ref[at, :]
        pre = conv_of(shifted(x_tail[at, :], x_raw), taps)
        x_tail[at, :] = x_raw[:, span - EDGE :]
        x = pre * sigmoid(pre)
        xd = x * steps[h : h + 1, :]
        mixing = scores * jnp.exp(jnp.minimum(decay[h : h + 1, :] - decay_n[:, h : h + 1], 0.0))
        y = nn(xd.astype(BF), mixing.astype(BF)) + carry[at, :] * grown[h : h + 1, :] + taps[:, 5:6] * x
        tailed[at, :] = (xd * left[h : h + 1, :]).astype(BF)
        gated = y * (z * sigmoid(z))
        square = square + gated * gated
        gated_ref[at, :] = (gated * taps[:, 6:7]).astype(BF)
        state[at, :] = state[at, :] * kept[h : h + 1, :]
    square_ref[...] = jnp.sum(square, axis=0, keepdims=True)
    state[...] = state[...] + nn(tailed[...], b_n)


def backward_kernel(
    heads, zx_ref, zx_before_ref, bc_ref, bc_before_ref, dt_ref, enter_ref, gn_ref, coef_ref,
    taps_ref, bc_taps_ref, dt_par_ref,
    gzx_ref, gx_sum_ref, gbc_sum_ref, gdt_sum_ref,
    dstate, x_head, bc_head, carry, from_state, grown_g, tailed, x_acc, bc_acc, dt_acc, rsum, dsum,
):
    span = zx_ref.shape[1]
    size = zx_ref.shape[0] // heads // 2
    half = bc_ref.shape[0] // 2
    wide = zx_ref.shape[0]
    step = pl.program_id(0)
    count = pl.num_programs(0)
    first = step == count - 1

    @pl.when(step == 0)
    def _():
        dstate[...] = jnp.zeros_like(dstate)
        x_head[...] = jnp.zeros_like(x_head)
        bc_head[...] = jnp.zeros_like(bc_head)
        x_acc[...] = jnp.zeros_like(x_acc)
        bc_acc[...] = jnp.zeros_like(bc_acc)
        dt_acc[...] = jnp.zeros_like(dt_acc)
        rsum[...] = jnp.zeros_like(rsum)
        dsum[...] = jnp.zeros_like(dsum)

    live = jnp.where(first, 0.0, 1.0)
    bc_taps = bc_taps_ref[...]
    dt_raw = dt_ref[...]
    bc_shifts, bc_pre, bc_sig, b_t, c_t, causal, steps, rate, decay = span_common(
        bc_before_ref[...] * live, bc_ref[...], dt_raw, bc_taps, dt_par_ref[...]
    )
    b_n = b_t.astype(F32).T.astype(BF)
    scores = jnp.where(causal, nn(b_n, c_t), 0.0)
    decay_n = decay.T
    grown = jnp.exp(decay)
    last = decay[:, span - 1 : span]
    left = jnp.exp(last - decay)
    kept = jnp.exp(last)
    entering = enter_ref[...]
    leaving = dstate[...].astype(BF)
    carry[...] = nn(entering, c_t)
    from_state[...] = nn(leaving, b_t)
    coef = coef_ref[...]
    dscores = jnp.zeros((span, span), F32)
    def fold(v):
        total = v[:, :EDGE]
        for k in range(1, span // EDGE):
            total = total + v[:, k * EDGE : (k + 1) * EDGE]
        return total
    for h in range(heads):
        at = slice(h * size, (h + 1) * size)
        z = zx_ref[2 * h * size : (2 * h + 1) * size, :]
        x_raw = zx_ref[(2 * h + 1) * size : (2 * h + 2) * size, :]
        x_before = zx_before_ref[(2 * h + 1) * size : (2 * h + 2) * size, :] * live
        taps = taps_ref[at, :]
        shifts = shifted(x_before, x_raw)
        pre = conv_of(shifts, taps)
        sig = sigmoid(pre)
        x = pre * sig
        steps_h = steps[h : h + 1, :]
        grown_h = grown[h : h + 1, :]
        left_h = left[h : h + 1, :]
        xd = x * steps_h
        xd_low = xd.astype(BF)
        ratio = jnp.exp(jnp.minimum(decay[h : h + 1, :] - decay_n[:, h : h + 1], 0.0))
        mixing = (scores * ratio).astype(BF)
        skip = taps[:, 5:6]
        y_scan = nn(xd_low, mixing) + carry[at, :] * grown_h
        y = y_scan + skip * x
        zsig = sigmoid(z)
        silu_z = z * zsig
        gated = y * silu_z
        gn = gn_ref[at, :].astype(F32)
        g_gated = taps[:, 6:7] * gn - gated * coef
        gy = g_gated * silu_z
        gzx_ref[2 * h * size : (2 * h + 1) * size, :] = (
            g_gated * y * (zsig + silu_z * (1.0 - zsig))
        ).astype(BF)
        gy_low = gy.astype(BF)
        gy_wide = gy_low.astype(F32)
        grown_g[at, :] = (gy * grown_h).astype(BF)
        tailed[at, :] = (xd * left_h).astype(BF)
        dx_state = from_state[at, :] * left_h
        dxd = nt(gy_low, mixing) + dx_state
        xd_wide = xd_low.astype(F32)
        rsum[h : h + 1, :] = jnp.sum(gy_wide * y_scan - xd_wide * dxd, axis=0, keepdims=True)
        dsum[h : h + 1, :] = jnp.sum(x * dxd, axis=0, keepdims=True)
        held = jnp.sum(xd_wide * dx_state, axis=0, keepdims=True)
        held = jnp.sum(held, axis=1, keepdims=True)
        flow = jnp.sum(dstate[at, :] * entering[at, :].astype(F32), axis=0, keepdims=True)
        flow = jnp.sum(flow, axis=1, keepdims=True) * kept[h : h + 1, :]
        dt_acc[h : h + 1, 0:1] = held + flow
        dscores = dscores + tn(xd_low, gy_low) * ratio
        dx = dxd * steps_h + skip * gy
        gpre = dx * (sig + x * (1.0 - sig))
        later = ahead(gpre, x_head[at, :])
        x_head[at, :] = gpre[:, :EDGE]
        g_raw = taps[:, 3:4] * later[0]
        for k in (1, 2, 3):
            g_raw = g_raw + taps[:, 3 - k : 4 - k] * later[k]
        gzx_ref[(2 * h + 1) * size : (2 * h + 2) * size, :] = g_raw.astype(BF)
        for k in range(4):
            x_acc[3 - k, at, :] = x_acc[3 - k, at, :] + fold(gpre * shifts[k])
        x_acc[4, at, :] = x_acc[4, at, :] + fold(gpre)
        x_acc[5, at, :] = x_acc[5, at, :] + fold(gy * x)
        x_acc[6, at, :] = x_acc[6, at, :] + fold(gn * gated)
    dscores = jnp.where(causal, dscores, 0.0).astype(BF)
    dc = nn(b_t, dscores) + tn(entering, grown_g[...])
    db = nt(c_t, dscores) + tn(leaving, tailed[...])
    dstate[...] = nt(grown_g[...], c_t)  + dstate[...] * jnp.concatenate(
        [jnp.broadcast_to(kept[h : h + 1, :], (size, dstate.shape[1])) for h in range(heads)], axis=0
    )
    gbc = jnp.concatenate([db, dc], axis=0) * (bc_sig + bc_pre * bc_sig * (1.0 - bc_sig))
    later = ahead(gbc, bc_head[...])
    bc_head[...] = gbc[:, :EDGE]
    g_raw = bc_taps[:, 3:4] * later[0]
    for k in (1, 2, 3):
        g_raw = g_raw + bc_taps[:, 3 - k : 4 - k] * later[k]
    gzx_ref[wide : wide + 2 * half, :] = g_raw.astype(BF)
    for k in range(4):
        bc_acc[3 - k] = bc_acc[3 - k] + fold(gbc * bc_shifts[k])
    bc_acc[4] = bc_acc[4] + fold(gbc)
    rows = lax.broadcasted_iota(jnp.int32, (span, span), 0)
    cols = lax.broadcasted_iota(jnp.int32, (span, span), 1)
    da = exact(rsum[...], (rows >= cols).astype(F32)) + dt_acc[:, 0:1]
    g_steps = dsum[...] + rate * da
    g_dt = g_steps * sigmoid(dt_raw + dt_par_ref[:, 0:1])
    gzx_ref[wide + 2 * half :, :] = g_dt.astype(BF)
    dt_acc[:, 1:2] = dt_acc[:, 1:2] + jnp.sum(g_dt, axis=1, keepdims=True)
    dt_acc[:, 2:3] = dt_acc[:, 2:3] + jnp.sum(da * steps * rate, axis=1, keepdims=True)

    @pl.when(first)
    def _():
        for k in range(7):
            gx_sum_ref[:, k : k + 1] = jnp.sum(x_acc[k], axis=1, keepdims=True)
        for k in range(5):
            gbc_sum_ref[:, k : k + 1] = jnp.sum(bc_acc[k], axis=1, keepdims=True)
        gdt_sum_ref[...] = dt_acc[...]


def scan_forward(zx, taps, bc_taps, dt_par, heads, span=SPAN):
    inner = taps.shape[0]
    length = zx.shape[1]
    aux = bc_taps.shape[0]
    steps = dt_par.shape[0]
    states = aux // 2
    body = functools.partial(forward_kernel, heads)
    whole = lambda r, c: pl.BlockSpec((r, c), lambda i: (0, 0))
    return pl.pallas_call(
        body,
        grid=(length // span,),
        in_specs=[
            pl.BlockSpec((2 * inner, span), lambda i: (0, i)),
            pl.BlockSpec((aux, span), lambda i: (2 * inner // aux, i)),
            pl.BlockSpec((steps, span), lambda i: ((2 * inner + aux) // steps, i)),
            whole(inner, 8), whole(aux, 8), whole(steps, 8),
        ],
        out_specs=[
            pl.BlockSpec((inner, span), lambda i: (0, i)),
            pl.BlockSpec((1, span), lambda i: (0, i)),
            pl.BlockSpec((inner, states), lambda i: (i, 0)),
        ],
        out_shape=[
            jax.ShapeDtypeStruct((inner, length), BF),
            jax.ShapeDtypeStruct((1, length), F32),
            jax.ShapeDtypeStruct((length // span * inner, states), BF),
        ],
        scratch_shapes=[
            pltpu.VMEM((inner, states), F32),
            pltpu.VMEM((inner, EDGE), F32),
            pltpu.VMEM((aux, EDGE), F32),
            pltpu.VMEM((inner, span), F32),
            pltpu.VMEM((inner, span), BF),
        ],
        compiler_params=pltpu.CompilerParams(vmem_limit_bytes=48 * 2**20),
        name="scan_forward",
    )(zx, zx, zx, taps, bc_taps, dt_par)


def scan_backward(zx, entering, gn, coef, taps, bc_taps, dt_par, heads, span=SPAN):
    inner = taps.shape[0]
    length = zx.shape[1]
    aux = bc_taps.shape[0]
    steps = dt_par.shape[0]
    states = aux // 2
    count = length // span
    ratio = span // EDGE
    body = functools.partial(backward_kernel, heads)
    whole = lambda r, c: pl.BlockSpec((r, c), lambda i: (0, 0))
    rev = lambda i: count - 1 - i
    before = lambda i: jnp.maximum((count - 1 - i) * ratio - 1, 0)
    return pl.pallas_call(
        body,
        grid=(count,),
        in_specs=[
            pl.BlockSpec((2 * inner, span), lambda i: (0, rev(i))),
            pl.BlockSpec((2 * inner, EDGE), lambda i: (0, before(i))),
            pl.BlockSpec((aux, span), lambda i: (2 * inner // aux, rev(i))),
            pl.BlockSpec((aux, EDGE), lambda i: (2 * inner // aux, before(i))),
            pl.BlockSpec((steps, span), lambda i: ((2 * inner + aux) // steps, rev(i))),
            pl.BlockSpec((inner, states), lambda i: (rev(i), 0)),
            pl.BlockSpec((inner, span), lambda i: (0, rev(i))),
            pl.BlockSpec((1, span), lambda i: (0, rev(i))),
            whole(inner, 8), whole(aux, 8), whole(steps, 8),
        ],
        out_specs=[
            pl.BlockSpec((2 * inner + aux + steps, span), lambda i: (0, rev(i))),
            whole(inner, 8), whole(aux, 8), whole(steps, EDGE),
        ],
        out_shape=[
            jax.ShapeDtypeStruct((2 * inner + aux + steps, length), BF),
            jax.ShapeDtypeStruct((inner, 8), F32),
            jax.ShapeDtypeStruct((aux, 8), F32),
            jax.ShapeDtypeStruct((steps, EDGE), F32),
        ],
        scratch_shapes=[
            pltpu.VMEM((inner, states), F32),
            pltpu.VMEM((inner, EDGE), F32),
            pltpu.VMEM((aux, EDGE), F32),
            pltpu.VMEM((inner, span), F32),
            pltpu.VMEM((inner, span), F32),
            pltpu.VMEM((inner, span), BF),
            pltpu.VMEM((inner, span), BF),
            pltpu.VMEM((7, inner, EDGE), F32),
            pltpu.VMEM((5, aux, EDGE), F32),
            pltpu.VMEM((steps, EDGE), F32),
            pltpu.VMEM((steps, span), F32),
            pltpu.VMEM((steps, span), F32),
        ],
        compiler_params=pltpu.CompilerParams(vmem_limit_bytes=56 * 2**20),
        name="scan_backward",
    )(zx, zx, zx, zx, zx, entering, gn, coef, taps, bc_taps, dt_par)


def tie(value, *before):
    return lax.optimization_barrier((value, *before))[0]


def split(v, width):
    rows = []
    rest = v
    for _ in range(3):
        part = lax.reduce_precision(rest, 8, 7)
        rows.append(part.astype(BF))
        rest = rest - part
    return jnp.pad(jnp.stack(rows), ((0, 13), (0, width - v.shape[0])))


def joined(rows, size):
    return jnp.sum(rows[:3, :size].astype(F32), axis=0)


def flip(v, bit):
    return lax.ppermute(v, "row", [(i, i ^ bit) for i in range(4)])


class Scatter:
    def __init__(self, x, small=None):
        self.count = lax.axis_size("row")
        self.x, self.small = x, small
        if self.count != 4:
            self.sent = (x,)
            return
        me = lax.axis_index("row")
        self.size, width = x.shape[0] // 4, x.shape[1]
        half = width // 2
        self.half = half
        self.my_y, self.my_x = me // 2, me % 2
        blocks = x.reshape(2, 2, self.size, width)
        self.at_x = lambda i: lax.dynamic_slice(blocks, (0, i, 0, 0), (2, 1, self.size, half))[:, 0]
        self.at_y = lambda i: lax.dynamic_slice(blocks, (i, 0, 0, half), (1, 2, self.size, half))[0]
        send_x = self.at_x(1 - self.my_x)
        if small is not None:
            pieces = small.reshape(2, 2, self.size)
            there = lax.dynamic_index_in_dim(pieces, 1 - self.my_x, 1, keepdims=False)
            self.here = lax.dynamic_index_in_dim(pieces, self.my_x, 1, keepdims=False)
            send_x = jnp.concatenate(
                [send_x, jnp.stack([split(there[0], half), split(there[1], half)])], axis=1
            )
        self.sent = (send_x, self.at_y(1 - self.my_y))

    def first(self):
        self.got = self.sent
        if self.count == 4:
            self.got = (flip(self.sent[0], 1), flip(self.sent[1], 2))

    def second(self, *before):
        if self.count != 4:
            self.passed = self.ended = self.sent
            return
        got_x, got_y = tie(self.got, *before)
        pick = lambda v, i: lax.dynamic_index_in_dim(v, i, 0, keepdims=False).astype(F32)
        size = self.size
        both_x = lambda i: pick(self.at_x(self.my_x), i) + pick(got_x[:, :size], i)
        both_y = lambda i: pick(self.at_y(self.my_y), i) + pick(got_y, i)
        pass_x = both_x(1 - self.my_y).astype(BF)
        if self.small is not None:
            little = lambda i: pick(self.here, i) + joined(
                lax.dynamic_index_in_dim(got_x[:, size:], i, 0, keepdims=False), size
            )
            pass_x = jnp.concatenate([pass_x, split(little(1 - self.my_y), self.half)], axis=0)
            self.little = little(self.my_y)
        self.passed = (pass_x, both_y(1 - self.my_x).astype(BF))
        self.left = both_x(self.my_y)
        self.right = both_y(self.my_x)
        self.ended = (flip(self.passed[0], 2), flip(self.passed[1], 1))

    def last(self, *before):
        if self.count != 4:
            total = lax.psum_scatter(self.passed[0], "row", scatter_dimension=0, tiled=True).astype(F32)
            little = None
            if self.small is not None:
                size = total.shape[0]
                little = butterfly(self.small, "row")[0]
                little = lax.dynamic_slice_in_dim(little, lax.axis_index("row") * size, size, 0)
            return total, little
        end_x, end_y = tie(self.ended, *before)
        size = self.size
        left = self.left + end_x[:size].astype(F32)
        right = self.right + end_y.astype(F32)
        little = None
        if self.small is not None:
            little = self.little + joined(end_x[size:], size)
        return jnp.concatenate([left, right], axis=1), little


def butterfly(v, axis):
    count = lax.axis_size(axis)
    bit = 1
    while bit < count:
        v = v + lax.ppermute(v, axis, [(i, i ^ bit) for i in range(count)])
        bit *= 2
    return v


def sum_over_row_dp(v):
    if lax.axis_size("row") != 4:
        return lax.psum(butterfly(v, "row"), "dp")
    me = lax.axis_index("row")
    for bit in (1, 2):
        size = v.shape[0] // 2
        side = me // bit % 2
        away = lax.dynamic_slice_in_dim(v, (1 - side) * size, size, 0)
        keep = lax.dynamic_slice_in_dim(v, side * size, size, 0)
        v = keep + flip(away, bit)
    v = butterfly(v, "dp")
    for bit in (2, 1):
        other = flip(v, bit)
        first = me // bit % 2 == 0
        v = jnp.concatenate([jnp.where(first, v, other), jnp.where(first, other, v)], axis=0)
    return v


def other_col(v):
    return lax.ppermute(v, "col", [(0, 1), (1, 0)])


def dealt_rows(rows):
    half = rows[0].shape[1] // 2
    own = jnp.stack([r[:, :half] for r in rows])
    got = other_col(jnp.stack([r[:, half:] for r in rows]))
    at_start = lax.axis_index("col") == 0
    return jnp.concatenate([jnp.where(at_start, own, got), jnp.where(at_start, got, own)], axis=0)


def sent_back(dealt):
    groups = lax.axis_size("dp")
    me = lax.axis_index("dp")
    parts = []
    for hop in range(groups):
        piece = lax.dynamic_index_in_dim(dealt, (me + hop) % groups, 0, keepdims=False)
        if hop:
            piece = lax.ppermute(piece, "dp", [(i, (i + hop) % groups) for i in range(groups)])
        parts.append(piece)
    return parts


def in_given_order(parts, dest_group):
    groups = lax.axis_size("dp")
    hops = ((lax.axis_index("dp") - dest_group) % groups)[:, None, None]
    out = jnp.where(hops == 0, parts[0][None], jnp.zeros((), BF))
    for hop in range(1, groups):
        out = jnp.where(hops == hop, parts[hop][None], out)
    return out


def matmul(a, b, over_a, over_b):
    return lax.dot_general(a, b, (((over_a,), (over_b,)), ((), ())), preferred_element_type=F32)


def per_device(
    hidden, targets, lengths, dest_group, norm_gain, gate_input_weight, auxiliary_weight,
    conv_x, conv_x_bias, conv_bc, conv_bc_bias, dt_bias, a_log, d_skip, out_gain, output_weight,
):
    row_count = lax.axis_size("row")
    col_count = lax.axis_size("col")
    row_index = lax.axis_index("row")
    col_index = lax.axis_index("col")
    group_index = lax.axis_index("dp")
    seq_group, local_len, width_col = hidden.shape
    heads = gate_input_weight.shape[1]
    pair = gate_input_weight.shape[2]
    head_dim = pair // 2
    inner = heads * head_dim
    wide = heads * pair
    aux = conv_bc.shape[1]
    head_total = auxiliary_weight.shape[1] - aux
    steps = -(-heads // 16) * 16
    seq_col = seq_group // col_count
    model_width = width_col * col_count
    inner_width = inner * row_count
    all_tokens = lengths.shape[0] * local_len * row_count
    valid_count = jnp.sum(lengths).astype(F32)
    group_lengths = lax.dynamic_slice_in_dim(lengths, group_index * seq_group, seq_group, 0)
    own_lengths = lax.dynamic_slice_in_dim(group_lengths, col_index * seq_col, seq_col, 0)

    def widened(v):
        mine = lax.dynamic_slice_in_dim(v, col_index * seq_col, seq_col, 0)
        theirs = lax.dynamic_slice_in_dim(v, (1 - col_index) * seq_col, seq_col, 0)
        return jnp.concatenate([mine, other_col(theirs)], axis=2)

    u_low = widened(hidden)
    gain = jnp.concatenate([norm_gain, other_col(norm_gain)])
    u = [u_low[k].astype(F32) for k in range(seq_col)]
    inv_rms = [lax.rsqrt(jnp.mean(v * v, axis=1, keepdims=True) + EPSILON) for v in u]
    spread = lambda v: lax.all_gather(v, "row", axis=0, tiled=True)
    normed = [(v * r * gain[None, :]).astype(BF) for v, r in zip(u, inv_rms, strict=True)]
    scaled = [spread(normed[0])]
    for v in normed[1:]:
        scaled.append(spread(tie(v, scaled[-1])))
    in_own = tie(
        jnp.concatenate(
            [
                gate_input_weight.reshape(width_col, wide),
                auxiliary_weight[:, :aux],
                lax.dynamic_slice_in_dim(auxiliary_weight, aux + row_index * heads, heads, 1),
                jnp.zeros((width_col, steps - heads), BF),
            ],
            axis=1,
        )
    )
    out_own = output_weight.reshape(inner, width_col)
    in_weight = tie(jnp.concatenate([in_own, other_col(in_own)], axis=0))
    out_weight = tie(jnp.concatenate([out_own, other_col(out_own)], axis=1))

    scaled[0] = tie(scaled[0], in_weight)

    column = lambda v: v.reshape(-1, 1)
    taps = jnp.concatenate(
        [
            conv_x.reshape(-1, inner).T,
            column(conv_x_bias),
            column(jnp.repeat(d_skip, head_dim)),
            column(out_gain),
            jnp.zeros((inner, 1), F32),
        ],
        axis=1,
    )
    bc_taps = jnp.concatenate([conv_bc.T, column(conv_bc_bias), jnp.zeros((aux, 3), F32)], axis=1)
    dt_par = jnp.pad(jnp.stack([dt_bias, a_log], axis=1), ((0, steps - heads), (0, 6)))

    targets_own = widened(targets)
    positions = row_index * local_len + jnp.arange(local_len, dtype=jnp.int32)

    zx, gated, entering, scatters = [], [], [], []
    result, g_result, g_rows, coef = [], [], [], []
    loss_part = jnp.zeros((), F32)

    def finish(k, *before):
        nonlocal loss_part
        summed, total_square = scatters[k].last(*before)
        gate_inv = lax.rsqrt(total_square / inner_width + EPSILON)[:, None]
        branch = summed * gate_inv
        full = u[k] + branch
        valid = (positions < own_lengths[k]).astype(F32)[:, None]
        difference = (full - targets_own[k].astype(F32)) * valid
        loss_part = loss_part + jnp.sum(difference * difference)
        grad = difference * (all_tokens / valid_count)
        result.append(full.astype(BF))
        g_result.append(grad)
        share = gate_inv[:, 0] * gate_inv[:, 0] * jnp.sum(grad * branch, axis=1) / inner_width
        placed = lax.dynamic_update_slice_in_dim(
            jnp.zeros((local_len * row_count,), F32), share, row_index * local_len, 0
        )
        coef.append(butterfly(placed[None, :], "row"))
        sent = (grad * gate_inv).astype(BF)
        g_rows.append(spread(tie(sent, *g_rows[-1:])))
        return sent

    for k in range(seq_col):
        source = scaled[k] if k == 0 else tie(scaled[k], *scatters[-1].sent)
        projected = matmul(in_weight, source, 0, 1)
        if k > 0:
            scatters[-1].second(projected)
            projected = tie(projected, *scatters[-1].passed)
        zx.append(projected)
        g, square, e = scan_forward(projected, taps, bc_taps, dt_par, heads)
        gated.append(g)
        entering.append(e)
        if k > 0:
            g = tie(g, finish(k - 1, g))
        part = matmul(g, out_weight, 0, 0).astype(BF)
        scatters.append(Scatter(part, square))
        scatters[-1].first()
    scatters[-1].second()
    finish(seq_col - 1)

    g_in, scatters = [], []
    sums = [0.0, 0.0, 0.0]
    for k in range(seq_col):
        final = k == seq_col - 1
        whole = g_rows[k] if k == 0 else tie(g_rows[k], g_in[-1], coef[k])
        if k == 0:
            dealt_output = dealt_rows(result)
            output_parts = sent_back(dealt_output)
        gn = matmul(out_weight, whole, 1, 1)
        if final:
            w_out_part = sum(
                matmul(gated[i], whole if i == k else g_rows[i], 1, 0) for i in range(seq_col)
            )
            received = tie(other_col(w_out_part[:, width_col:].astype(BF)), gn)
            w_out_low = (w_out_part[:, :width_col] + received.astype(F32)).astype(BF)
            w_out_sum = lax.psum(w_out_low, "dp")
            if k > 0:
                scatters.append(Scatter(matmul(tie(g_in[-1], w_out_low), in_weight, 0, 1).astype(BF)))
        elif k > 0:
            scatters.append(Scatter(matmul(g_in[-1], in_weight, 0, 1).astype(BF)))
        if k > 0:
            scatters[-1].first()
            gn = tie(gn, *scatters[-1].sent)
        g, gx, gbc, gdt = scan_backward(
            zx[k], entering[k], gn, coef[k], taps, bc_taps, dt_par, heads
        )
        sums = [a + b for a, b in zip(sums, (gx, gbc, gdt), strict=True)]
        if k == 0:
            g = tie(g, *output_parts)
        if k > 0:
            scatters[-1].second(g)
            g = tie(g, *scatters[-1].passed)
        if final:
            g = tie(g, w_out_sum)
        g_in.append(g)

    scatters.append(Scatter(matmul(g_in[-1], in_weight, 0, 1).astype(BF)))
    scatters[-1].first()
    half_of = lambda start, g: sum(
        matmul(scaled[i][:, start : start + width_col], g[i], 0, 1) for i in range(seq_col)
    )
    g_wide = [g[:wide] for g in g_in]
    g_wide[-1] = tie(g_wide[-1], *scatters[-1].sent)
    in_there = half_of(width_col, g_wide).astype(BF)
    scatters[-1].second(in_there)
    g_wide[-1] = tie(g_wide[-1], *scatters[-1].passed)
    in_low = (half_of(0, g_wide) + other_col(in_there).astype(F32)).astype(BF)
    in_low = tie(in_low.reshape(width_col, heads, pair))
    w_zx = lax.psum(in_low, "dp")
    g_aux = [g[wide:] for g in g_in]
    g_aux[-1] = tie(g_aux[-1], in_low)
    aux_part = sum(matmul(scaled[i], g_aux[i], 0, 1) for i in range(seq_col))
    aux_half = aux_part[:width_col] + other_col(aux_part[width_col:])
    aux_half = jnp.concatenate(
        [
            aux_half[:, :aux],
            lax.dynamic_update_slice_in_dim(
                jnp.zeros((width_col, head_total), F32),
                aux_half[:, aux : aux + heads],
                row_index * heads,
                1,
            ),
        ],
        axis=1,
    )
    w_aux = sum_over_row_dp(aux_half)
    gain_part = jnp.zeros((model_width,), F32)
    g_u = []
    for k in range(seq_col):
        g_scaled, _ = scatters[k].last()
        gain_part = gain_part + jnp.sum(g_scaled * u[k] * inv_rms[k], axis=0)
        weighted = g_scaled * gain[None, :]
        dot = jnp.sum(weighted * u[k], axis=1, keepdims=True) / model_width
        cube = inv_rms[k] * inv_rms[k] * inv_rms[k]
        g_u.append((g_result[k] + inv_rms[k] * weighted - u[k] * (cube * dot)).astype(BF))
    hidden_parts = sent_back(tie(dealt_rows(g_u), w_zx))

    gx, gbc, gdt = sums
    flat = jnp.concatenate(
        [gx.reshape(-1), gdt[:, 1:3].reshape(-1), gbc.reshape(-1), loss_part[None]]
    )
    vector = jnp.concatenate([flat, gain_part[:width_col]]) + other_col(
        jnp.concatenate([flat, gain_part[width_col:]])
    )
    own_size = inner * 8 + steps * 2
    vector = jnp.concatenate([vector[:own_size], butterfly(vector[own_size:], "row")])
    vector = butterfly(vector, "dp")
    gx = vector[: inner * 8].reshape(inner, 8)
    gdt = vector[inner * 8 : own_size].reshape(steps, 2)
    shared = vector[own_size:]
    gbc = shared[: aux * 8].reshape(aux, 8)
    loss = shared[aux * 8] * 0.5 / valid_count
    gain_sum = shared[aux * 8 + 1 :]
    return (
        loss,
        in_given_order(output_parts, dest_group),
        in_given_order(hidden_parts, dest_group),
        gain_sum,
        w_zx.astype(F32),
        w_aux.astype(F32),
        gx[:, :4].T.reshape(4, heads, head_dim),
        gx[:, 4].reshape(heads, head_dim),
        gbc[:, :4].T,
        gbc[:, 4],
        gdt[:heads, 0],
        gdt[:heads, 1],
        gx[:, 5].reshape(heads, head_dim).sum(axis=1),
        gx[:, 6].reshape(heads, head_dim),
        w_out_sum.astype(F32).reshape(heads, head_dim, width_col),
    )


def solution(mesh):
    placed = (
        P("dp", "row", "col"),
        P("dp", "row", "col"),
        P(),
        P("dp"),
        P("col"),
        P("col", "row", None),
        P("col", None),
        P(None, "row", None),
        P("row", None),
        P(),
        P(),
        P("row"),
        P("row"),
        P("row"),
        P("row", None),
        P("row", None, "col"),
    )
    return jax.shard_map(
        per_device,
        mesh=mesh,
        in_specs=placed,
        out_specs=(
            P(),
            P("dp", "row", "col"),
            P("dp", "row", "col"),
            P("col"),
            P("col", "row", None),
            P("col", None),
            P(None, "row", None),
            P("row", None),
            P(),
            P(),
            P("row"),
            P("row"),
            P("row"),
            P("row", None),
            P("row", None, "col"),
        ),
        check_vma=False,
    )
```

```python
import functools
import jax
import jax.numpy as jnp
from jax import lax
from jax.experimental import pallas as pl
from jax.experimental.pallas import tpu as pltpu
from jax.sharding import PartitionSpec as P

BF = jnp.bfloat16
F32 = jnp.float32
SPAN = 512
PART = 128
LOG2E = 1.4426950408889634
EDGE = 128
EPSILON = 1e-05


def nn(a, b):
    return lax.dot_general(a, b, (((1,), (0,)), ((), ())), preferred_element_type=F32)


def nt(a, b):
    return lax.dot_general(a, b, (((1,), (1,)), ((), ())), preferred_element_type=F32)


def tn(a, b):
    return lax.dot_general(a, b, (((0,), (0,)), ((), ())), preferred_element_type=F32)


def exact(a, b):
    return lax.dot_general(
        a, b, (((1,), (0,)), ((), ())), precision=lax.Precision.HIGHEST, preferred_element_type=F32
    )


def sigmoid(v):
    return 0.5 * jnp.tanh(0.5 * v) + 0.5


def softplus(v):
    return jnp.maximum(v, 0.0) + jnp.log1p(jnp.exp(-jnp.abs(v)))


def wide(v, span):
    return jnp.concatenate([v] * (span // v.shape[1]), axis=1)


def taps_at(taps_ref, at, span):
    return lambda k: wide(taps_ref[k, at, :], span)


def spread_taps(from_ref, to_ref):
    for k in range(to_ref.shape[0]):
        to_ref[k] = jnp.broadcast_to(from_ref[:, k : k + 1], to_ref.shape[1:])


def move_matrix(ahead):
    rows = lax.broadcasted_iota(jnp.int32, (2 * EDGE, EDGE), 0)
    cols = lax.broadcasted_iota(jnp.int32, (2 * EDGE, EDGE), 1)
    moves = [rows == (cols + k if ahead else cols + EDGE - k) for k in (1, 2, 3)]
    return jnp.concatenate([m.astype(F32).astype(BF) for m in moves], axis=1)


def moved(joined, matrix):
    size = joined.shape[0]
    parts = range(joined.shape[1] // EDGE - 1)
    low = joined.astype(BF)
    stacked = jnp.concatenate([low[:, q * EDGE : (q + 2) * EDGE] for q in parts], axis=0)
    out = nn(stacked, matrix)
    return [
        jnp.concatenate(
            [out[q * size : (q + 1) * size, k * EDGE : (k + 1) * EDGE] for q in parts], axis=1
        )
        for k in range(3)
    ]


def conv_of(before, now, tap, matrix):
    one, two, three = moved(jnp.concatenate([before, now], axis=1), matrix)
    return tap(4) + tap(3) * now + tap(2) * one + tap(1) * two + tap(0) * three


def conv_back(now, after, tap, matrix):
    one, two, three = moved(jnp.concatenate([now, after], axis=1), matrix)
    return tap(3) * now + tap(2) * one + tap(1) * two + tap(0) * three, (one, two, three)


def fold(v):
    total = v[:, :EDGE]
    for k in range(1, v.shape[1] // EDGE):
        total = total + v[:, k * EDGE : (k + 1) * EDGE]
    return total


def lanes(q):
    return slice(q * PART, (q + 1) * PART)


def span_common(bc_before, bc_now, dt_raw, bc_tap, dt_par, matrix):
    pre = conv_of(bc_before, bc_now, bc_tap, matrix)
    sig = sigmoid(pre)
    act = pre * sig
    half = act.shape[0] // 2
    b_t = act[:half].astype(BF)
    c_t = act[half:].astype(BF)
    parts = range(bc_now.shape[1] // PART)
    rows = lax.broadcasted_iota(jnp.int32, (PART, PART), 0)
    cols = lax.broadcasted_iota(jnp.int32, (PART, PART), 1)
    causal = rows <= cols
    steps = softplus(dt_raw + dt_par[:, 0:1])
    rate = -jnp.exp(dt_par[:, 1:2])
    gone = steps * (rate * LOG2E)
    decay = [exact(gone[:, lanes(q)], causal.astype(F32)) for q in parts]
    last = [d[:, PART - 1 :] for d in decay]
    decay_n = [d.T for d in decay]
    left = jnp.concatenate([jnp.exp2(e - d) for e, d in zip(last, decay)], axis=1)
    kept = [jnp.exp2(e) for e in last]
    decay = jnp.concatenate(decay, axis=1)
    grown = jnp.exp2(decay)
    b_n = [b_t[:, lanes(q)].astype(F32).T.astype(BF) for q in parts]
    scores = [jnp.where(causal, nn(b_n[q], c_t[:, lanes(q)]), 0.0) for q in parts]
    return pre, sig, b_t, c_t, b_n, scores, causal, steps, rate, decay, decay_n, grown, left, kept


def forward_kernel(
    heads, zx_ref, bc_ref, dt_ref, taps_ref, bc_taps_ref, dt_par_ref,
    gated_ref, square_ref, enter_ref,
    state, x_tail, bc_tail, carry, x_all, xd_all, tailed, scores_all, x_taps, bc_taps, matrix_ref,
):
    span = zx_ref.shape[1]
    inner = state.shape[0]
    size = inner // heads
    parts = range(span // PART)

    @pl.when(pl.program_id(0) == 0)
    def _():
        state[...] = jnp.zeros_like(state)
        x_tail[...] = jnp.zeros_like(x_tail)
        bc_tail[...] = jnp.zeros_like(bc_tail)
        spread_taps(taps_ref, x_taps)
        spread_taps(bc_taps_ref, bc_taps)
        matrix_ref[...] = move_matrix(False)

    matrix = matrix_ref[...]
    bc_now = bc_ref[...]
    _, _, _, c_t, b_n, scores, _, steps, _, decay, decay_n, grown, left, kept = span_common(
        bc_tail[...], bc_now, dt_ref[...], taps_at(bc_taps, slice(None), span), dt_par_ref[...], matrix
    )
    bc_tail[...] = bc_now[:, span - EDGE :]
    for q in parts:
        scores_all[q] = scores[q]
    for h in range(heads):
        at = slice(h * size, (h + 1) * size)
        x_raw = zx_ref[(2 * h + 1) * size : (2 * h + 2) * size, :]
        pre = conv_of(x_tail[at, :], x_raw, taps_at(x_taps, at, span), matrix)
        x_tail[at, :] = x_raw[:, span - EDGE :]
        x = pre * sigmoid(pre)
        xd = x * steps[h : h + 1, :]
        x_all[at, :] = x
        xd_all[at, :] = xd.astype(BF)
        tailed[at, :] = (xd * left[h : h + 1, :]).astype(BF)
    for q in parts:
        entering = state[...].astype(BF)
        enter_ref[q * inner : (q + 1) * inner, :] = entering
        carry[:, lanes(q)] = nn(entering, c_t[:, lanes(q)])
        more = nn(tailed[:, lanes(q)], b_n[q])
        for h in range(heads):
            at = slice(h * size, (h + 1) * size)
            state[at, :] = state[at, :] * kept[q][h : h + 1, :] + more[at, :]
    square = jnp.zeros((size, span), F32)
    for h in range(heads):
        at = slice(h * size, (h + 1) * size)
        z = zx_ref[2 * h * size : (2 * h + 1) * size, :]
        tap = taps_at(x_taps, at, span)
        mixed = []
        for q in parts:
            gap = decay[h : h + 1, lanes(q)] - decay_n[q][:, h : h + 1]
            mixing = scores_all[q] * jnp.exp2(jnp.minimum(gap, 0.0))
            mixed.append(nn(xd_all[at, lanes(q)], mixing.astype(BF)))
        y = jnp.concatenate(mixed, axis=1) + carry[at, :] * grown[h : h + 1, :]
        y = y + tap(5) * x_all[at, :]
        gated = y * (z * sigmoid(z))
        square = square + gated * gated
        gated_ref[at, :] = (gated * tap(6)).astype(BF)
    square_ref[...] = jnp.sum(square, axis=0, keepdims=True)


def backward_kernel(
    heads, zx_ref, zx_before_ref, bc_ref, bc_before_ref, dt_ref, enter_ref, gn_ref, coef_ref,
    taps_ref, bc_taps_ref, dt_par_ref,
    gzx_ref, gx_sum_ref, gbc_sum_ref, gdt_sum_ref,
    dstate, x_head, bc_head, carry, from_state, grown_g, tailed, x_acc, bc_acc, dt_acc, rsum, dsum,
    x_all, slope_all, dxd_all, gy_all, scores_all, dscores_all, held_all, x_taps, bc_taps_all, matrix_ref,
    back_matrix_ref,
):
    span = zx_ref.shape[1]
    inner = dstate.shape[0]
    size = inner // heads
    half = bc_ref.shape[0] // 2
    wide = zx_ref.shape[0]
    parts = range(span // PART)
    step = pl.program_id(0)
    count = pl.num_programs(0)
    first = step == count - 1

    @pl.when(step == 0)
    def _():
        dstate[...] = jnp.zeros_like(dstate)
        x_head[...] = jnp.zeros_like(x_head)
        bc_head[...] = jnp.zeros_like(bc_head)
        x_acc[...] = jnp.zeros_like(x_acc)
        bc_acc[...] = jnp.zeros_like(bc_acc)
        dt_acc[...] = jnp.zeros_like(dt_acc)
        rsum[...] = jnp.zeros_like(rsum)
        dsum[...] = jnp.zeros_like(dsum)
        held_all[...] = jnp.zeros_like(held_all)
        spread_taps(taps_ref, x_taps)
        spread_taps(bc_taps_ref, bc_taps_all)
        matrix_ref[...] = move_matrix(False)
        back_matrix_ref[...] = move_matrix(True)

    matrix, back_matrix = matrix_ref[...], back_matrix_ref[...]
    live = jnp.where(first, 0.0, 1.0)
    bc_tap = taps_at(bc_taps_all, slice(None), span)
    dt_raw = dt_ref[...]
    bc_now = bc_ref[...]
    (
        bc_pre, bc_sig, b_t, c_t, b_n, scores, causal, steps, rate, decay, decay_n, grown, left, kept
    ) = span_common(bc_before_ref[...] * live, bc_now, dt_raw, bc_tap, dt_par_ref[...], matrix)
    for q in parts:
        scores_all[q] = scores[q]
        dscores_all[q] = jnp.zeros((PART, PART), F32)
        carry[:, lanes(q)] = nn(enter_ref[q * inner : (q + 1) * inner, :], c_t[:, lanes(q)])
    coef = coef_ref[...]
    for h in range(heads):
        at = slice(h * size, (h + 1) * size)
        z = zx_ref[2 * h * size : (2 * h + 1) * size, :]
        x_raw = zx_ref[(2 * h + 1) * size : (2 * h + 2) * size, :]
        x_before = zx_before_ref[(2 * h + 1) * size : (2 * h + 2) * size, :] * live
        tap = taps_at(x_taps, at, span)
        pre = conv_of(x_before, x_raw, tap, matrix)
        sig = sigmoid(pre)
        x = pre * sig
        x_all[at, :] = x
        slope_all[at, :] = sig + x * (1.0 - sig)
        xd = x * steps[h : h + 1, :]
        xd_low = xd.astype(BF)
        tailed[at, :] = (xd * left[h : h + 1, :]).astype(BF)
        ratios, mixings, mixed = [], [], []
        for q in parts:
            gap = decay[h : h + 1, lanes(q)] - decay_n[q][:, h : h + 1]
            ratios.append(jnp.exp2(jnp.minimum(gap, 0.0)))
            mixings.append((scores_all[q] * ratios[q]).astype(BF))
            mixed.append(nn(xd_low[:, lanes(q)], mixings[q]))
        grown_h = grown[h : h + 1, :]
        y_scan = jnp.concatenate(mixed, axis=1) + carry[at, :] * grown_h
        y = y_scan + tap(5) * x
        zsig = sigmoid(z)
        silu_z = z * zsig
        gated = y * silu_z
        gn = gn_ref[at, :].astype(F32)
        g_gated = tap(6) * gn - gated * coef
        gy = g_gated * silu_z
        gzx_ref[2 * h * size : (2 * h + 1) * size, :] = (
            g_gated * y * (zsig + silu_z * (1.0 - zsig))
        ).astype(BF)
        gy_low = gy.astype(BF)
        gy_all[at, :] = gy_low
        grown_g[at, :] = (gy * grown_h).astype(BF)
        rsum[h : h + 1, :] = jnp.sum(gy_low.astype(F32) * y_scan, axis=0, keepdims=True)
        x_acc[5, at, :] = x_acc[5, at, :] + fold(gy * x)
        x_acc[6, at, :] = x_acc[6, at, :] + fold(gn * gated)
        for q in parts:
            dxd_all[at, lanes(q)] = nt(gy_low[:, lanes(q)], mixings[q])
            dscores_all[q] = dscores_all[q] + tn(xd_low[:, lanes(q)], gy_low[:, lanes(q)]) * ratios[q]
    db, dc, flows = [], [], []
    for q in reversed(parts):
        entering = enter_ref[q * inner : (q + 1) * inner, :]
        leaving = dstate[...].astype(BF)
        from_state[:, lanes(q)] = nn(leaving, b_t[:, lanes(q)])
        low = jnp.where(causal, dscores_all[q], 0.0).astype(BF)
        dc.insert(0, nn(b_t[:, lanes(q)], low) + tn(entering, grown_g[:, lanes(q)]))
        db.insert(0, nt(c_t[:, lanes(q)], low) + tn(leaving, tailed[:, lanes(q)]))
        more = nt(grown_g[:, lanes(q)], c_t[:, lanes(q)])
        for h in range(heads):
            at = slice(h * size, (h + 1) * size)
            passed = dstate[at, :] * kept[q][h : h + 1, :]
            held_all[q, h : h + 1, :] = jnp.sum(passed * entering[at, :].astype(F32), axis=0, keepdims=True)
            dstate[at, :] = passed + more[at, :]
    for h in range(heads):
        at = slice(h * size, (h + 1) * size)
        x_raw = zx_ref[(2 * h + 1) * size : (2 * h + 2) * size, :]
        tap = taps_at(x_taps, at, span)
        x = x_all[at, :]
        steps_h = steps[h : h + 1, :]
        dx_state = from_state[at, :] * left[h : h + 1, :]
        dxd = dxd_all[at, :] + dx_state
        xd_wide = (x * steps_h).astype(BF).astype(F32)
        rsum[h : h + 1, :] = rsum[h : h + 1, :] - jnp.sum(xd_wide * dxd, axis=0, keepdims=True)
        dsum[h : h + 1, :] = jnp.sum(x * dxd, axis=0, keepdims=True)
        held = jnp.sum(xd_wide * dx_state, axis=0, keepdims=True)
        for q in parts:
            held_all[q, h : h + 1, :] = held_all[q, h : h + 1, :] + held[:, lanes(q)]
        dx = dxd * steps_h + tap(5) * gy_all[at, :].astype(F32)
        gpre = dx * slope_all[at, :]
        g_raw, later = conv_back(gpre, x_head[at, :], tap, back_matrix)
        x_head[at, :] = gpre[:, :EDGE]
        gzx_ref[(2 * h + 1) * size : (2 * h + 2) * size, :] = g_raw.astype(BF)
        for k, moved_g in enumerate((gpre, *later)):
            x_acc[3 - k, at, :] = x_acc[3 - k, at, :] + fold(moved_g * x_raw)
        x_acc[4, at, :] = x_acc[4, at, :] + fold(gpre)
    gbc = jnp.concatenate([jnp.concatenate(db, axis=1), jnp.concatenate(dc, axis=1)], axis=0)
    gbc = gbc * (bc_sig + bc_pre * bc_sig * (1.0 - bc_sig))
    g_raw, later = conv_back(gbc, bc_head[...], bc_tap, back_matrix)
    bc_head[...] = gbc[:, :EDGE]
    gzx_ref[wide : wide + 2 * half, :] = g_raw.astype(BF)
    for k, moved_g in enumerate((gbc, *later)):
        bc_acc[3 - k] = bc_acc[3 - k] + fold(moved_g * bc_now)
    bc_acc[4] = bc_acc[4] + fold(gbc)
    after = jnp.logical_or(
        jnp.logical_not(causal),
        lax.broadcasted_iota(jnp.int32, (PART, PART), 0) == lax.broadcasted_iota(jnp.int32, (PART, PART), 1),
    ).astype(F32)
    da = jnp.concatenate(
        [
            exact(rsum[:, lanes(q)], after) + jnp.sum(held_all[q], axis=1, keepdims=True)
            for q in parts
        ],
        axis=1,
    )
    g_steps = dsum[...] + rate * da
    g_dt = g_steps * sigmoid(dt_raw + dt_par_ref[:, 0:1])
    gzx_ref[wide + 2 * half :, :] = g_dt.astype(BF)
    dt_acc[:, 1:2] = dt_acc[:, 1:2] + jnp.sum(g_dt, axis=1, keepdims=True)
    dt_acc[:, 2:3] = dt_acc[:, 2:3] + jnp.sum(da * steps * rate, axis=1, keepdims=True)

    @pl.when(first)
    def _():
        for k in range(7):
            gx_sum_ref[:, k : k + 1] = jnp.sum(x_acc[k], axis=1, keepdims=True)
        for k in range(5):
            gbc_sum_ref[:, k : k + 1] = jnp.sum(bc_acc[k], axis=1, keepdims=True)
        gdt_sum_ref[...] = dt_acc[...]


def scan_forward(zx, taps, bc_taps, dt_par, heads, span=SPAN):
    inner = taps.shape[0]
    length = zx.shape[1]
    aux = bc_taps.shape[0]
    steps = dt_par.shape[0]
    states = aux // 2
    body = functools.partial(forward_kernel, heads)
    whole = lambda r, c: pl.BlockSpec((r, c), lambda i: (0, 0))
    return pl.pallas_call(
        body,
        grid=(length // span,),
        in_specs=[
            pl.BlockSpec((2 * inner, span), lambda i: (0, i)),
            pl.BlockSpec((aux, span), lambda i: (2 * inner // aux, i)),
            pl.BlockSpec((steps, span), lambda i: ((2 * inner + aux) // steps, i)),
            whole(inner, 8), whole(aux, 8), whole(steps, 8),
        ],
        out_specs=[
            pl.BlockSpec((inner, span), lambda i: (0, i)),
            pl.BlockSpec((1, span), lambda i: (0, i)),
            pl.BlockSpec((span // PART * inner, states), lambda i: (i, 0)),
        ],
        out_shape=[
            jax.ShapeDtypeStruct((inner, length), BF),
            jax.ShapeDtypeStruct((1, length), F32),
            jax.ShapeDtypeStruct((length // PART * inner, states), BF),
        ],
        scratch_shapes=[
            pltpu.VMEM((inner, states), F32),
            pltpu.VMEM((inner, EDGE), F32),
            pltpu.VMEM((aux, EDGE), F32),
            pltpu.VMEM((inner, span), F32),
            pltpu.VMEM((inner, span), F32),
            pltpu.VMEM((inner, span), BF),
            pltpu.VMEM((inner, span), BF),
            pltpu.VMEM((span // PART, PART, PART), F32),
            pltpu.VMEM((7, inner, EDGE), F32),
            pltpu.VMEM((5, aux, EDGE), F32),
            pltpu.VMEM((2 * EDGE, 3 * EDGE), BF),
        ],
        compiler_params=pltpu.CompilerParams(vmem_limit_bytes=48 * 2**20),
        name="scan_forward",
    )(zx, zx, zx, taps, bc_taps, dt_par)


def scan_backward(zx, entering, gn, coef, taps, bc_taps, dt_par, heads, span=SPAN):
    inner = taps.shape[0]
    length = zx.shape[1]
    aux = bc_taps.shape[0]
    steps = dt_par.shape[0]
    states = aux // 2
    count = length // span
    ratio = span // EDGE
    body = functools.partial(backward_kernel, heads)
    whole = lambda r, c: pl.BlockSpec((r, c), lambda i: (0, 0))
    rev = lambda i: count - 1 - i
    before = lambda i: jnp.maximum((count - 1 - i) * ratio - 1, 0)
    return pl.pallas_call(
        body,
        grid=(count,),
        in_specs=[
            pl.BlockSpec((2 * inner, span), lambda i: (0, rev(i))),
            pl.BlockSpec((2 * inner, EDGE), lambda i: (0, before(i))),
            pl.BlockSpec((aux, span), lambda i: (2 * inner // aux, rev(i))),
            pl.BlockSpec((aux, EDGE), lambda i: (2 * inner // aux, before(i))),
            pl.BlockSpec((steps, span), lambda i: ((2 * inner + aux) // steps, rev(i))),
            pl.BlockSpec((span // PART * inner, states), lambda i: (rev(i), 0)),
            pl.BlockSpec((inner, span), lambda i: (0, rev(i))),
            pl.BlockSpec((1, span), lambda i: (0, rev(i))),
            whole(inner, 8), whole(aux, 8), whole(steps, 8),
        ],
        out_specs=[
            pl.BlockSpec((2 * inner + aux + steps, span), lambda i: (0, rev(i))),
            whole(inner, 8), whole(aux, 8), whole(steps, EDGE),
        ],
        out_shape=[
            jax.ShapeDtypeStruct((2 * inner + aux + steps, length), BF),
            jax.ShapeDtypeStruct((inner, 8), F32),
            jax.ShapeDtypeStruct((aux, 8), F32),
            jax.ShapeDtypeStruct((steps, EDGE), F32),
        ],
        scratch_shapes=[
            pltpu.VMEM((inner, states), F32),
            pltpu.VMEM((inner, EDGE), F32),
            pltpu.VMEM((aux, EDGE), F32),
            pltpu.VMEM((inner, span), F32),
            pltpu.VMEM((inner, span), F32),
            pltpu.VMEM((inner, span), BF),
            pltpu.VMEM((inner, span), BF),
            pltpu.VMEM((7, inner, EDGE), F32),
            pltpu.VMEM((5, aux, EDGE), F32),
            pltpu.VMEM((steps, EDGE), F32),
            pltpu.VMEM((steps, span), F32),
            pltpu.VMEM((steps, span), F32),
            pltpu.VMEM((inner, span), F32),
            pltpu.VMEM((inner, span), F32),
            pltpu.VMEM((inner, span), F32),
            pltpu.VMEM((inner, span), BF),
            pltpu.VMEM((span // PART, PART, PART), F32),
            pltpu.VMEM((span // PART, PART, PART), F32),
            pltpu.VMEM((span // PART, steps, PART), F32),
            pltpu.VMEM((7, inner, EDGE), F32),
            pltpu.VMEM((5, aux, EDGE), F32),
            pltpu.VMEM((2 * EDGE, 3 * EDGE), BF),
            pltpu.VMEM((2 * EDGE, 3 * EDGE), BF),
        ],
        compiler_params=pltpu.CompilerParams(vmem_limit_bytes=56 * 2**20),
        name="scan_backward",
    )(zx, zx, zx, zx, zx, entering, gn, coef, taps, bc_taps, dt_par)


def tie(value, *before):
    return lax.optimization_barrier((value, *before))[0]


def split(v, width):
    rows = []
    rest = v
    for _ in range(3):
        part = lax.reduce_precision(rest, 8, 7)
        rows.append(part.astype(BF))
        rest = rest - part
    return jnp.pad(jnp.stack(rows), ((0, 13), (0, width - v.shape[0])))


def joined(rows, size):
    return jnp.sum(rows[:3, :size].astype(F32), axis=0)


def flip(v, bit):
    return lax.ppermute(v, "row", [(i, i ^ bit) for i in range(4)])


class Scatter:
    def __init__(self, left, right, small=None):
        self.count = lax.axis_size("row")
        self.small = small
        if self.count != 4:
            self.sent = (jnp.concatenate([left, right], axis=1),)
            return
        me = lax.axis_index("row")
        self.size, half = left.shape[0] // 4, left.shape[1]
        self.half = half
        self.my_y, self.my_x = me // 2, me % 2
        left = left.reshape(2, 2, self.size, half)
        right = right.reshape(2, 2, self.size, half)
        self.at_x = lambda i: lax.dynamic_index_in_dim(left, i, 1, keepdims=False)
        self.at_y = lambda i: lax.dynamic_index_in_dim(right, i, 0, keepdims=False)
        send_x = self.at_x(1 - self.my_x)
        if small is not None:
            pieces = small.reshape(2, 2, self.size)
            there = lax.dynamic_index_in_dim(pieces, 1 - self.my_x, 1, keepdims=False)
            self.here = lax.dynamic_index_in_dim(pieces, self.my_x, 1, keepdims=False)
            send_x = jnp.concatenate(
                [send_x, jnp.stack([split(there[0], half), split(there[1], half)])], axis=1
            )
        self.sent = (send_x, self.at_y(1 - self.my_y))

    def first(self):
        self.got = self.sent
        if self.count == 4:
            self.got = (flip(self.sent[0], 1), flip(self.sent[1], 2))

    def second(self, *before):
        if self.count != 4:
            self.passed = self.ended = self.sent
            return
        got_x, got_y = tie(self.got, *before)
        pick = lambda v, i: lax.dynamic_index_in_dim(v, i, 0, keepdims=False).astype(F32)
        size = self.size
        both_x = lambda i: pick(self.at_x(self.my_x), i) + pick(got_x[:, :size], i)
        both_y = lambda i: pick(self.at_y(self.my_y), i) + pick(got_y, i)
        pass_x = both_x(1 - self.my_y).astype(BF)
        if self.small is not None:
            little = lambda i: pick(self.here, i) + joined(
                lax.dynamic_index_in_dim(got_x[:, size:], i, 0, keepdims=False), size
            )
            pass_x = jnp.concatenate([pass_x, split(little(1 - self.my_y), self.half)], axis=0)
            self.little = little(self.my_y)
        self.passed = (pass_x, both_y(1 - self.my_x).astype(BF))
        self.left = both_x(self.my_y)
        self.right = both_y(self.my_x)
        self.ended = (flip(self.passed[0], 2), flip(self.passed[1], 1))

    def last(self, *before):
        if self.count != 4:
            total = lax.psum_scatter(self.passed[0], "row", scatter_dimension=0, tiled=True).astype(F32)
            little = None
            if self.small is not None:
                size = total.shape[0]
                little = butterfly(self.small, "row")[0]
                little = lax.dynamic_slice_in_dim(little, lax.axis_index("row") * size, size, 0)
            return total, little
        end_x, end_y = tie(self.ended, *before)
        size = self.size
        left = self.left + end_x[:size].astype(F32)
        right = self.right + end_y.astype(F32)
        little = None
        if self.small is not None:
            little = self.little + joined(end_x[size:], size)
        return jnp.concatenate([left, right], axis=1), little


def butterfly(v, axis):
    count = lax.axis_size(axis)
    bit = 1
    while bit < count:
        v = v + lax.ppermute(v, axis, [(i, i ^ bit) for i in range(count)])
        bit *= 2
    return v


def sum_over_row_dp(v, *before):
    if lax.axis_size("row") != 4:
        return lax.psum(butterfly(v, "row"), "dp")
    me = lax.axis_index("row")
    for bit in (1, 2):
        size = v.shape[0] // 2
        side = me // bit % 2
        away = lax.dynamic_slice_in_dim(v, (1 - side) * size, size, 0)
        keep = lax.dynamic_slice_in_dim(v, side * size, size, 0)
        v = keep + flip(away, bit)
    v = butterfly(tie(v, *before), "dp")
    for bit in (2, 1):
        other = flip(v, bit)
        first = me // bit % 2 == 0
        v = jnp.concatenate([jnp.where(first, v, other), jnp.where(first, other, v)], axis=0)
    return v


def sum_over_row(v):
    if lax.axis_size("row") != 4:
        return butterfly(v, "row")
    return v + flip(v, 1) + flip(v, 2) + flip(v, 3)


def other_col(v):
    return lax.ppermute(v, "col", [(0, 1), (1, 0)])


def dealt_rows(rows):
    half = rows[0].shape[1] // 2
    own = jnp.stack([r[:, :half] for r in rows])
    got = other_col(jnp.stack([r[:, half:] for r in rows]))
    at_start = lax.axis_index("col") == 0
    return jnp.concatenate([jnp.where(at_start, own, got), jnp.where(at_start, got, own)], axis=0)


def sent_back(dealt):
    groups = lax.axis_size("dp")
    me = lax.axis_index("dp")
    parts = []
    for hop in range(groups):
        piece = lax.dynamic_index_in_dim(dealt, (me + hop) % groups, 0, keepdims=False)
        if hop:
            piece = lax.ppermute(piece, "dp", [(i, (i + hop) % groups) for i in range(groups)])
        parts.append(piece)
    return parts


def in_given_order(parts, dest_group):
    groups = lax.axis_size("dp")
    hops = ((lax.axis_index("dp") - dest_group) % groups)[:, None, None]
    out = jnp.where(hops == 0, parts[0][None], jnp.zeros((), BF))
    for hop in range(1, groups):
        out = jnp.where(hops == hop, parts[hop][None], out)
    return out


def matmul(a, b, over_a, over_b):
    return lax.dot_general(a, b, (((over_a,), (over_b,)), ((), ())), preferred_element_type=F32)


def per_device(
    hidden, targets, lengths, dest_group, norm_gain, gate_input_weight, auxiliary_weight,
    conv_x, conv_x_bias, conv_bc, conv_bc_bias, dt_bias, a_log, d_skip, out_gain, output_weight,
):
    row_count = lax.axis_size("row")
    col_count = lax.axis_size("col")
    row_index = lax.axis_index("row")
    col_index = lax.axis_index("col")
    group_index = lax.axis_index("dp")
    seq_group, local_len, width_col = hidden.shape
    heads = gate_input_weight.shape[1]
    pair = gate_input_weight.shape[2]
    head_dim = pair // 2
    inner = heads * head_dim
    wide = heads * pair
    aux = conv_bc.shape[1]
    head_total = auxiliary_weight.shape[1] - aux
    steps = -(-heads // 16) * 16
    seq_col = seq_group // col_count
    model_width = width_col * col_count
    inner_width = inner * row_count
    all_tokens = lengths.shape[0] * local_len * row_count
    valid_count = jnp.sum(lengths).astype(F32)
    group_lengths = lax.dynamic_slice_in_dim(lengths, group_index * seq_group, seq_group, 0)
    own_lengths = lax.dynamic_slice_in_dim(group_lengths, col_index * seq_col, seq_col, 0)

    def widened(v):
        mine = lax.dynamic_slice_in_dim(v, col_index * seq_col, seq_col, 0)
        theirs = lax.dynamic_slice_in_dim(v, (1 - col_index) * seq_col, seq_col, 0)
        return jnp.concatenate([mine, other_col(theirs)], axis=2)

    u_low = widened(hidden)
    gain = jnp.concatenate([norm_gain, other_col(norm_gain)])
    u = [u_low[k].astype(F32) for k in range(seq_col)]
    inv_rms = [lax.rsqrt(jnp.mean(v * v, axis=1, keepdims=True) + EPSILON) for v in u]
    spread = lambda v: lax.all_gather(v, "row", axis=0, tiled=True)
    normed = [(v * r * gain[None, :]).astype(BF) for v, r in zip(u, inv_rms, strict=True)]
    scaled = [spread(normed[0])]
    for v in normed[1:]:
        scaled.append(spread(tie(v, scaled[-1])))
    in_own = tie(
        jnp.concatenate(
            [
                gate_input_weight.reshape(width_col, wide),
                auxiliary_weight[:, :aux],
                lax.dynamic_slice_in_dim(auxiliary_weight, aux + row_index * heads, heads, 1),
                jnp.zeros((width_col, steps - heads), BF),
            ],
            axis=1,
        )
    )
    out_own = output_weight.reshape(inner, width_col)
    in_other, out_other = other_col(in_own), other_col(out_own)
    in_weight = tie(jnp.concatenate([in_own, in_other], axis=0))

    scaled[0] = tie(scaled[0], in_weight)

    column = lambda v: v.reshape(-1, 1)
    taps = jnp.concatenate(
        [
            conv_x.reshape(-1, inner).T,
            column(conv_x_bias),
            column(jnp.repeat(d_skip, head_dim)),
            column(out_gain),
            jnp.zeros((inner, 1), F32),
        ],
        axis=1,
    )
    bc_taps = jnp.concatenate([conv_bc.T, column(conv_bc_bias), jnp.zeros((aux, 3), F32)], axis=1)
    dt_par = jnp.pad(jnp.stack([dt_bias, a_log], axis=1), ((0, steps - heads), (0, 6)))

    targets_own = widened(targets)
    positions = row_index * local_len + jnp.arange(local_len, dtype=jnp.int32)

    zx, gated, entering, scatters = [], [], [], []
    result, g_result, g_rows, coef = [], [], [], []
    loss_part = jnp.zeros((), F32)

    def finish(k, *before):
        nonlocal loss_part
        summed, total_square = scatters[k].last(*before)
        gate_inv = lax.rsqrt(total_square / inner_width + EPSILON)[:, None]
        branch = summed * gate_inv
        full = u[k] + branch
        valid = (positions < own_lengths[k]).astype(F32)[:, None]
        difference = (full - targets_own[k].astype(F32)) * valid
        loss_part = loss_part + jnp.sum(difference * difference)
        grad = difference * (all_tokens / valid_count)
        result.append(full.astype(BF))
        g_result.append(grad)
        share = gate_inv[:, 0] * gate_inv[:, 0] * jnp.sum(grad * branch, axis=1) / inner_width
        placed = lax.dynamic_update_slice_in_dim(
            jnp.zeros((local_len * row_count,), F32), share, row_index * local_len, 0
        )
        coef.append(sum_over_row(placed[None, :]))
        sent = (grad * gate_inv).astype(BF)
        g_rows.append(spread(tie(sent, *g_rows[-1:])))
        return sent

    for k in range(seq_col):
        source = scaled[k] if k == 0 else tie(scaled[k], *scatters[-1].sent)
        projected = matmul(in_weight, source, 0, 1)
        if k > 0:
            scatters[-1].second(projected)
            projected = tie(projected, *scatters[-1].passed)
        zx.append(projected)
        g, square, e = scan_forward(projected, taps, bc_taps, dt_par, heads)
        gated.append(g)
        entering.append(e)
        if k > 0:
            g = tie(g, finish(k - 1, g))
        left, right = (matmul(g, w, 0, 0).astype(BF) for w in (out_own, out_other))
        scatters.append(Scatter(left, right, square))
        scatters[-1].first()
    out_weight = tie(jnp.concatenate(tie((out_own, out_other), *scatters[-1].sent), axis=1))
    scatters[-1].second(out_weight, *coef)
    finish(seq_col - 1)

    to_rows = lambda g: Scatter(*(matmul(g, w, 0, 1).astype(BF) for w in (in_own, in_other)))
    g_in, scatters = [], []
    sums = [0.0, 0.0, 0.0]
    w_out_part = 0.0
    for k in range(seq_col):
        final = k == seq_col - 1
        whole = g_rows[k] if k == 0 else tie(g_rows[k], g_in[-1], coef[k])
        w_out_part = w_out_part + matmul(gated[k], whole, 1, 0)
        before = (w_out_part,)
        if k == 0:
            dealt_output = dealt_rows(result)
            output_parts = sent_back(dealt_output)
        if final:
            received = other_col(w_out_part[:, width_col:].astype(BF))
            w_out_low = (w_out_part[:, :width_col] + received.astype(F32)).astype(BF)
            w_out_sum = lax.psum(w_out_low, "dp")
            before = (w_out_low,)
        gn = matmul(out_weight, whole, 1, 1)
        if k > 0:
            scatters.append(to_rows(tie(g_in[-1], *before)))
            scatters[-1].first()
            before = scatters[-1].sent
        gn = tie(gn, *before)
        g, gx, gbc, gdt = scan_backward(
            zx[k], entering[k], gn, coef[k], taps, bc_taps, dt_par, heads
        )
        sums = [a + b for a, b in zip(sums, (gx, gbc, gdt), strict=True)]
        if k == 0:
            g = tie(g, *output_parts)
        if k > 0:
            scatters[-1].second(g)
            g = tie(g, *scatters[-1].passed)
        g_in.append(g)

    def rows_of(start, g):
        return sum(matmul(scaled[i][:, start : start + width_col], g[i], 0, 1) for i in range(seq_col))

    g_in[-1] = tie(g_in[-1], w_out_sum)
    g_wide = [g[:wide] for g in g_in]
    there = rows_of(width_col, g_wide).astype(BF)
    scatters.append(to_rows(tie(g_in[-1], there)))
    scatters[-1].first()
    g_wide[-1] = tie(g_wide[-1], *scatters[-1].sent)
    in_low = (rows_of(0, g_wide) + other_col(there).astype(F32)).astype(BF)
    in_low = tie(in_low.reshape(width_col, heads, pair))
    scatters[-1].second(in_low)
    w_zx = lax.psum(in_low, "dp")
    g_aux = [g[wide:] for g in g_in]
    g_aux[-1] = tie(g_aux[-1], in_low)
    aux_part = sum(matmul(scaled[i], g_aux[i], 0, 1) for i in range(seq_col))
    aux_half = aux_part[:width_col] + other_col(aux_part[width_col:])
    aux_half = jnp.concatenate(
        [
            aux_half[:, :aux],
            lax.dynamic_update_slice_in_dim(
                jnp.zeros((width_col, head_total), F32),
                aux_half[:, aux : aux + heads],
                row_index * heads,
                1,
            ),
        ],
        axis=1,
    )
    gain_part = jnp.zeros((model_width,), F32)
    g_u = []
    for k in range(seq_col):
        g_scaled, _ = scatters[k].last()
        gain_part = gain_part + jnp.sum(g_scaled * u[k] * inv_rms[k], axis=0)
        weighted = g_scaled * gain[None, :]
        dot = jnp.sum(weighted * u[k], axis=1, keepdims=True) / model_width
        cube = inv_rms[k] * inv_rms[k] * inv_rms[k]
        g_u.append((g_result[k] + inv_rms[k] * weighted - u[k] * (cube * dot)).astype(BF))
    hidden_parts = sent_back(tie(dealt_rows(g_u), w_zx))
    w_aux = sum_over_row_dp(aux_half)

    gx, gbc, gdt = sums
    flat = jnp.concatenate(
        [gx.reshape(-1), gdt[:, 1:3].reshape(-1), gbc.reshape(-1), loss_part[None]]
    )
    vector = jnp.concatenate([flat, gain_part[:width_col]]) + other_col(
        jnp.concatenate([flat, gain_part[width_col:]])
    )
    own_size = inner * 8 + steps * 2
    vector = jnp.concatenate([vector[:own_size], butterfly(vector[own_size:], "row")])
    vector = butterfly(vector, "dp")
    gx = vector[: inner * 8].reshape(inner, 8)
    gdt = vector[inner * 8 : own_size].reshape(steps, 2)
    shared = vector[own_size:]
    gbc = shared[: aux * 8].reshape(aux, 8)
    loss = shared[aux * 8] * 0.5 / valid_count
    gain_sum = shared[aux * 8 + 1 :]
    return (
        loss,
        in_given_order(output_parts, dest_group),
        in_given_order(hidden_parts, dest_group),
        gain_sum,
        w_zx.astype(F32),
        w_aux.astype(F32),
        gx[:, :4].T.reshape(4, heads, head_dim),
        gx[:, 4].reshape(heads, head_dim),
        gbc[:, :4].T,
        gbc[:, 4],
        gdt[:heads, 0],
        gdt[:heads, 1],
        gx[:, 5].reshape(heads, head_dim).sum(axis=1),
        gx[:, 6].reshape(heads, head_dim),
        w_out_sum.astype(F32).reshape(heads, head_dim, width_col),
    )


def solution(mesh):
    placed = (
        P("dp", "row", "col"),
        P("dp", "row", "col"),
        P(),
        P("dp"),
        P("col"),
        P("col", "row", None),
        P("col", None),
        P(None, "row", None),
        P("row", None),
        P(),
        P(),
        P("row"),
        P("row"),
        P("row"),
        P("row", None),
        P("row", None, "col"),
    )
    return jax.shard_map(
        per_device,
        mesh=mesh,
        in_specs=placed,
        out_specs=(
            P(),
            P("dp", "row", "col"),
            P("dp", "row", "col"),
            P("col"),
            P("col", "row", None),
            P("col", None),
            P(None, "row", None),
            P("row", None),
            P(),
            P(),
            P("row"),
            P("row"),
            P("row"),
            P("row", None),
            P("row", None, "col"),
        ),
        check_vma=False,
    )
```

```python
import functools
import jax
import jax.numpy as jnp
from jax import lax
from jax.experimental import pallas as pl
from jax.experimental.pallas import tpu as pltpu
from jax.sharding import PartitionSpec as P

BF = jnp.bfloat16
F32 = jnp.float32
SPAN = 512
PART = 128
TILE = 256
LOG2E = 1.4426950408889634
EDGE = 128
EPSILON = 1e-05


def nn(a, b):
    return lax.dot_general(a, b, (((1,), (0,)), ((), ())), preferred_element_type=F32)


def nt(a, b):
    return lax.dot_general(a, b, (((1,), (1,)), ((), ())), preferred_element_type=F32)


def tn(a, b):
    return lax.dot_general(a, b, (((0,), (0,)), ((), ())), preferred_element_type=F32)


def exact(a, b):
    return lax.dot_general(
        a, b, (((1,), (0,)), ((), ())), precision=lax.Precision.HIGHEST, preferred_element_type=F32
    )


def sigmoid(v):
    return 0.5 * jnp.tanh(0.5 * v) + 0.5


def softplus(v):
    return jnp.maximum(v, 0.0) + jnp.log1p(jnp.exp(-jnp.abs(v)))


def wide(v, span):
    return jnp.concatenate([v] * (span // v.shape[1]), axis=1)


def taps_at(taps_ref, at, span):
    return lambda k: wide(taps_ref[k, at, :], span)


def spread_taps(from_ref, to_ref):
    for k in range(to_ref.shape[0]):
        to_ref[k] = jnp.broadcast_to(from_ref[:, k : k + 1], to_ref.shape[1:])


def move_matrix(ahead):
    rows = lax.broadcasted_iota(jnp.int32, (2 * EDGE, EDGE), 0)
    cols = lax.broadcasted_iota(jnp.int32, (2 * EDGE, EDGE), 1)
    moves = [rows == (cols + k if ahead else cols + EDGE - k) for k in (1, 2, 3)]
    return jnp.concatenate([m.astype(F32).astype(BF) for m in moves], axis=1)


def moved(joined, matrix):
    size = joined.shape[0]
    parts = range(joined.shape[1] // EDGE - 1)
    low = joined.astype(BF)
    stacked = jnp.concatenate([low[:, q * EDGE : (q + 2) * EDGE] for q in parts], axis=0)
    out = nn(stacked, matrix)
    return [
        jnp.concatenate(
            [out[q * size : (q + 1) * size, k * EDGE : (k + 1) * EDGE] for q in parts], axis=1
        )
        for k in range(3)
    ]


def conv_of(before, now, tap, matrix):
    one, two, three = moved(jnp.concatenate([before, now], axis=1), matrix)
    return tap(4) + tap(3) * now + tap(2) * one + tap(1) * two + tap(0) * three


def conv_back(now, after, tap, matrix):
    one, two, three = moved(jnp.concatenate([now, after], axis=1), matrix)
    return tap(3) * now + tap(2) * one + tap(1) * two + tap(0) * three, (one, two, three)


def fold(v):
    total = v[:, :EDGE]
    for k in range(1, v.shape[1] // EDGE):
        total = total + v[:, k * EDGE : (k + 1) * EDGE]
    return total


def lanes(q):
    return slice(q * PART, (q + 1) * PART)


def span_common(bc_before, bc_now, dt_raw, bc_tap, dt_par, matrix):
    pre = conv_of(bc_before, bc_now, bc_tap, matrix)
    sig = sigmoid(pre)
    act = pre * sig
    half = act.shape[0] // 2
    b_t = act[:half].astype(BF)
    c_t = act[half:].astype(BF)
    parts = range(bc_now.shape[1] // PART)
    rows = lax.broadcasted_iota(jnp.int32, (PART, PART), 0)
    cols = lax.broadcasted_iota(jnp.int32, (PART, PART), 1)
    causal = rows <= cols
    steps = softplus(dt_raw + dt_par[:, 0:1])
    rate = -jnp.exp(dt_par[:, 1:2])
    gone = steps * (rate * LOG2E)
    decay = [exact(gone[:, lanes(q)], causal.astype(F32)) for q in parts]
    last = [d[:, PART - 1 :] for d in decay]
    decay_n = [d.T for d in decay]
    left = jnp.concatenate([jnp.exp2(e - d) for e, d in zip(last, decay)], axis=1)
    kept = [jnp.exp2(e) for e in last]
    decay = jnp.concatenate(decay, axis=1)
    grown = jnp.exp2(decay)
    b_n = [b_t[:, lanes(q)].astype(F32).T.astype(BF) for q in parts]
    scores = [jnp.where(causal, nn(b_n[q], c_t[:, lanes(q)]), 0.0) for q in parts]
    return pre, sig, b_t, c_t, b_n, scores, causal, steps, rate, decay, decay_n, grown, left, kept


def forward_kernel(
    heads, zx_ref, bc_ref, dt_ref, taps_ref, bc_taps_ref, dt_par_ref,
    gated_ref, square_ref, enter_ref, x_ref, slope_ref, y_ref,
    state, x_tail, bc_tail, carry, xd_all, tailed, scores_all, x_taps, bc_taps, matrix_ref,
):
    span = zx_ref.shape[1]
    inner = state.shape[0]
    size = inner // heads
    parts = range(span // PART)

    @pl.when(pl.program_id(0) == 0)
    def _():
        state[...] = jnp.zeros_like(state)
        x_tail[...] = jnp.zeros_like(x_tail)
        bc_tail[...] = jnp.zeros_like(bc_tail)
        spread_taps(taps_ref, x_taps)
        spread_taps(bc_taps_ref, bc_taps)
        matrix_ref[...] = move_matrix(False)

    matrix = matrix_ref[...]
    bc_now = bc_ref[...]
    _, _, _, c_t, b_n, scores, _, steps, _, decay, decay_n, grown, left, kept = span_common(
        bc_tail[...], bc_now, dt_ref[...], taps_at(bc_taps, slice(None), span), dt_par_ref[...], matrix
    )
    bc_tail[...] = bc_now[:, span - EDGE :]
    for q in parts:
        scores_all[q] = scores[q]
    for h in range(heads):
        at = slice(h * size, (h + 1) * size)
        x_raw = zx_ref[(2 * h + 1) * size : (2 * h + 2) * size, :]
        pre = conv_of(x_tail[at, :], x_raw, taps_at(x_taps, at, span), matrix)
        x_tail[at, :] = x_raw[:, span - EDGE :]
        sig = sigmoid(pre)
        x = pre * sig
        xd = x * steps[h : h + 1, :]
        x_ref[at, :] = x
        slope_ref[at, :] = sig + x * (1.0 - sig)
        xd_all[at, :] = xd.astype(BF)
        tailed[at, :] = (xd * left[h : h + 1, :]).astype(BF)
    for q in parts:
        entering = state[...].astype(BF)
        enter_ref[q * inner : (q + 1) * inner, :] = entering
        carry[:, lanes(q)] = nn(entering, c_t[:, lanes(q)])
        more = nn(tailed[:, lanes(q)], b_n[q])
        for h in range(heads):
            at = slice(h * size, (h + 1) * size)
            state[at, :] = state[at, :] * kept[q][h : h + 1, :] + more[at, :]
    square = jnp.zeros((size, span), F32)
    for h in range(heads):
        at = slice(h * size, (h + 1) * size)
        z = zx_ref[2 * h * size : (2 * h + 1) * size, :]
        tap = taps_at(x_taps, at, span)
        mixed = []
        for q in parts:
            gap = decay[h : h + 1, lanes(q)] - decay_n[q][:, h : h + 1]
            mixing = scores_all[q] * jnp.exp2(jnp.minimum(gap, 0.0))
            mixed.append(nn(xd_all[at, lanes(q)], mixing.astype(BF)))
        y = jnp.concatenate(mixed, axis=1) + carry[at, :] * grown[h : h + 1, :]
        y_ref[at, :] = y
        y = y + tap(5) * x_ref[at, :]
        gated = y * (z * sigmoid(z))
        square = square + gated * gated
        gated_ref[at, :] = (gated * tap(6)).astype(BF)
    square_ref[...] = jnp.sum(square, axis=0, keepdims=True)


def backward_kernel(
    heads, zx_ref, x_ref, slope_ref, y_ref, bc_ref, bc_before_ref, dt_ref, enter_ref, gn_ref, coef_ref,
    taps_ref, bc_taps_ref, dt_par_ref,
    gzx_ref, gx_sum_ref, gbc_sum_ref, gdt_sum_ref,
    dstate, x_head, bc_head, from_state, grown_g, tailed, x_acc, bc_acc, dt_acc, rsum, dsum,
    dxd_all, gy_all, scores_all, dscores_all, held_all, x_taps, bc_taps_all, matrix_ref,
    back_matrix_ref,
):
    span = zx_ref.shape[1]
    inner = dstate.shape[0]
    size = inner // heads
    half = bc_ref.shape[0] // 2
    wide = zx_ref.shape[0]
    parts = range(span // PART)
    step = pl.program_id(0)
    count = pl.num_programs(0)
    first = step == count - 1

    @pl.when(step == 0)
    def _():
        dstate[...] = jnp.zeros_like(dstate)
        x_head[...] = jnp.zeros_like(x_head)
        bc_head[...] = jnp.zeros_like(bc_head)
        x_acc[...] = jnp.zeros_like(x_acc)
        bc_acc[...] = jnp.zeros_like(bc_acc)
        dt_acc[...] = jnp.zeros_like(dt_acc)
        rsum[...] = jnp.zeros_like(rsum)
        dsum[...] = jnp.zeros_like(dsum)
        held_all[...] = jnp.zeros_like(held_all)
        spread_taps(taps_ref, x_taps)
        spread_taps(bc_taps_ref, bc_taps_all)
        matrix_ref[...] = move_matrix(False)
        back_matrix_ref[...] = move_matrix(True)

    matrix, back_matrix = matrix_ref[...], back_matrix_ref[...]
    live = jnp.where(first, 0.0, 1.0)
    bc_tap = taps_at(bc_taps_all, slice(None), span)
    dt_raw = dt_ref[...]
    bc_now = bc_ref[...]
    (
        bc_pre, bc_sig, b_t, c_t, b_n, scores, causal, steps, rate, decay, decay_n, grown, left, kept
    ) = span_common(bc_before_ref[...] * live, bc_now, dt_raw, bc_tap, dt_par_ref[...], matrix)
    for q in parts:
        scores_all[q] = scores[q]
        dscores_all[q] = jnp.zeros((PART, PART), F32)
    coef = coef_ref[...]
    for h in range(heads):
        at = slice(h * size, (h + 1) * size)
        z = zx_ref[2 * h * size : (2 * h + 1) * size, :]
        tap = taps_at(x_taps, at, span)
        x = x_ref[at, :]
        xd = x * steps[h : h + 1, :]
        xd_low = xd.astype(BF)
        tailed[at, :] = (xd * left[h : h + 1, :]).astype(BF)
        ratios, mixings = [], []
        for q in parts:
            gap = decay[h : h + 1, lanes(q)] - decay_n[q][:, h : h + 1]
            ratios.append(jnp.exp2(jnp.minimum(gap, 0.0)))
            mixings.append((scores_all[q] * ratios[q]).astype(BF))
        grown_h = grown[h : h + 1, :]
        y_scan = y_ref[at, :]
        y = y_scan + tap(5) * x
        zsig = sigmoid(z)
        silu_z = z * zsig
        gated = y * silu_z
        gn = gn_ref[at, :].astype(F32)
        g_gated = tap(6) * gn - gated * coef
        gy = g_gated * silu_z
        gzx_ref[2 * h * size : (2 * h + 1) * size, :] = (
            g_gated * y * (zsig + silu_z * (1.0 - zsig))
        ).astype(BF)
        gy_low = gy.astype(BF)
        gy_all[at, :] = gy_low
        grown_g[at, :] = (gy * grown_h).astype(BF)
        rsum[h : h + 1, :] = jnp.sum(gy_low.astype(F32) * y_scan, axis=0, keepdims=True)
        x_acc[5, at, :] = x_acc[5, at, :] + fold(gy * x)
        x_acc[6, at, :] = x_acc[6, at, :] + fold(gn * gated)
        for q in parts:
            dxd_all[at, lanes(q)] = nt(gy_low[:, lanes(q)], mixings[q])
            dscores_all[q] = dscores_all[q] + tn(xd_low[:, lanes(q)], gy_low[:, lanes(q)]) * ratios[q]
    db, dc, flows = [], [], []
    for q in reversed(parts):
        entering = enter_ref[q * inner : (q + 1) * inner, :]
        leaving = dstate[...].astype(BF)
        from_state[:, lanes(q)] = nn(leaving, b_t[:, lanes(q)])
        low = jnp.where(causal, dscores_all[q], 0.0).astype(BF)
        dc.insert(0, nn(b_t[:, lanes(q)], low) + tn(entering, grown_g[:, lanes(q)]))
        db.insert(0, nt(c_t[:, lanes(q)], low) + tn(leaving, tailed[:, lanes(q)]))
        more = nt(grown_g[:, lanes(q)], c_t[:, lanes(q)])
        for h in range(heads):
            at = slice(h * size, (h + 1) * size)
            passed = dstate[at, :] * kept[q][h : h + 1, :]
            held_all[q, h : h + 1, :] = jnp.sum(passed * entering[at, :].astype(F32), axis=0, keepdims=True)
            dstate[at, :] = passed + more[at, :]
    for h in range(heads):
        at = slice(h * size, (h + 1) * size)
        x_raw = zx_ref[(2 * h + 1) * size : (2 * h + 2) * size, :]
        tap = taps_at(x_taps, at, span)
        x = x_ref[at, :]
        steps_h = steps[h : h + 1, :]
        dx_state = from_state[at, :] * left[h : h + 1, :]
        dxd = dxd_all[at, :] + dx_state
        xd_wide = (x * steps_h).astype(BF).astype(F32)
        rsum[h : h + 1, :] = rsum[h : h + 1, :] - jnp.sum(xd_wide * dxd, axis=0, keepdims=True)
        dsum[h : h + 1, :] = jnp.sum(x * dxd, axis=0, keepdims=True)
        held = jnp.sum(xd_wide * dx_state, axis=0, keepdims=True)
        for q in parts:
            held_all[q, h : h + 1, :] = held_all[q, h : h + 1, :] + held[:, lanes(q)]
        dx = dxd * steps_h + tap(5) * gy_all[at, :].astype(F32)
        gpre = dx * slope_ref[at, :]
        g_raw, later = conv_back(gpre, x_head[at, :], tap, back_matrix)
        x_head[at, :] = gpre[:, :EDGE]
        gzx_ref[(2 * h + 1) * size : (2 * h + 2) * size, :] = g_raw.astype(BF)
        for k, moved_g in enumerate((gpre, *later)):
            x_acc[3 - k, at, :] = x_acc[3 - k, at, :] + fold(moved_g * x_raw)
        x_acc[4, at, :] = x_acc[4, at, :] + fold(gpre)
    gbc = jnp.concatenate([jnp.concatenate(db, axis=1), jnp.concatenate(dc, axis=1)], axis=0)
    gbc = gbc * (bc_sig + bc_pre * bc_sig * (1.0 - bc_sig))
    g_raw, later = conv_back(gbc, bc_head[...], bc_tap, back_matrix)
    bc_head[...] = gbc[:, :EDGE]
    gzx_ref[wide : wide + 2 * half, :] = g_raw.astype(BF)
    for k, moved_g in enumerate((gbc, *later)):
        bc_acc[3 - k] = bc_acc[3 - k] + fold(moved_g * bc_now)
    bc_acc[4] = bc_acc[4] + fold(gbc)
    after = jnp.logical_or(
        jnp.logical_not(causal),
        lax.broadcasted_iota(jnp.int32, (PART, PART), 0) == lax.broadcasted_iota(jnp.int32, (PART, PART), 1),
    ).astype(F32)
    da = jnp.concatenate(
        [
            exact(rsum[:, lanes(q)], after) + jnp.sum(held_all[q], axis=1, keepdims=True)
            for q in parts
        ],
        axis=1,
    )
    g_steps = dsum[...] + rate * da
    g_dt = g_steps * sigmoid(dt_raw + dt_par_ref[:, 0:1])
    gzx_ref[wide + 2 * half :, :] = g_dt.astype(BF)
    dt_acc[:, 1:2] = dt_acc[:, 1:2] + jnp.sum(g_dt, axis=1, keepdims=True)
    dt_acc[:, 2:3] = dt_acc[:, 2:3] + jnp.sum(da * steps * rate, axis=1, keepdims=True)

    @pl.when(first)
    def _():
        for k in range(7):
            gx_sum_ref[:, k : k + 1] = jnp.sum(x_acc[k], axis=1, keepdims=True)
        for k in range(5):
            gbc_sum_ref[:, k : k + 1] = jnp.sum(bc_acc[k], axis=1, keepdims=True)
        gdt_sum_ref[...] = dt_acc[...]


def scan_forward(zx, taps, bc_taps, dt_par, heads, span=SPAN):
    inner = taps.shape[0]
    length = zx.shape[1]
    aux = bc_taps.shape[0]
    steps = dt_par.shape[0]
    states = aux // 2
    body = functools.partial(forward_kernel, heads)
    whole = lambda r, c: pl.BlockSpec((r, c), lambda i: (0, 0))
    return pl.pallas_call(
        body,
        grid=(length // span,),
        in_specs=[
            pl.BlockSpec((2 * inner, span), lambda i: (0, i)),
            pl.BlockSpec((aux, span), lambda i: (2 * inner // aux, i)),
            pl.BlockSpec((steps, span), lambda i: ((2 * inner + aux) // steps, i)),
            whole(inner, 8), whole(aux, 8), whole(steps, 8),
        ],
        out_specs=[
            pl.BlockSpec((inner, span), lambda i: (0, i)),
            pl.BlockSpec((1, span), lambda i: (0, i)),
            pl.BlockSpec((span // PART * inner, states), lambda i: (i, 0)),
        ]
        + [pl.BlockSpec((inner, span), lambda i: (0, i))] * 3,
        out_shape=[
            jax.ShapeDtypeStruct((inner, length), BF),
            jax.ShapeDtypeStruct((1, length), F32),
            jax.ShapeDtypeStruct((length // PART * inner, states), BF),
        ]
        + [jax.ShapeDtypeStruct((inner, length), F32)] * 3,
        scratch_shapes=[
            pltpu.VMEM((inner, states), F32),
            pltpu.VMEM((inner, EDGE), F32),
            pltpu.VMEM((aux, EDGE), F32),
            pltpu.VMEM((inner, span), F32),
            pltpu.VMEM((inner, span), BF),
            pltpu.VMEM((inner, span), BF),
            pltpu.VMEM((span // PART, PART, PART), F32),
            pltpu.VMEM((7, inner, EDGE), F32),
            pltpu.VMEM((5, aux, EDGE), F32),
            pltpu.VMEM((2 * EDGE, 3 * EDGE), BF),
        ],
        compiler_params=pltpu.CompilerParams(vmem_limit_bytes=56 * 2**20),
        name="scan_forward",
    )(zx, zx, zx, taps, bc_taps, dt_par)


def scan_backward(zx, kept, entering, gn, coef, taps, bc_taps, dt_par, heads, span=SPAN):
    inner = taps.shape[0]
    length = zx.shape[1]
    aux = bc_taps.shape[0]
    steps = dt_par.shape[0]
    states = aux // 2
    count = length // span
    ratio = span // EDGE
    body = functools.partial(backward_kernel, heads)
    whole = lambda r, c: pl.BlockSpec((r, c), lambda i: (0, 0))
    rev = lambda i: count - 1 - i
    before = lambda i: jnp.maximum((count - 1 - i) * ratio - 1, 0)
    return pl.pallas_call(
        body,
        grid=(count,),
        in_specs=[
            pl.BlockSpec((2 * inner, span), lambda i: (0, rev(i))),
            pl.BlockSpec((inner, span), lambda i: (0, rev(i))),
            pl.BlockSpec((inner, span), lambda i: (0, rev(i))),
            pl.BlockSpec((inner, span), lambda i: (0, rev(i))),
            pl.BlockSpec((aux, span), lambda i: (2 * inner // aux, rev(i))),
            pl.BlockSpec((aux, EDGE), lambda i: (2 * inner // aux, before(i))),
            pl.BlockSpec((steps, span), lambda i: ((2 * inner + aux) // steps, rev(i))),
            pl.BlockSpec((span // PART * inner, states), lambda i: (rev(i), 0)),
            pl.BlockSpec((inner, span), lambda i: (0, rev(i))),
            pl.BlockSpec((1, span), lambda i: (0, rev(i))),
            whole(inner, 8), whole(aux, 8), whole(steps, 8),
        ],
        out_specs=[
            pl.BlockSpec((2 * inner + aux + steps, span), lambda i: (0, rev(i))),
            whole(inner, 8), whole(aux, 8), whole(steps, EDGE),
        ],
        out_shape=[
            jax.ShapeDtypeStruct((2 * inner + aux + steps, length), BF),
            jax.ShapeDtypeStruct((inner, 8), F32),
            jax.ShapeDtypeStruct((aux, 8), F32),
            jax.ShapeDtypeStruct((steps, EDGE), F32),
        ],
        scratch_shapes=[
            pltpu.VMEM((inner, states), F32),
            pltpu.VMEM((inner, EDGE), F32),
            pltpu.VMEM((aux, EDGE), F32),
            pltpu.VMEM((inner, span), F32),
            pltpu.VMEM((inner, span), BF),
            pltpu.VMEM((inner, span), BF),
            pltpu.VMEM((7, inner, EDGE), F32),
            pltpu.VMEM((5, aux, EDGE), F32),
            pltpu.VMEM((steps, EDGE), F32),
            pltpu.VMEM((steps, span), F32),
            pltpu.VMEM((steps, span), F32),
            pltpu.VMEM((inner, span), F32),
            pltpu.VMEM((inner, span), BF),
            pltpu.VMEM((span // PART, PART, PART), F32),
            pltpu.VMEM((span // PART, PART, PART), F32),
            pltpu.VMEM((span // PART, steps, PART), F32),
            pltpu.VMEM((7, inner, EDGE), F32),
            pltpu.VMEM((5, aux, EDGE), F32),
            pltpu.VMEM((2 * EDGE, 3 * EDGE), BF),
            pltpu.VMEM((2 * EDGE, 3 * EDGE), BF),
        ],
        compiler_params=pltpu.CompilerParams(vmem_limit_bytes=56 * 2**20),
        name="scan_backward",
    )(zx, *kept, zx, zx, zx, entering, gn, coef, taps, bc_taps, dt_par)


def product_kernel(form, count, added, *refs):
    out_ref = refs[-1]
    total = refs[2 * count][...].astype(F32) if added else None
    for i in range(count):
        a, b = refs[2 * i][...], refs[2 * i + 1][...]
        if form == "tt":
            a = a.T
        over = 0 if form == "nn" else 1
        term = lax.dot_general(a, b, (((1,), (over,)), ((), ())), preferred_element_type=F32)
        total = term if total is None else total + term
    out_ref[...] = total.astype(out_ref.dtype)


def product(form, pairs, tile, added=None, dtype=BF, start=0, columns=None, wide=None):
    first, other = pairs[0]
    rows = columns or first.shape[1 if form == "tt" else 0]
    cols = wide or other.shape[1 if form == "nn" else 0]
    operands, specs = [], []
    for a, b in pairs:
        operands += [a, b]
        if form == "tt":
            specs.append(pl.BlockSpec((a.shape[0], tile), lambda i: (0, start // tile + i)))
        else:
            specs.append(pl.BlockSpec((tile, a.shape[1]), lambda i: (i, 0)))
        block = b.shape if form == "nn" else (cols, b.shape[1])
        specs.append(pl.BlockSpec(block, lambda i: (0, 0), pipeline_mode=pl.Buffered(1)))
    if added is not None:
        operands.append(added)
        specs.append(pl.BlockSpec((tile, cols), lambda i: (i, 0)))
    return pl.pallas_call(
        functools.partial(product_kernel, form, len(pairs), added is not None),
        grid=(rows // tile,),
        in_specs=specs,
        out_specs=pl.BlockSpec((tile, cols), lambda i: (i, 0)),
        out_shape=jax.ShapeDtypeStruct((rows, cols), dtype),
        compiler_params=pltpu.CompilerParams(vmem_limit_bytes=56 * 2**20),
        name="product_" + form,
    )(*operands)


def late_kernel(count, wide, first, *refs):
    scaled, g_all, g_tile = refs[:count], refs[count : 2 * count], refs[2 * count]
    weights, outs = refs[2 * count + 1 : 2 * count + 3], refs[2 * count + 3 : 2 * count + 6]
    held, sems = refs[2 * count + 6 : 2 * count + 8], refs[2 * count + 8]
    step = pl.program_id(0)
    copies = [pltpu.make_async_copy(weights[k], held[k], sems.at[k]) for k in range(2)]

    @pl.when(step == 0)
    def _():
        for copy in copies:
            copy.start()

    @pl.when(step < first)
    def _():
        total = None
        for s, g in zip(scaled, g_all):
            term = nt(s[...].T, g[:wide, :])
            total = term if total is None else total + term
        outs[0][...] = total.astype(BF)

    @pl.when(step == first)
    def _():
        for copy in copies:
            copy.wait()

    @pl.when(step >= first)
    def _():
        rows = g_tile[...].T
        for k in range(2):
            outs[1 + k][...] = nn(rows, held[k][...]).astype(BF)


def late_products(scaled, g_in, own, other, wide):
    depth, width = own.shape
    length = scaled[0].shape[0]
    first = width // TILE
    count = len(scaled)
    at = lambda i: jnp.maximum(i - first, 0)
    until = lambda i: jnp.minimum(i, first - 1)
    return pl.pallas_call(
        functools.partial(late_kernel, count, wide, first),
        grid=(first + length // TILE,),
        in_specs=[pl.BlockSpec((length, TILE), lambda i: (0, first + until(i))) for _ in scaled]
        + [pl.BlockSpec(g.shape, lambda i: (0, 0), pipeline_mode=pl.Buffered(1)) for g in g_in]
        + [pl.BlockSpec((depth, TILE), lambda i: (0, at(i)))]
        + [pl.BlockSpec(memory_space=pl.ANY)] * 2,
        out_specs=[
            pl.BlockSpec((TILE, wide), lambda i: (until(i), 0)),
            pl.BlockSpec((TILE, width), lambda i: (at(i), 0)),
            pl.BlockSpec((TILE, width), lambda i: (at(i), 0)),
        ],
        out_shape=[
            jax.ShapeDtypeStruct((width, wide), BF),
            jax.ShapeDtypeStruct((length, width), BF),
            jax.ShapeDtypeStruct((length, width), BF),
        ],
        scratch_shapes=[
            pltpu.VMEM(own.shape, BF),
            pltpu.VMEM(own.shape, BF),
            pltpu.SemaphoreType.DMA((2,)),
        ],
        compiler_params=pltpu.CompilerParams(vmem_limit_bytes=56 * 2**20),
        name="late_products",
    )(*scaled, *g_in, g_in[-1], own, other)


def tie(value, *before):
    return lax.optimization_barrier((value, *before))[0]


def split(v, width):
    rows = []
    rest = v
    for _ in range(3):
        part = lax.reduce_precision(rest, 8, 7)
        rows.append(part.astype(BF))
        rest = rest - part
    return jnp.pad(jnp.stack(rows), ((0, 13), (0, width - v.shape[0])))


def joined(rows, size):
    return jnp.sum(rows[:3, :size].astype(F32), axis=0)


def flip(v, bit):
    return lax.ppermute(v, "row", [(i, i ^ bit) for i in range(4)])


class Scatter:
    def __init__(self, left, right, small=None):
        self.count = lax.axis_size("row")
        self.small = small
        if self.count != 4:
            self.sent = (jnp.concatenate([left, right], axis=1),)
            return
        me = lax.axis_index("row")
        self.size, half = left.shape[0] // 4, left.shape[1]
        self.half = half
        self.my_y, self.my_x = me // 2, me % 2
        left = left.reshape(2, 2, self.size, half)
        right = right.reshape(2, 2, self.size, half)
        self.at_x = lambda i: lax.dynamic_index_in_dim(left, i, 1, keepdims=False)
        self.at_y = lambda i: lax.dynamic_index_in_dim(right, i, 0, keepdims=False)
        send_x = self.at_x(1 - self.my_x)
        if small is not None:
            pieces = small.reshape(2, 2, self.size)
            there = lax.dynamic_index_in_dim(pieces, 1 - self.my_x, 1, keepdims=False)
            self.here = lax.dynamic_index_in_dim(pieces, self.my_x, 1, keepdims=False)
            send_x = jnp.concatenate(
                [send_x, jnp.stack([split(there[0], half), split(there[1], half)])], axis=1
            )
        self.sent = (send_x, self.at_y(1 - self.my_y))

    def first(self):
        self.got = self.sent
        if self.count == 4:
            self.got = (flip(self.sent[0], 1), flip(self.sent[1], 2))

    def second(self, *before):
        if self.count != 4:
            self.passed = self.ended = self.sent
            return
        got_x, got_y = tie(self.got, *before)
        pick = lambda v, i: lax.dynamic_index_in_dim(v, i, 0, keepdims=False).astype(F32)
        size = self.size
        both_x = lambda i: pick(self.at_x(self.my_x), i) + pick(got_x[:, :size], i)
        both_y = lambda i: pick(self.at_y(self.my_y), i) + pick(got_y, i)
        pass_x = both_x(1 - self.my_y).astype(BF)
        if self.small is not None:
            little = lambda i: pick(self.here, i) + joined(
                lax.dynamic_index_in_dim(got_x[:, size:], i, 0, keepdims=False), size
            )
            pass_x = jnp.concatenate([pass_x, split(little(1 - self.my_y), self.half)], axis=0)
            self.little = little(self.my_y)
        self.passed = (pass_x, both_y(1 - self.my_x).astype(BF))
        self.left = both_x(self.my_y)
        self.right = both_y(self.my_x)
        self.ended = (flip(self.passed[0], 2), flip(self.passed[1], 1))

    def last(self, *before):
        if self.count != 4:
            total = lax.psum_scatter(self.passed[0], "row", scatter_dimension=0, tiled=True).astype(F32)
            little = None
            if self.small is not None:
                size = total.shape[0]
                little = butterfly(self.small, "row")[0]
                little = lax.dynamic_slice_in_dim(little, lax.axis_index("row") * size, size, 0)
            return total, little
        end_x, end_y = tie(self.ended, *before)
        size = self.size
        left = self.left + end_x[:size].astype(F32)
        right = self.right + end_y.astype(F32)
        little = None
        if self.small is not None:
            little = self.little + joined(end_x[size:], size)
        return jnp.concatenate([left, right], axis=1), little


def butterfly(v, axis):
    count = lax.axis_size(axis)
    bit = 1
    while bit < count:
        v = v + lax.ppermute(v, axis, [(i, i ^ bit) for i in range(count)])
        bit *= 2
    return v


def sum_over_row_dp(v, *before):
    if lax.axis_size("row") != 4:
        return lax.psum(butterfly(v, "row"), "dp")
    me = lax.axis_index("row")
    for bit in (1, 2):
        size = v.shape[0] // 2
        side = me // bit % 2
        away = lax.dynamic_slice_in_dim(v, (1 - side) * size, size, 0)
        keep = lax.dynamic_slice_in_dim(v, side * size, size, 0)
        v = keep + flip(away, bit)
    v = butterfly(tie(v, *before), "dp")
    for bit in (2, 1):
        other = flip(v, bit)
        first = me // bit % 2 == 0
        v = jnp.concatenate([jnp.where(first, v, other), jnp.where(first, other, v)], axis=0)
    return v


def sum_over_row(v):
    if lax.axis_size("row") != 4:
        return butterfly(v, "row")
    return v + flip(v, 1) + flip(v, 2) + flip(v, 3)


def other_col(v):
    return lax.ppermute(v, "col", [(0, 1), (1, 0)])


def dealt_rows(rows):
    half = rows[0].shape[1] // 2
    own = jnp.stack([r[:, :half] for r in rows])
    got = other_col(jnp.stack([r[:, half:] for r in rows]))
    at_start = lax.axis_index("col") == 0
    return jnp.concatenate([jnp.where(at_start, own, got), jnp.where(at_start, got, own)], axis=0)


def sent_back(dealt):
    groups = lax.axis_size("dp")
    me = lax.axis_index("dp")
    parts = []
    for hop in range(groups):
        piece = lax.dynamic_index_in_dim(dealt, (me + hop) % groups, 0, keepdims=False)
        if hop:
            piece = lax.ppermute(piece, "dp", [(i, (i + hop) % groups) for i in range(groups)])
        parts.append(piece)
    return parts


def in_given_order(parts, dest_group):
    groups = lax.axis_size("dp")
    hops = ((lax.axis_index("dp") - dest_group) % groups)[:, None, None]
    out = jnp.where(hops == 0, parts[0][None], jnp.zeros((), BF))
    for hop in range(1, groups):
        out = jnp.where(hops == hop, parts[hop][None], out)
    return out


def matmul(a, b, over_a, over_b):
    return lax.dot_general(a, b, (((over_a,), (over_b,)), ((), ())), preferred_element_type=F32)


def per_device(
    hidden, targets, lengths, dest_group, norm_gain, gate_input_weight, auxiliary_weight,
    conv_x, conv_x_bias, conv_bc, conv_bc_bias, dt_bias, a_log, d_skip, out_gain, output_weight,
):
    row_count = lax.axis_size("row")
    col_count = lax.axis_size("col")
    row_index = lax.axis_index("row")
    col_index = lax.axis_index("col")
    group_index = lax.axis_index("dp")
    seq_group, local_len, width_col = hidden.shape
    heads = gate_input_weight.shape[1]
    pair = gate_input_weight.shape[2]
    head_dim = pair // 2
    inner = heads * head_dim
    wide = heads * pair
    aux = conv_bc.shape[1]
    head_total = auxiliary_weight.shape[1] - aux
    steps = -(-heads // 16) * 16
    seq_col = seq_group // col_count
    model_width = width_col * col_count
    inner_width = inner * row_count
    all_tokens = lengths.shape[0] * local_len * row_count
    valid_count = jnp.sum(lengths).astype(F32)
    group_lengths = lax.dynamic_slice_in_dim(lengths, group_index * seq_group, seq_group, 0)
    own_lengths = lax.dynamic_slice_in_dim(group_lengths, col_index * seq_col, seq_col, 0)

    def widened(v):
        mine = lax.dynamic_slice_in_dim(v, col_index * seq_col, seq_col, 0)
        theirs = lax.dynamic_slice_in_dim(v, (1 - col_index) * seq_col, seq_col, 0)
        return jnp.concatenate([mine, other_col(theirs)], axis=2)

    u_low = widened(hidden)
    gain = jnp.concatenate([norm_gain, other_col(norm_gain)])
    u = [u_low[k].astype(F32) for k in range(seq_col)]
    inv_rms = [lax.rsqrt(jnp.mean(v * v, axis=1, keepdims=True) + EPSILON) for v in u]
    spread = lambda v: lax.all_gather(v, "row", axis=0, tiled=True)
    normed = [(v * r * gain[None, :]).astype(BF) for v, r in zip(u, inv_rms, strict=True)]
    scaled = [spread(normed[0])]
    for v in normed[1:]:
        scaled.append(spread(tie(v, scaled[-1])))
    in_own = tie(
        jnp.concatenate(
            [
                gate_input_weight.reshape(width_col, wide),
                auxiliary_weight[:, :aux],
                lax.dynamic_slice_in_dim(auxiliary_weight, aux + row_index * heads, heads, 1),
                jnp.zeros((width_col, steps - heads), BF),
            ],
            axis=1,
        )
    )
    out_own = output_weight.reshape(inner, width_col)
    in_other, out_other = other_col(in_own), other_col(out_own)
    in_weight = tie(jnp.concatenate([in_own, in_other], axis=0))

    scaled[0] = tie(scaled[0], in_weight)

    column = lambda v: v.reshape(-1, 1)
    taps = jnp.concatenate(
        [
            conv_x.reshape(-1, inner).T,
            column(conv_x_bias),
            column(jnp.repeat(d_skip, head_dim)),
            column(out_gain),
            jnp.zeros((inner, 1), F32),
        ],
        axis=1,
    )
    bc_taps = jnp.concatenate([conv_bc.T, column(conv_bc_bias), jnp.zeros((aux, 3), F32)], axis=1)
    dt_par = jnp.pad(jnp.stack([dt_bias, a_log], axis=1), ((0, steps - heads), (0, 6)))

    targets_own = widened(targets)
    positions = row_index * local_len + jnp.arange(local_len, dtype=jnp.int32)

    zx, gated, entering, kept_rows, scatters = [], [], [], [], []
    result, g_result, g_rows, coef = [], [], [], []
    loss_part = jnp.zeros((), F32)

    def finish(k, *before):
        nonlocal loss_part
        summed, total_square = scatters[k].last(*before)
        gate_inv = lax.rsqrt(total_square / inner_width + EPSILON)[:, None]
        branch = summed * gate_inv
        full = u[k] + branch
        valid = (positions < own_lengths[k]).astype(F32)[:, None]
        difference = (full - targets_own[k].astype(F32)) * valid
        loss_part = loss_part + jnp.sum(difference * difference)
        grad = difference * (all_tokens / valid_count)
        result.append(full.astype(BF))
        g_result.append(grad)
        share = gate_inv[:, 0] * gate_inv[:, 0] * jnp.sum(grad * branch, axis=1) / inner_width
        placed = lax.dynamic_update_slice_in_dim(
            jnp.zeros((local_len * row_count,), F32), share, row_index * local_len, 0
        )
        coef.append(sum_over_row(placed[None, :]))
        sent = (grad * gate_inv).astype(BF)
        g_rows.append(spread(tie(sent, *g_rows[-1:])))
        return sent

    for k in range(seq_col):
        source = scaled[k] if k == 0 else tie(scaled[k], *scatters[-1].sent)
        projected = matmul(in_weight, source, 0, 1)
        if k > 0:
            scatters[-1].second(projected)
            projected = tie(projected, *scatters[-1].passed)
        zx.append(projected)
        g, square, e, *kept = scan_forward(projected, taps, bc_taps, dt_par, heads)
        kept_rows.append(kept)
        gated.append(g)
        entering.append(e)
        if k > 0:
            g = tie(g, finish(k - 1, g))
        left, right = (matmul(g, w, 0, 0).astype(BF) for w in (out_own, out_other))
        scatters.append(Scatter(left, right, square))
        scatters[-1].first()
    out_weight = tie(jnp.concatenate(tie((out_own, out_other), *scatters[-1].sent), axis=1))
    scatters[-1].second(out_weight, *coef)
    finish(seq_col - 1)

    to_rows = lambda g: Scatter(*(matmul(g, w, 0, 1).astype(BF) for w in (in_own, in_other)))
    g_in, scatters = [], []
    sums = [0.0, 0.0, 0.0]
    w_out_part = 0.0
    for k in range(seq_col):
        final = k == seq_col - 1
        whole = g_rows[k] if k == 0 else tie(g_rows[k], g_in[-1], coef[k])
        w_out_part = w_out_part + matmul(gated[k], whole, 1, 0)
        gn = matmul(out_weight, tie(whole, w_out_part) if final else whole, 1, 1)
        before = (w_out_part,)
        if k == 0:
            dealt_output = dealt_rows(result)
            output_parts = sent_back(dealt_output)
        if final:
            received = other_col(w_out_part[:, width_col:].astype(BF))
            w_out_low = (w_out_part[:, :width_col] + received.astype(F32)).astype(BF)
            w_out_sum = lax.psum(w_out_low, "dp")
            before = (w_out_low,)
        if k > 0:
            scatters.append(to_rows(tie(g_in[-1], *before)))
            scatters[-1].first()
            before = scatters[-1].sent
        gn = tie(gn, *before)
        g, gx, gbc, gdt = scan_backward(
            zx[k], kept_rows[k], entering[k], gn, coef[k], taps, bc_taps, dt_par, heads
        )
        sums = [a + b for a, b in zip(sums, (gx, gbc, gdt), strict=True)]
        if k == 0:
            g = tie(g, *output_parts)
        if k > 0:
            scatters[-1].second(g)
            g = tie(g, *scatters[-1].passed)
        g_in.append(g)

    there, left, right = late_products(scaled, g_in, in_own.T, in_other.T, wide)
    there, left, right, g_in[-1] = tie((there, left, right, g_in[-1]), w_out_sum)
    scatters.append(Scatter(left, right))
    scatters[-1].first()
    g_late = g_in[:-1] + [tie(g_in[-1], *scatters[-1].sent)]
    in_low = product(
        "tt", list(zip(scaled, g_late)), TILE, added=other_col(there), columns=width_col, wide=wide
    )
    scatters[-1].second(in_low)
    w_zx = lax.psum(in_low, "dp")
    g_aux = [g[wide:] for g in g_in]
    g_aux[-1] = tie(g_aux[-1], in_low)
    aux_part = sum(matmul(scaled[i], g_aux[i], 0, 1) for i in range(seq_col))
    aux_half = aux_part[:width_col] + other_col(aux_part[width_col:])
    aux_half = jnp.concatenate(
        [
            aux_half[:, :aux],
            lax.dynamic_update_slice_in_dim(
                jnp.zeros((width_col, head_total), F32),
                aux_half[:, aux : aux + heads],
                row_index * heads,
                1,
            ),
        ],
        axis=1,
    )
    gain_part = jnp.zeros((model_width,), F32)
    g_u = []
    for k in range(seq_col):
        g_scaled, _ = scatters[k].last(*((in_low,) if k < seq_col - 1 else ()))
        gain_part = gain_part + jnp.sum(g_scaled * u[k] * inv_rms[k], axis=0)
        weighted = g_scaled * gain[None, :]
        dot = jnp.sum(weighted * u[k], axis=1, keepdims=True) / model_width
        cube = inv_rms[k] * inv_rms[k] * inv_rms[k]
        g_u.append((g_result[k] + inv_rms[k] * weighted - u[k] * (cube * dot)).astype(BF))
    hidden_parts = sent_back(tie(dealt_rows(g_u), w_zx))
    w_aux = sum_over_row_dp(aux_half)

    gx, gbc, gdt = sums
    flat = jnp.concatenate(
        [gx.reshape(-1), gdt[:, 1:3].reshape(-1), gbc.reshape(-1), loss_part[None]]
    )
    vector = jnp.concatenate([flat, gain_part[:width_col]]) + other_col(
        jnp.concatenate([flat, gain_part[width_col:]])
    )
    own_size = inner * 8 + steps * 2
    vector = jnp.concatenate([vector[:own_size], butterfly(vector[own_size:], "row")])
    vector = butterfly(vector, "dp")
    gx = vector[: inner * 8].reshape(inner, 8)
    gdt = vector[inner * 8 : own_size].reshape(steps, 2)
    shared = vector[own_size:]
    gbc = shared[: aux * 8].reshape(aux, 8)
    loss = shared[aux * 8] * 0.5 / valid_count
    gain_sum = shared[aux * 8 + 1 :]
    return (
        loss,
        in_given_order(output_parts, dest_group),
        in_given_order(hidden_parts, dest_group),
        gain_sum,
        w_zx.astype(F32).reshape(width_col, heads, pair),
        w_aux.astype(F32),
        gx[:, :4].T.reshape(4, heads, head_dim),
        gx[:, 4].reshape(heads, head_dim),
        gbc[:, :4].T,
        gbc[:, 4],
        gdt[:heads, 0],
        gdt[:heads, 1],
        gx[:, 5].reshape(heads, head_dim).sum(axis=1),
        gx[:, 6].reshape(heads, head_dim),
        w_out_sum.astype(F32).reshape(heads, head_dim, width_col),
    )


def solution(mesh):
    placed = (
        P("dp", "row", "col"),
        P("dp", "row", "col"),
        P(),
        P("dp"),
        P("col"),
        P("col", "row", None),
        P("col", None),
        P(None, "row", None),
        P("row", None),
        P(),
        P(),
        P("row"),
        P("row"),
        P("row"),
        P("row", None),
        P("row", None, "col"),
    )
    return jax.shard_map(
        per_device,
        mesh=mesh,
        in_specs=placed,
        out_specs=(
            P(),
            P("dp", "row", "col"),
            P("dp", "row", "col"),
            P("col"),
            P("col", "row", None),
            P("col", None),
            P(None, "row", None),
            P("row", None),
            P(),
            P(),
            P("row"),
            P("row"),
            P("row"),
            P("row", None),
            P("row", None, "col"),
        ),
        check_vma=False,
    )
```

```python
import functools
import jax
import jax.numpy as jnp
from jax import lax
from jax.experimental import pallas as pl
from jax.experimental.pallas import tpu as pltpu
from jax.sharding import PartitionSpec as P

BF = jnp.bfloat16
F32 = jnp.float32
SPAN = 512
PART = 128
TILE = 256
LOG2E = 1.4426950408889634
EDGE = 128
EPSILON = 1e-05


def nn(a, b):
    return lax.dot_general(a, b, (((1,), (0,)), ((), ())), preferred_element_type=F32)


def nt(a, b):
    return lax.dot_general(a, b, (((1,), (1,)), ((), ())), preferred_element_type=F32)


def tn(a, b):
    return lax.dot_general(a, b, (((0,), (0,)), ((), ())), preferred_element_type=F32)


def exact(a, b):
    return lax.dot_general(
        a, b, (((1,), (0,)), ((), ())), precision=lax.Precision.HIGHEST, preferred_element_type=F32
    )


def sigmoid(v):
    return 0.5 * jnp.tanh(0.5 * v) + 0.5


def softplus(v):
    return jnp.maximum(v, 0.0) + jnp.log1p(jnp.exp(-jnp.abs(v)))


def wide(v, span):
    return jnp.concatenate([v] * (span // v.shape[1]), axis=1)


def taps_at(taps_ref, at, span):
    return lambda k: wide(taps_ref[k, at, :], span)


def spread_taps(from_ref, to_ref):
    for k in range(to_ref.shape[0]):
        to_ref[k] = jnp.broadcast_to(from_ref[:, k : k + 1], to_ref.shape[1:])


def move_matrix(ahead):
    rows = lax.broadcasted_iota(jnp.int32, (2 * EDGE, EDGE), 0)
    cols = lax.broadcasted_iota(jnp.int32, (2 * EDGE, EDGE), 1)
    moves = [rows == (cols + k if ahead else cols + EDGE - k) for k in (1, 2, 3)]
    return jnp.concatenate([m.astype(F32).astype(BF) for m in moves], axis=1)


def moved(joined, matrix):
    size = joined.shape[0]
    parts = range(joined.shape[1] // EDGE - 1)
    low = joined.astype(BF)
    stacked = jnp.concatenate([low[:, q * EDGE : (q + 2) * EDGE] for q in parts], axis=0)
    out = nn(stacked, matrix)
    return [
        jnp.concatenate(
            [out[q * size : (q + 1) * size, k * EDGE : (k + 1) * EDGE] for q in parts], axis=1
        )
        for k in range(3)
    ]


def conv_of(before, now, tap, matrix):
    one, two, three = moved(jnp.concatenate([before, now], axis=1), matrix)
    return tap(4) + tap(3) * now + tap(2) * one + tap(1) * two + tap(0) * three


def conv_back(now, after, tap, matrix):
    one, two, three = moved(jnp.concatenate([now, after], axis=1), matrix)
    return tap(3) * now + tap(2) * one + tap(1) * two + tap(0) * three, (one, two, three)


def fold(v):
    total = v[:, :EDGE]
    for k in range(1, v.shape[1] // EDGE):
        total = total + v[:, k * EDGE : (k + 1) * EDGE]
    return total


def lanes(q):
    return slice(q * PART, (q + 1) * PART)


def span_common(bc_before, bc_now, dt_raw, bc_tap, dt_par, matrix):
    pre = conv_of(bc_before, bc_now, bc_tap, matrix)
    sig = sigmoid(pre)
    act = pre * sig
    half = act.shape[0] // 2
    b_t = act[:half].astype(BF)
    c_t = act[half:].astype(BF)
    parts = range(bc_now.shape[1] // PART)
    rows = lax.broadcasted_iota(jnp.int32, (PART, PART), 0)
    cols = lax.broadcasted_iota(jnp.int32, (PART, PART), 1)
    causal = rows <= cols
    steps = softplus(dt_raw + dt_par[:, 0:1])
    rate = -jnp.exp(dt_par[:, 1:2])
    gone = steps * (rate * LOG2E)
    decay = [exact(gone[:, lanes(q)], causal.astype(F32)) for q in parts]
    last = [d[:, PART - 1 :] for d in decay]
    decay_n = [d.T for d in decay]
    left = jnp.concatenate([jnp.exp2(e - d) for e, d in zip(last, decay)], axis=1)
    kept = [jnp.exp2(e) for e in last]
    decay = jnp.concatenate(decay, axis=1)
    grown = jnp.exp2(decay)
    b_n = [b_t[:, lanes(q)].astype(F32).T.astype(BF) for q in parts]
    scores = [jnp.where(causal, nn(b_n[q], c_t[:, lanes(q)]), 0.0) for q in parts]
    return pre, sig, b_t, c_t, b_n, scores, causal, steps, rate, decay, decay_n, grown, left, kept


def forward_kernel(
    heads, zx_ref, bc_ref, dt_ref, taps_ref, bc_taps_ref, dt_par_ref,
    gated_ref, square_ref, enter_ref, x_ref, slope_ref, y_ref,
    state, x_tail, bc_tail, carry, xd_all, tailed, scores_all, x_taps, bc_taps, matrix_ref,
):
    span = zx_ref.shape[1]
    inner = state.shape[0]
    size = inner // heads
    parts = range(span // PART)

    @pl.when(pl.program_id(0) == 0)
    def _():
        state[...] = jnp.zeros_like(state)
        x_tail[...] = jnp.zeros_like(x_tail)
        bc_tail[...] = jnp.zeros_like(bc_tail)
        spread_taps(taps_ref, x_taps)
        spread_taps(bc_taps_ref, bc_taps)
        matrix_ref[...] = move_matrix(False)

    matrix = matrix_ref[...]
    bc_now = bc_ref[...]
    _, _, _, c_t, b_n, scores, _, steps, _, decay, decay_n, grown, left, kept = span_common(
        bc_tail[...], bc_now, dt_ref[...], taps_at(bc_taps, slice(None), span), dt_par_ref[...], matrix
    )
    bc_tail[...] = bc_now[:, span - EDGE :]
    for q in parts:
        scores_all[q] = scores[q]
    for h in range(heads):
        at = slice(h * size, (h + 1) * size)
        x_raw = zx_ref[(2 * h + 1) * size : (2 * h + 2) * size, :]
        pre = conv_of(x_tail[at, :], x_raw, taps_at(x_taps, at, span), matrix)
        x_tail[at, :] = x_raw[:, span - EDGE :]
        sig = sigmoid(pre)
        x = pre * sig
        xd = x * steps[h : h + 1, :]
        x_ref[at, :] = x
        slope_ref[at, :] = sig + x * (1.0 - sig)
        xd_all[at, :] = xd.astype(BF)
        tailed[at, :] = (xd * left[h : h + 1, :]).astype(BF)
    for q in parts:
        entering = state[...].astype(BF)
        enter_ref[q * inner : (q + 1) * inner, :] = entering
        carry[:, lanes(q)] = nn(entering, c_t[:, lanes(q)])
        more = nn(tailed[:, lanes(q)], b_n[q])
        for h in range(heads):
            at = slice(h * size, (h + 1) * size)
            state[at, :] = state[at, :] * kept[q][h : h + 1, :] + more[at, :]
    square = jnp.zeros((size, span), F32)
    for h in range(heads):
        at = slice(h * size, (h + 1) * size)
        z = zx_ref[2 * h * size : (2 * h + 1) * size, :]
        tap = taps_at(x_taps, at, span)
        mixed = []
        for q in parts:
            gap = decay[h : h + 1, lanes(q)] - decay_n[q][:, h : h + 1]
            mixing = scores_all[q] * jnp.exp2(jnp.minimum(gap, 0.0))
            mixed.append(nn(xd_all[at, lanes(q)], mixing.astype(BF)))
        y = jnp.concatenate(mixed, axis=1) + carry[at, :] * grown[h : h + 1, :]
        y_ref[at, :] = y
        y = y + tap(5) * x_ref[at, :]
        gated = y * (z * sigmoid(z))
        square = square + gated * gated
        gated_ref[at, :] = (gated * tap(6)).astype(BF)
    square_ref[...] = jnp.sum(square, axis=0, keepdims=True)


def backward_kernel(
    heads, zx_ref, x_ref, slope_ref, y_ref, bc_ref, bc_before_ref, dt_ref, enter_ref, gn_ref, coef_ref,
    taps_ref, bc_taps_ref, dt_par_ref,
    gzx_ref, gx_sum_ref, gbc_sum_ref, gdt_sum_ref,
    dstate, x_head, bc_head, from_state, grown_g, tailed, x_acc, bc_acc, dt_acc, rsum, dsum,
    dxd_all, gy_all, scores_all, dscores_all, held_all, x_taps, bc_taps_all, matrix_ref,
    back_matrix_ref,
):
    span = zx_ref.shape[1]
    inner = dstate.shape[0]
    size = inner // heads
    half = bc_ref.shape[0] // 2
    wide = zx_ref.shape[0]
    parts = range(span // PART)
    step = pl.program_id(0)
    count = pl.num_programs(0)
    first = step == count - 1

    @pl.when(step == 0)
    def _():
        dstate[...] = jnp.zeros_like(dstate)
        x_head[...] = jnp.zeros_like(x_head)
        bc_head[...] = jnp.zeros_like(bc_head)
        x_acc[...] = jnp.zeros_like(x_acc)
        bc_acc[...] = jnp.zeros_like(bc_acc)
        dt_acc[...] = jnp.zeros_like(dt_acc)
        rsum[...] = jnp.zeros_like(rsum)
        dsum[...] = jnp.zeros_like(dsum)
        held_all[...] = jnp.zeros_like(held_all)
        spread_taps(taps_ref, x_taps)
        spread_taps(bc_taps_ref, bc_taps_all)
        matrix_ref[...] = move_matrix(False)
        back_matrix_ref[...] = move_matrix(True)

    matrix, back_matrix = matrix_ref[...], back_matrix_ref[...]
    live = jnp.where(first, 0.0, 1.0)
    bc_tap = taps_at(bc_taps_all, slice(None), span)
    dt_raw = dt_ref[...]
    bc_now = bc_ref[...]
    (
        bc_pre, bc_sig, b_t, c_t, b_n, scores, causal, steps, rate, decay, decay_n, grown, left, kept
    ) = span_common(bc_before_ref[...] * live, bc_now, dt_raw, bc_tap, dt_par_ref[...], matrix)
    for q in parts:
        scores_all[q] = scores[q]
        dscores_all[q] = jnp.zeros((PART, PART), F32)
    coef = coef_ref[...]
    for h in range(heads):
        at = slice(h * size, (h + 1) * size)
        z = zx_ref[2 * h * size : (2 * h + 1) * size, :]
        tap = taps_at(x_taps, at, span)
        x = x_ref[at, :]
        xd = x * steps[h : h + 1, :]
        xd_low = xd.astype(BF)
        tailed[at, :] = (xd * left[h : h + 1, :]).astype(BF)
        ratios, mixings = [], []
        for q in parts:
            gap = decay[h : h + 1, lanes(q)] - decay_n[q][:, h : h + 1]
            ratios.append(jnp.exp2(jnp.minimum(gap, 0.0)))
            mixings.append((scores_all[q] * ratios[q]).astype(BF))
        grown_h = grown[h : h + 1, :]
        y_scan = y_ref[at, :]
        y = y_scan + tap(5) * x
        zsig = sigmoid(z)
        silu_z = z * zsig
        gated = y * silu_z
        gn = gn_ref[at, :].astype(F32)
        g_gated = tap(6) * gn - gated * coef
        gy = g_gated * silu_z
        gzx_ref[2 * h * size : (2 * h + 1) * size, :] = (
            g_gated * y * (zsig + silu_z * (1.0 - zsig))
        ).astype(BF)
        gy_low = gy.astype(BF)
        gy_all[at, :] = gy_low
        grown_g[at, :] = (gy * grown_h).astype(BF)
        rsum[h : h + 1, :] = jnp.sum(gy_low.astype(F32) * y_scan, axis=0, keepdims=True)
        x_acc[5, at, :] = x_acc[5, at, :] + fold(gy * x)
        x_acc[6, at, :] = x_acc[6, at, :] + fold(gn * gated)
        for q in parts:
            dxd_all[at, lanes(q)] = nt(gy_low[:, lanes(q)], mixings[q])
            dscores_all[q] = dscores_all[q] + tn(xd_low[:, lanes(q)], gy_low[:, lanes(q)]) * ratios[q]
    db, dc, flows = [], [], []
    for q in reversed(parts):
        entering = enter_ref[q * inner : (q + 1) * inner, :]
        leaving = dstate[...].astype(BF)
        from_state[:, lanes(q)] = nn(leaving, b_t[:, lanes(q)])
        low = jnp.where(causal, dscores_all[q], 0.0).astype(BF)
        dc.insert(0, nn(b_t[:, lanes(q)], low) + tn(entering, grown_g[:, lanes(q)]))
        db.insert(0, nt(c_t[:, lanes(q)], low) + tn(leaving, tailed[:, lanes(q)]))
        more = nt(grown_g[:, lanes(q)], c_t[:, lanes(q)])
        for h in range(heads):
            at = slice(h * size, (h + 1) * size)
            passed = dstate[at, :] * kept[q][h : h + 1, :]
            held_all[q, h : h + 1, :] = jnp.sum(passed * entering[at, :].astype(F32), axis=0, keepdims=True)
            dstate[at, :] = passed + more[at, :]
    for h in range(heads):
        at = slice(h * size, (h + 1) * size)
        x_raw = zx_ref[(2 * h + 1) * size : (2 * h + 2) * size, :]
        tap = taps_at(x_taps, at, span)
        x = x_ref[at, :]
        steps_h = steps[h : h + 1, :]
        dx_state = from_state[at, :] * left[h : h + 1, :]
        dxd = dxd_all[at, :] + dx_state
        xd_wide = (x * steps_h).astype(BF).astype(F32)
        rsum[h : h + 1, :] = rsum[h : h + 1, :] - jnp.sum(xd_wide * dxd, axis=0, keepdims=True)
        dsum[h : h + 1, :] = jnp.sum(x * dxd, axis=0, keepdims=True)
        held = jnp.sum(xd_wide * dx_state, axis=0, keepdims=True)
        for q in parts:
            held_all[q, h : h + 1, :] = held_all[q, h : h + 1, :] + held[:, lanes(q)]
        dx = dxd * steps_h + tap(5) * gy_all[at, :].astype(F32)
        gpre = dx * slope_ref[at, :]
        g_raw, later = conv_back(gpre, x_head[at, :], tap, back_matrix)
        x_head[at, :] = gpre[:, :EDGE]
        gzx_ref[(2 * h + 1) * size : (2 * h + 2) * size, :] = g_raw.astype(BF)
        for k, moved_g in enumerate((gpre, *later)):
            x_acc[3 - k, at, :] = x_acc[3 - k, at, :] + fold(moved_g * x_raw)
        x_acc[4, at, :] = x_acc[4, at, :] + fold(gpre)
    gbc = jnp.concatenate([jnp.concatenate(db, axis=1), jnp.concatenate(dc, axis=1)], axis=0)
    gbc = gbc * (bc_sig + bc_pre * bc_sig * (1.0 - bc_sig))
    g_raw, later = conv_back(gbc, bc_head[...], bc_tap, back_matrix)
    bc_head[...] = gbc[:, :EDGE]
    gzx_ref[wide : wide + 2 * half, :] = g_raw.astype(BF)
    for k, moved_g in enumerate((gbc, *later)):
        bc_acc[3 - k] = bc_acc[3 - k] + fold(moved_g * bc_now)
    bc_acc[4] = bc_acc[4] + fold(gbc)
    after = jnp.logical_or(
        jnp.logical_not(causal),
        lax.broadcasted_iota(jnp.int32, (PART, PART), 0) == lax.broadcasted_iota(jnp.int32, (PART, PART), 1),
    ).astype(F32)
    da = jnp.concatenate(
        [
            exact(rsum[:, lanes(q)], after) + jnp.sum(held_all[q], axis=1, keepdims=True)
            for q in parts
        ],
        axis=1,
    )
    g_steps = dsum[...] + rate * da
    g_dt = g_steps * sigmoid(dt_raw + dt_par_ref[:, 0:1])
    gzx_ref[wide + 2 * half :, :] = g_dt.astype(BF)
    dt_acc[:, 1:2] = dt_acc[:, 1:2] + jnp.sum(g_dt, axis=1, keepdims=True)
    dt_acc[:, 2:3] = dt_acc[:, 2:3] + jnp.sum(da * steps * rate, axis=1, keepdims=True)

    @pl.when(first)
    def _():
        for k in range(7):
            gx_sum_ref[:, k : k + 1] = jnp.sum(x_acc[k], axis=1, keepdims=True)
        for k in range(5):
            gbc_sum_ref[:, k : k + 1] = jnp.sum(bc_acc[k], axis=1, keepdims=True)
        gdt_sum_ref[...] = dt_acc[...]


def scan_forward(zx, taps, bc_taps, dt_par, heads, span=SPAN):
    inner = taps.shape[0]
    length = zx.shape[1]
    aux = bc_taps.shape[0]
    steps = dt_par.shape[0]
    states = aux // 2
    body = functools.partial(forward_kernel, heads)
    whole = lambda r, c: pl.BlockSpec((r, c), lambda i: (0, 0))
    return pl.pallas_call(
        body,
        grid=(length // span,),
        in_specs=[
            pl.BlockSpec((2 * inner, span), lambda i: (0, i)),
            pl.BlockSpec((aux, span), lambda i: (2 * inner // aux, i)),
            pl.BlockSpec((steps, span), lambda i: ((2 * inner + aux) // steps, i)),
            whole(inner, 8), whole(aux, 8), whole(steps, 8),
        ],
        out_specs=[
            pl.BlockSpec((inner, span), lambda i: (0, i)),
            pl.BlockSpec((1, span), lambda i: (0, i)),
            pl.BlockSpec((span // PART * inner, states), lambda i: (i, 0)),
        ]
        + [pl.BlockSpec((inner, span), lambda i: (0, i))] * 3,
        out_shape=[
            jax.ShapeDtypeStruct((inner, length), BF),
            jax.ShapeDtypeStruct((1, length), F32),
            jax.ShapeDtypeStruct((length // PART * inner, states), BF),
        ]
        + [jax.ShapeDtypeStruct((inner, length), F32)] * 3,
        scratch_shapes=[
            pltpu.VMEM((inner, states), F32),
            pltpu.VMEM((inner, EDGE), F32),
            pltpu.VMEM((aux, EDGE), F32),
            pltpu.VMEM((inner, span), F32),
            pltpu.VMEM((inner, span), BF),
            pltpu.VMEM((inner, span), BF),
            pltpu.VMEM((span // PART, PART, PART), F32),
            pltpu.VMEM((7, inner, EDGE), F32),
            pltpu.VMEM((5, aux, EDGE), F32),
            pltpu.VMEM((2 * EDGE, 3 * EDGE), BF),
        ],
        compiler_params=pltpu.CompilerParams(vmem_limit_bytes=56 * 2**20),
        name="scan_forward",
    )(zx, zx, zx, taps, bc_taps, dt_par)


def scan_backward(zx, kept, entering, gn, coef, taps, bc_taps, dt_par, heads, span=SPAN):
    inner = taps.shape[0]
    length = zx.shape[1]
    aux = bc_taps.shape[0]
    steps = dt_par.shape[0]
    states = aux // 2
    count = length // span
    ratio = span // EDGE
    body = functools.partial(backward_kernel, heads)
    whole = lambda r, c: pl.BlockSpec((r, c), lambda i: (0, 0))
    rev = lambda i: count - 1 - i
    before = lambda i: jnp.maximum((count - 1 - i) * ratio - 1, 0)
    return pl.pallas_call(
        body,
        grid=(count,),
        in_specs=[
            pl.BlockSpec((2 * inner, span), lambda i: (0, rev(i))),
            pl.BlockSpec((inner, span), lambda i: (0, rev(i))),
            pl.BlockSpec((inner, span), lambda i: (0, rev(i))),
            pl.BlockSpec((inner, span), lambda i: (0, rev(i))),
            pl.BlockSpec((aux, span), lambda i: (2 * inner // aux, rev(i))),
            pl.BlockSpec((aux, EDGE), lambda i: (2 * inner // aux, before(i))),
            pl.BlockSpec((steps, span), lambda i: ((2 * inner + aux) // steps, rev(i))),
            pl.BlockSpec((span // PART * inner, states), lambda i: (rev(i), 0)),
            pl.BlockSpec((inner, span), lambda i: (0, rev(i))),
            pl.BlockSpec((1, span), lambda i: (0, rev(i))),
            whole(inner, 8), whole(aux, 8), whole(steps, 8),
        ],
        out_specs=[
            pl.BlockSpec((2 * inner + aux + steps, span), lambda i: (0, rev(i))),
            whole(inner, 8), whole(aux, 8), whole(steps, EDGE),
        ],
        out_shape=[
            jax.ShapeDtypeStruct((2 * inner + aux + steps, length), BF),
            jax.ShapeDtypeStruct((inner, 8), F32),
            jax.ShapeDtypeStruct((aux, 8), F32),
            jax.ShapeDtypeStruct((steps, EDGE), F32),
        ],
        scratch_shapes=[
            pltpu.VMEM((inner, states), F32),
            pltpu.VMEM((inner, EDGE), F32),
            pltpu.VMEM((aux, EDGE), F32),
            pltpu.VMEM((inner, span), F32),
            pltpu.VMEM((inner, span), BF),
            pltpu.VMEM((inner, span), BF),
            pltpu.VMEM((7, inner, EDGE), F32),
            pltpu.VMEM((5, aux, EDGE), F32),
            pltpu.VMEM((steps, EDGE), F32),
            pltpu.VMEM((steps, span), F32),
            pltpu.VMEM((steps, span), F32),
            pltpu.VMEM((inner, span), F32),
            pltpu.VMEM((inner, span), BF),
            pltpu.VMEM((span // PART, PART, PART), F32),
            pltpu.VMEM((span // PART, PART, PART), F32),
            pltpu.VMEM((span // PART, steps, PART), F32),
            pltpu.VMEM((7, inner, EDGE), F32),
            pltpu.VMEM((5, aux, EDGE), F32),
            pltpu.VMEM((2 * EDGE, 3 * EDGE), BF),
            pltpu.VMEM((2 * EDGE, 3 * EDGE), BF),
        ],
        compiler_params=pltpu.CompilerParams(vmem_limit_bytes=56 * 2**20),
        name="scan_backward",
    )(zx, *kept, zx, zx, zx, entering, gn, coef, taps, bc_taps, dt_par)


def product_kernel(form, count, added, *refs):
    out_ref = refs[-1]
    total = refs[2 * count][...].astype(F32) if added else None
    for i in range(count):
        a, b = refs[2 * i][...], refs[2 * i + 1][...]
        if form == "tt":
            a = a.T
        over = 0 if form == "nn" else 1
        term = lax.dot_general(a, b, (((1,), (over,)), ((), ())), preferred_element_type=F32)
        total = term if total is None else total + term
    out_ref[...] = total.astype(out_ref.dtype)


def product(form, pairs, tile, added=None, dtype=BF, start=0, columns=None, wide=None):
    first, other = pairs[0]
    rows = columns or first.shape[1 if form == "tt" else 0]
    cols = wide or other.shape[1 if form == "nn" else 0]
    operands, specs = [], []
    for a, b in pairs:
        operands += [a, b]
        if form == "tt":
            specs.append(pl.BlockSpec((a.shape[0], tile), lambda i: (0, start // tile + i)))
        else:
            specs.append(pl.BlockSpec((tile, a.shape[1]), lambda i: (i, 0)))
        block = b.shape if form == "nn" else (cols, b.shape[1])
        specs.append(pl.BlockSpec(block, lambda i: (0, 0), pipeline_mode=pl.Buffered(1)))
    if added is not None:
        operands.append(added)
        specs.append(pl.BlockSpec((tile, cols), lambda i: (i, 0)))
    return pl.pallas_call(
        functools.partial(product_kernel, form, len(pairs), added is not None),
        grid=(rows // tile,),
        in_specs=specs,
        out_specs=pl.BlockSpec((tile, cols), lambda i: (i, 0)),
        out_shape=jax.ShapeDtypeStruct((rows, cols), dtype),
        compiler_params=pltpu.CompilerParams(vmem_limit_bytes=56 * 2**20),
        name="product_" + form,
    )(*operands)


def late_kernel(count, wide, first, *refs):
    scaled, g_all, g_tile = refs[:count], refs[count : 2 * count], refs[2 * count]
    weights, outs = refs[2 * count + 1 : 2 * count + 3], refs[2 * count + 3 : 2 * count + 6]
    held, sems = refs[2 * count + 6 : 2 * count + 8], refs[2 * count + 8]
    step = pl.program_id(0)
    copies = [pltpu.make_async_copy(weights[k], held[k], sems.at[k]) for k in range(2)]

    @pl.when(step == 0)
    def _():
        for copy in copies:
            copy.start()

    @pl.when(step < first)
    def _():
        total = None
        for s, g in zip(scaled, g_all):
            term = nt(s[...].T, g[:wide, :])
            total = term if total is None else total + term
        outs[0][...] = total.astype(BF)

    @pl.when(step == first)
    def _():
        for copy in copies:
            copy.wait()

    @pl.when(step >= first)
    def _():
        rows = g_tile[...].T
        for k in range(2):
            outs[1 + k][...] = nn(rows, held[k][...]).astype(BF)


def late_products(scaled, g_in, own, other, wide):
    depth, width = own.shape
    length = scaled[0].shape[0]
    first = width // TILE
    count = len(scaled)
    at = lambda i: jnp.maximum(i - first, 0)
    until = lambda i: jnp.minimum(i, first - 1)
    return pl.pallas_call(
        functools.partial(late_kernel, count, wide, first),
        grid=(first + length // TILE,),
        in_specs=[pl.BlockSpec((length, TILE), lambda i: (0, first + until(i))) for _ in scaled]
        + [pl.BlockSpec(g.shape, lambda i: (0, 0), pipeline_mode=pl.Buffered(1)) for g in g_in]
        + [pl.BlockSpec((depth, TILE), lambda i: (0, at(i)))]
        + [pl.BlockSpec(memory_space=pl.ANY)] * 2,
        out_specs=[
            pl.BlockSpec((TILE, wide), lambda i: (until(i), 0)),
            pl.BlockSpec((TILE, width), lambda i: (at(i), 0)),
            pl.BlockSpec((TILE, width), lambda i: (at(i), 0)),
        ],
        out_shape=[
            jax.ShapeDtypeStruct((width, wide), BF),
            jax.ShapeDtypeStruct((length, width), BF),
            jax.ShapeDtypeStruct((length, width), BF),
        ],
        scratch_shapes=[
            pltpu.VMEM(own.shape, BF),
            pltpu.VMEM(own.shape, BF),
            pltpu.SemaphoreType.DMA((2,)),
        ],
        compiler_params=pltpu.CompilerParams(vmem_limit_bytes=56 * 2**20),
        name="late_products",
    )(*scaled, *g_in, g_in[-1], own, other)


def tie(value, *before):
    return lax.optimization_barrier((value, *before))[0]


def split(v, width):
    rows = []
    rest = v
    for _ in range(3):
        part = lax.reduce_precision(rest, 8, 7)
        rows.append(part.astype(BF))
        rest = rest - part
    return jnp.pad(jnp.stack(rows), ((0, 13), (0, width - v.shape[0])))


def joined(rows, size):
    return jnp.sum(rows[:3, :size].astype(F32), axis=0)


def flip(v, bit):
    return lax.ppermute(v, "row", [(i, i ^ bit) for i in range(4)])


class Gather:
    def __init__(self, x, small=None):
        self.count = lax.axis_size("row")
        self.x, self.small, self.size = x, small, x.shape[0]
        self.sent = x
        if self.count == 4 and small is not None:
            self.sent = jnp.concatenate([x, split(small, x.shape[1])], axis=0)

    def first(self):
        self.got = self.cross = (self.sent,)
        if self.count == 4:
            self.got = (flip(self.sent, 1), flip(self.sent, 2))

    def second(self, *before):
        self.cross = self.passing = self.got
        if self.count == 4:
            from_x, from_y = tie(self.got, *before)
            self.passing = tie((from_y[: self.size // 2], from_x[self.size // 2 :]))
            self.cross = (flip(self.passing[0], 1), flip(self.passing[1], 2))

    def last(self, *before):
        count, x, small, size = self.count, self.x, self.small, self.size
        me = lax.axis_index("row")
        if count != 4:
            if small is not None:
                placed = jnp.zeros((count * size,), F32)
                placed = lax.dynamic_update_slice_in_dim(placed, small, me * size, 0)
                small = butterfly(placed[None, :], "row")
            return lax.all_gather(x, "row", axis=0, tiled=True), small
        from_x, from_y = self.got
        cross_a, cross_b = tie(self.cross, *before)
        out = jnp.zeros((4 * size, x.shape[1]), x.dtype)
        put = lambda o, v, bit, off: lax.dynamic_update_slice(o, v, ((me ^ bit) * size + off, 0))
        out = put(out, x, 0, 0)
        out = put(out, from_x[:size], 1, 0)
        out = put(out, from_y[:size], 2, 0)
        out = put(out, cross_a, 3, 0)
        out = put(out, cross_b[: size // 2], 3, size // 2)
        if small is not None:
            whole = jnp.zeros((1, 4 * size), F32)
            tails = (
                small,
                joined(from_x[size:], size),
                joined(from_y[size:], size),
                joined(cross_b[size // 2 :], size),
            )
            for bit, v in enumerate(tails):
                whole = lax.dynamic_update_slice(whole, v[None, :], (0, (me ^ bit) * size))
            small = whole
        return out, small


class Scatter:
    def __init__(self, left, right, small=None):
        self.count = lax.axis_size("row")
        self.small = small
        if self.count != 4:
            self.sent = (jnp.concatenate([left, right], axis=1),)
            return
        me = lax.axis_index("row")
        self.size, half = left.shape[0] // 4, left.shape[1]
        self.half = half
        self.my_y, self.my_x = me // 2, me % 2
        left = left.reshape(2, 2, self.size, half)
        right = right.reshape(2, 2, self.size, half)
        self.at_x = lambda i: lax.dynamic_index_in_dim(left, i, 1, keepdims=False)
        self.at_y = lambda i: lax.dynamic_index_in_dim(right, i, 0, keepdims=False)
        send_x = self.at_x(1 - self.my_x)
        if small is not None:
            pieces = small.reshape(2, 2, self.size)
            there = lax.dynamic_index_in_dim(pieces, 1 - self.my_x, 1, keepdims=False)
            self.here = lax.dynamic_index_in_dim(pieces, self.my_x, 1, keepdims=False)
            send_x = jnp.concatenate(
                [send_x, jnp.stack([split(there[0], half), split(there[1], half)])], axis=1
            )
        self.sent = (send_x, self.at_y(1 - self.my_y))

    def first(self):
        self.got = self.sent
        if self.count == 4:
            self.got = (flip(self.sent[0], 1), flip(self.sent[1], 2))

    def second(self, *before):
        if self.count != 4:
            self.passed = self.ended = self.sent
            return
        got_x, got_y = tie(self.got, *before)
        pick = lambda v, i: lax.dynamic_index_in_dim(v, i, 0, keepdims=False).astype(F32)
        size = self.size
        both_x = lambda i: pick(self.at_x(self.my_x), i) + pick(got_x[:, :size], i)
        both_y = lambda i: pick(self.at_y(self.my_y), i) + pick(got_y, i)
        pass_x = both_x(1 - self.my_y).astype(BF)
        if self.small is not None:
            little = lambda i: pick(self.here, i) + joined(
                lax.dynamic_index_in_dim(got_x[:, size:], i, 0, keepdims=False), size
            )
            pass_x = jnp.concatenate([pass_x, split(little(1 - self.my_y), self.half)], axis=0)
            self.little = little(self.my_y)
        self.passed = (pass_x, both_y(1 - self.my_x).astype(BF))
        self.left = both_x(self.my_y)
        self.right = both_y(self.my_x)
        self.ended = (flip(self.passed[0], 2), flip(self.passed[1], 1))

    def last(self, *before):
        if self.count != 4:
            total = lax.psum_scatter(self.passed[0], "row", scatter_dimension=0, tiled=True).astype(F32)
            little = None
            if self.small is not None:
                size = total.shape[0]
                little = butterfly(self.small, "row")[0]
                little = lax.dynamic_slice_in_dim(little, lax.axis_index("row") * size, size, 0)
            return total, little
        end_x, end_y = tie(self.ended, *before)
        size = self.size
        left = self.left + end_x[:size].astype(F32)
        right = self.right + end_y.astype(F32)
        little = None
        if self.small is not None:
            little = self.little + joined(end_x[size:], size)
        return jnp.concatenate([left, right], axis=1), little


def butterfly(v, axis):
    count = lax.axis_size(axis)
    bit = 1
    while bit < count:
        v = v + lax.ppermute(v, axis, [(i, i ^ bit) for i in range(count)])
        bit *= 2
    return v


def sum_over_row_dp(v, *before):
    if lax.axis_size("row") != 4:
        return lax.psum(butterfly(v, "row"), "dp")
    me = lax.axis_index("row")
    for bit in (1, 2):
        size = v.shape[0] // 2
        side = me // bit % 2
        away = lax.dynamic_slice_in_dim(v, (1 - side) * size, size, 0)
        keep = lax.dynamic_slice_in_dim(v, side * size, size, 0)
        v = keep + flip(away, bit)
    v = butterfly(tie(v, *before), "dp")
    for bit in (2, 1):
        other = flip(v, bit)
        first = me // bit % 2 == 0
        v = jnp.concatenate([jnp.where(first, v, other), jnp.where(first, other, v)], axis=0)
    return v


def sum_over_row(v):
    if lax.axis_size("row") != 4:
        return butterfly(v, "row")
    return v + flip(v, 1) + flip(v, 2) + flip(v, 3)


def other_col(v):
    return lax.ppermute(v, "col", [(0, 1), (1, 0)])


def dealt_rows(rows):
    half = rows[0].shape[1] // 2
    own = jnp.stack([r[:, :half] for r in rows])
    got = other_col(jnp.stack([r[:, half:] for r in rows]))
    at_start = lax.axis_index("col") == 0
    return jnp.concatenate([jnp.where(at_start, own, got), jnp.where(at_start, got, own)], axis=0)


def sent_back(dealt):
    groups = lax.axis_size("dp")
    me = lax.axis_index("dp")
    parts = []
    for hop in range(groups):
        piece = lax.dynamic_index_in_dim(dealt, (me + hop) % groups, 0, keepdims=False)
        if hop:
            piece = lax.ppermute(piece, "dp", [(i, (i + hop) % groups) for i in range(groups)])
        parts.append(piece)
    return parts


def in_given_order(parts, dest_group):
    groups = lax.axis_size("dp")
    hops = ((lax.axis_index("dp") - dest_group) % groups)[:, None, None]
    out = jnp.where(hops == 0, parts[0][None], jnp.zeros((), BF))
    for hop in range(1, groups):
        out = jnp.where(hops == hop, parts[hop][None], out)
    return out


def matmul(a, b, over_a, over_b):
    return lax.dot_general(a, b, (((over_a,), (over_b,)), ((), ())), preferred_element_type=F32)


def per_device(
    hidden, targets, lengths, dest_group, norm_gain, gate_input_weight, auxiliary_weight,
    conv_x, conv_x_bias, conv_bc, conv_bc_bias, dt_bias, a_log, d_skip, out_gain, output_weight,
):
    row_count = lax.axis_size("row")
    col_count = lax.axis_size("col")
    row_index = lax.axis_index("row")
    col_index = lax.axis_index("col")
    group_index = lax.axis_index("dp")
    seq_group, local_len, width_col = hidden.shape
    heads = gate_input_weight.shape[1]
    pair = gate_input_weight.shape[2]
    head_dim = pair // 2
    inner = heads * head_dim
    wide = heads * pair
    aux = conv_bc.shape[1]
    head_total = auxiliary_weight.shape[1] - aux
    steps = -(-heads // 16) * 16
    seq_col = seq_group // col_count
    model_width = width_col * col_count
    inner_width = inner * row_count
    all_tokens = lengths.shape[0] * local_len * row_count
    valid_count = jnp.sum(lengths).astype(F32)
    group_lengths = lax.dynamic_slice_in_dim(lengths, group_index * seq_group, seq_group, 0)
    own_lengths = lax.dynamic_slice_in_dim(group_lengths, col_index * seq_col, seq_col, 0)

    def widened(v):
        mine = lax.dynamic_slice_in_dim(v, col_index * seq_col, seq_col, 0)
        theirs = lax.dynamic_slice_in_dim(v, (1 - col_index) * seq_col, seq_col, 0)
        return jnp.concatenate([mine, other_col(theirs)], axis=2)

    u_low = widened(hidden)
    gain = jnp.concatenate([norm_gain, other_col(norm_gain)])
    u = [u_low[k].astype(F32) for k in range(seq_col)]
    inv_rms = [lax.rsqrt(jnp.mean(v * v, axis=1, keepdims=True) + EPSILON) for v in u]
    spread = lambda v: lax.all_gather(v, "row", axis=0, tiled=True)
    normed = [(v * r * gain[None, :]).astype(BF) for v, r in zip(u, inv_rms, strict=True)]
    scaled = [spread(normed[0])]
    for v in normed[1:]:
        scaled.append(spread(tie(v, scaled[-1])))
    in_own = tie(
        jnp.concatenate(
            [
                gate_input_weight.reshape(width_col, wide),
                auxiliary_weight[:, :aux],
                lax.dynamic_slice_in_dim(auxiliary_weight, aux + row_index * heads, heads, 1),
                jnp.zeros((width_col, steps - heads), BF),
            ],
            axis=1,
        )
    )
    out_own = output_weight.reshape(inner, width_col)
    in_other, out_other = other_col(in_own), other_col(out_own)

    column = lambda v: v.reshape(-1, 1)
    taps = jnp.concatenate(
        [
            conv_x.reshape(-1, inner).T,
            column(conv_x_bias),
            column(jnp.repeat(d_skip, head_dim)),
            column(out_gain),
            jnp.zeros((inner, 1), F32),
        ],
        axis=1,
    )
    bc_taps = jnp.concatenate([conv_bc.T, column(conv_bc_bias), jnp.zeros((aux, 3), F32)], axis=1)
    dt_par = jnp.pad(jnp.stack([dt_bias, a_log], axis=1), ((0, steps - heads), (0, 6)))

    targets_own = widened(targets)
    positions = row_index * local_len + jnp.arange(local_len, dtype=jnp.int32)

    zx, gated, entering, kept_rows, scatters, gathers = [], [], [], [], [], []
    result, g_result, g_rows, coef = [], [], [], []
    loss_part = jnp.zeros((), F32)

    def finish(k, *before):
        nonlocal loss_part
        summed, total_square = scatters[k].last(*before)
        gate_inv = lax.rsqrt(total_square / inner_width + EPSILON)[:, None]
        branch = summed * gate_inv
        full = u[k] + branch
        valid = (positions < own_lengths[k]).astype(F32)[:, None]
        difference = (full - targets_own[k].astype(F32)) * valid
        loss_part = loss_part + jnp.sum(difference * difference)
        grad = difference * (all_tokens / valid_count)
        result.append(full.astype(BF))
        g_result.append(grad)
        share = gate_inv[:, 0] * gate_inv[:, 0] * jnp.sum(grad * branch, axis=1) / inner_width
        placed = lax.dynamic_update_slice_in_dim(
            jnp.zeros((local_len * row_count,), F32), share, row_index * local_len, 0
        )
        sent = (grad * gate_inv).astype(BF)
        if k < seq_col - 1:
            gathers.append(Gather(sent, share))
            gathers[-1].first()
            return gathers[-1].sent
        coef.append(sum_over_row(placed[None, :]))
        g_rows.append(spread(tie(sent, *g_rows[-1:])))
        return sent

    for k in range(seq_col):
        source = scaled[k] if k == 0 else tie(scaled[k], *scatters[-1].sent)
        projected = matmul(in_own, source[:, :width_col], 0, 1) + matmul(
            in_other, source[:, width_col:], 0, 1
        )
        if k > 0:
            scatters[-1].second(projected)
            projected = tie(projected, *scatters[-1].passed)
            projected = tie(projected, finish(k - 1, projected))
        zx.append(projected)
        g, square, e, *kept = scan_forward(projected, taps, bc_taps, dt_par, heads)
        kept_rows.append(kept)
        gated.append(g)
        entering.append(e)
        left, right = (matmul(g, w, 0, 0).astype(BF) for w in (out_own, out_other))
        scatters.append(Scatter(left, right, square))
        if k > 0:
            gathers[-1].second(left, right)
            scatters[-1].sent = tie(scatters[-1].sent, *gathers[-1].passing)
        scatters[-1].first()
    out_weight = tie(jnp.concatenate(tie((out_own, out_other), *scatters[-1].sent), axis=1))
    scatters[-1].second(out_weight)
    for spread_k in gathers:
        whole, c = spread_k.last()
        g_rows.append(whole)
        coef.append(c)
    early = []
    if seq_col > 1:
        early = [matmul(out_weight, g_rows[0], 1, 1), matmul(gated[0], g_rows[0], 1, 0)]
    finish(seq_col - 1, *early)

    to_rows = lambda g: Scatter(*(matmul(g, w, 0, 1).astype(BF) for w in (in_own, in_other)))
    g_in, scatters = [], []
    sums = [0.0, 0.0, 0.0]
    w_out_part = 0.0
    for k in range(seq_col):
        final = k == seq_col - 1
        whole = g_rows[k] if k == 0 else tie(g_rows[k], g_in[-1], coef[k])
        if k == 0 and early:
            gn, w_out_part = early
        else:
            w_out_part = w_out_part + matmul(gated[k], whole, 1, 0)
            gn = matmul(out_weight, tie(whole, w_out_part) if final else whole, 1, 1)
        before = (w_out_part,)
        if k == 0:
            dealt_output = dealt_rows(result)
            output_parts = sent_back(dealt_output)
        if final:
            received = other_col(w_out_part[:, width_col:].astype(BF))
            w_out_low = (w_out_part[:, :width_col] + received.astype(F32)).astype(BF)
            w_out_sum = lax.psum(w_out_low, "dp")
            before = (w_out_low,)
        if k > 0:
            scatters.append(to_rows(tie(g_in[-1], *before)))
            scatters[-1].first()
            before = scatters[-1].sent
        gn = tie(gn, *before)
        g, gx, gbc, gdt = scan_backward(
            zx[k], kept_rows[k], entering[k], gn, coef[k], taps, bc_taps, dt_par, heads
        )
        sums = [a + b for a, b in zip(sums, (gx, gbc, gdt), strict=True)]
        if k == 0:
            g = tie(g, *output_parts)
        if k > 0:
            scatters[-1].second(g)
            g = tie(g, *scatters[-1].passed)
        g_in.append(g)

    there, left, right = late_products(scaled, g_in, in_own.T, in_other.T, wide)
    there, left, right, g_in[-1] = tie(
        (there, left, right, g_in[-1]), w_out_sum, *(v for s in scatters for v in s.ended)
    )
    scatters.append(Scatter(left, right))
    scatters[-1].first()
    g_late = g_in[:-1] + [tie(g_in[-1], *scatters[-1].sent)]
    in_low = product(
        "tt", list(zip(scaled, g_late)), TILE, added=other_col(there), columns=width_col, wide=wide
    )
    scatters[-1].second(in_low)
    w_zx = lax.psum(in_low, "dp")
    g_aux = [g[wide:] for g in g_in]
    g_aux[-1] = tie(g_aux[-1], in_low)
    aux_part = sum(matmul(scaled[i], g_aux[i], 0, 1) for i in range(seq_col))
    aux_half = aux_part[:width_col] + other_col(aux_part[width_col:])
    aux_half = jnp.concatenate(
        [
            aux_half[:, :aux],
            lax.dynamic_update_slice_in_dim(
                jnp.zeros((width_col, head_total), F32),
                aux_half[:, aux : aux + heads],
                row_index * heads,
                1,
            ),
        ],
        axis=1,
    )
    gain_part = jnp.zeros((model_width,), F32)
    g_u = []
    for k in range(seq_col):
        g_scaled, _ = scatters[k].last(*((in_low,) if k < seq_col - 1 else ()))
        gain_part = gain_part + jnp.sum(g_scaled * u[k] * inv_rms[k], axis=0)
        weighted = g_scaled * gain[None, :]
        dot = jnp.sum(weighted * u[k], axis=1, keepdims=True) / model_width
        cube = inv_rms[k] * inv_rms[k] * inv_rms[k]
        g_u.append((g_result[k] + inv_rms[k] * weighted - u[k] * (cube * dot)).astype(BF))
    hidden_parts = sent_back(tie(dealt_rows(g_u), w_zx))
    w_aux = sum_over_row_dp(aux_half)

    gx, gbc, gdt = sums
    flat = jnp.concatenate(
        [gx.reshape(-1), gdt[:, 1:3].reshape(-1), gbc.reshape(-1), loss_part[None]]
    )
    vector = jnp.concatenate([flat, gain_part[:width_col]]) + other_col(
        jnp.concatenate([flat, gain_part[width_col:]])
    )
    own_size = inner * 8 + steps * 2
    vector = jnp.concatenate([vector[:own_size], butterfly(vector[own_size:], "row")])
    vector = butterfly(vector, "dp")
    gx = vector[: inner * 8].reshape(inner, 8)
    gdt = vector[inner * 8 : own_size].reshape(steps, 2)
    shared = vector[own_size:]
    gbc = shared[: aux * 8].reshape(aux, 8)
    loss = shared[aux * 8] * 0.5 / valid_count
    gain_sum = shared[aux * 8 + 1 :]
    return (
        loss,
        in_given_order(output_parts, dest_group),
        in_given_order(hidden_parts, dest_group),
        gain_sum,
        w_zx.astype(F32).reshape(width_col, heads, pair),
        w_aux.astype(F32),
        gx[:, :4].T.reshape(4, heads, head_dim),
        gx[:, 4].reshape(heads, head_dim),
        gbc[:, :4].T,
        gbc[:, 4],
        gdt[:heads, 0],
        gdt[:heads, 1],
        gx[:, 5].reshape(heads, head_dim).sum(axis=1),
        gx[:, 6].reshape(heads, head_dim),
        w_out_sum.astype(F32).reshape(heads, head_dim, width_col),
    )


def solution(mesh):
    placed = (
        P("dp", "row", "col"),
        P("dp", "row", "col"),
        P(),
        P("dp"),
        P("col"),
        P("col", "row", None),
        P("col", None),
        P(None, "row", None),
        P("row", None),
        P(),
        P(),
        P("row"),
        P("row"),
        P("row"),
        P("row", None),
        P("row", None, "col"),
    )
    return jax.shard_map(
        per_device,
        mesh=mesh,
        in_specs=placed,
        out_specs=(
            P(),
            P("dp", "row", "col"),
            P("dp", "row", "col"),
            P("col"),
            P("col", "row", None),
            P("col", None),
            P(None, "row", None),
            P("row", None),
            P(),
            P(),
            P("row"),
            P("row"),
            P("row"),
            P("row", None),
            P("row", None, "col"),
        ),
        check_vma=False,
    )
```

```python
import functools
import jax
import jax.numpy as jnp
from jax import lax
from jax.experimental import pallas as pl
from jax.experimental.pallas import tpu as pltpu
from jax.sharding import PartitionSpec as P

BF = jnp.bfloat16
F32 = jnp.float32
SPAN = 512
PART = 128
TILE = 256
LOG2E = 1.4426950408889634
EDGE = 128
EPSILON = 1e-05


def nn(a, b):
    return lax.dot_general(a, b, (((1,), (0,)), ((), ())), preferred_element_type=F32)


def nt(a, b):
    return lax.dot_general(a, b, (((1,), (1,)), ((), ())), preferred_element_type=F32)


def tn(a, b):
    return lax.dot_general(a, b, (((0,), (0,)), ((), ())), preferred_element_type=F32)


def exact(a, b):
    return lax.dot_general(
        a, b, (((1,), (0,)), ((), ())), precision=lax.Precision.HIGHEST, preferred_element_type=F32
    )


def sigmoid(v):
    return 0.5 * jnp.tanh(0.5 * v) + 0.5


def softplus(v):
    return jnp.maximum(v, 0.0) + jnp.log1p(jnp.exp(-jnp.abs(v)))


def wide(v, span):
    return jnp.concatenate([v] * (span // v.shape[1]), axis=1)


def taps_at(taps_ref, at, span):
    return lambda k: wide(taps_ref[k, at, :], span)


def spread_taps(from_ref, to_ref):
    for k in range(to_ref.shape[0]):
        to_ref[k] = jnp.broadcast_to(from_ref[:, k : k + 1], to_ref.shape[1:])


def move_matrix(ahead):
    rows = lax.broadcasted_iota(jnp.int32, (2 * EDGE, EDGE), 0)
    cols = lax.broadcasted_iota(jnp.int32, (2 * EDGE, EDGE), 1)
    moves = [rows == (cols + k if ahead else cols + EDGE - k) for k in (1, 2, 3)]
    return jnp.concatenate([m.astype(F32).astype(BF) for m in moves], axis=1)


def moved(joined, matrix):
    size = joined.shape[0]
    parts = range(joined.shape[1] // EDGE - 1)
    low = joined.astype(BF)
    stacked = jnp.concatenate([low[:, q * EDGE : (q + 2) * EDGE] for q in parts], axis=0)
    out = nn(stacked, matrix)
    return [
        jnp.concatenate(
            [out[q * size : (q + 1) * size, k * EDGE : (k + 1) * EDGE] for q in parts], axis=1
        )
        for k in range(3)
    ]


def conv_of(before, now, tap, matrix):
    one, two, three = moved(jnp.concatenate([before, now], axis=1), matrix)
    return tap(4) + tap(3) * now + tap(2) * one + tap(1) * two + tap(0) * three


def conv_back(now, after, tap, matrix):
    one, two, three = moved(jnp.concatenate([now, after], axis=1), matrix)
    return tap(3) * now + tap(2) * one + tap(1) * two + tap(0) * three, (one, two, three)


def fold(v):
    total = v[:, :EDGE]
    for k in range(1, v.shape[1] // EDGE):
        total = total + v[:, k * EDGE : (k + 1) * EDGE]
    return total


def lanes(q):
    return slice(q * PART, (q + 1) * PART)


def span_common(bc_before, bc_now, dt_raw, bc_tap, dt_par, matrix):
    pre = conv_of(bc_before, bc_now, bc_tap, matrix)
    sig = sigmoid(pre)
    act = pre * sig
    half = act.shape[0] // 2
    b_t = act[:half].astype(BF)
    c_t = act[half:].astype(BF)
    parts = range(bc_now.shape[1] // PART)
    rows = lax.broadcasted_iota(jnp.int32, (PART, PART), 0)
    cols = lax.broadcasted_iota(jnp.int32, (PART, PART), 1)
    causal = rows <= cols
    steps = softplus(dt_raw + dt_par[:, 0:1])
    rate = -jnp.exp(dt_par[:, 1:2])
    gone = steps * (rate * LOG2E)
    decay = [exact(gone[:, lanes(q)], causal.astype(F32)) for q in parts]
    last = [d[:, PART - 1 :] for d in decay]
    decay_n = [d.T for d in decay]
    left = jnp.concatenate([jnp.exp2(e - d) for e, d in zip(last, decay)], axis=1)
    kept = [jnp.exp2(e) for e in last]
    decay = jnp.concatenate(decay, axis=1)
    grown = jnp.exp2(decay)
    b_n = [b_t[:, lanes(q)].astype(F32).T.astype(BF) for q in parts]
    scores = [jnp.where(causal, nn(b_n[q], c_t[:, lanes(q)]), 0.0) for q in parts]
    return pre, sig, b_t, c_t, b_n, scores, causal, steps, rate, decay, decay_n, grown, left, kept


def forward_kernel(
    heads, zx_ref, bc_ref, dt_ref, taps_ref, bc_taps_ref, dt_par_ref,
    gated_ref, square_ref, enter_ref, x_ref, slope_ref, y_ref,
    state, x_tail, bc_tail, carry, xd_all, tailed, scores_all, x_taps, bc_taps, matrix_ref,
):
    span = zx_ref.shape[1]
    inner = state.shape[0]
    size = inner // heads
    parts = range(span // PART)

    @pl.when(pl.program_id(0) == 0)
    def _():
        state[...] = jnp.zeros_like(state)
        x_tail[...] = jnp.zeros_like(x_tail)
        bc_tail[...] = jnp.zeros_like(bc_tail)
        spread_taps(taps_ref, x_taps)
        spread_taps(bc_taps_ref, bc_taps)
        matrix_ref[...] = move_matrix(False)

    matrix = matrix_ref[...]
    bc_now = bc_ref[...]
    _, _, _, c_t, b_n, scores, _, steps, _, decay, decay_n, grown, left, kept = span_common(
        bc_tail[...], bc_now, dt_ref[...], taps_at(bc_taps, slice(None), span), dt_par_ref[...], matrix
    )
    bc_tail[...] = bc_now[:, span - EDGE :]
    for q in parts:
        scores_all[q] = scores[q]
    for h in range(heads):
        at = slice(h * size, (h + 1) * size)
        x_raw = zx_ref[(2 * h + 1) * size : (2 * h + 2) * size, :]
        pre = conv_of(x_tail[at, :], x_raw, taps_at(x_taps, at, span), matrix)
        x_tail[at, :] = x_raw[:, span - EDGE :]
        sig = sigmoid(pre)
        x = pre * sig
        xd = x * steps[h : h + 1, :]
        x_ref[at, :] = x
        slope_ref[at, :] = sig + x * (1.0 - sig)
        xd_all[at, :] = xd.astype(BF)
        tailed[at, :] = (xd * left[h : h + 1, :]).astype(BF)
    for q in parts:
        entering = state[...].astype(BF)
        enter_ref[q * inner : (q + 1) * inner, :] = entering
        carry[:, lanes(q)] = nn(entering, c_t[:, lanes(q)])
        more = nn(tailed[:, lanes(q)], b_n[q])
        for h in range(heads):
            at = slice(h * size, (h + 1) * size)
            state[at, :] = state[at, :] * kept[q][h : h + 1, :] + more[at, :]
    square = jnp.zeros((size, span), F32)
    for h in range(heads):
        at = slice(h * size, (h + 1) * size)
        z = zx_ref[2 * h * size : (2 * h + 1) * size, :]
        tap = taps_at(x_taps, at, span)
        mixed = []
        for q in parts:
            gap = decay[h : h + 1, lanes(q)] - decay_n[q][:, h : h + 1]
            mixing = scores_all[q] * jnp.exp2(jnp.minimum(gap, 0.0))
            mixed.append(nn(xd_all[at, lanes(q)], mixing.astype(BF)))
        y = jnp.concatenate(mixed, axis=1) + carry[at, :] * grown[h : h + 1, :]
        y_ref[at, :] = y
        y = y + tap(5) * x_ref[at, :]
        gated = y * (z * sigmoid(z))
        square = square + gated * gated
        gated_ref[at, :] = (gated * tap(6)).astype(BF)
    square_ref[...] = jnp.sum(square, axis=0, keepdims=True)


def backward_kernel(
    heads, zx_ref, x_ref, slope_ref, y_ref, bc_ref, bc_before_ref, dt_ref, enter_ref, gn_ref, coef_ref,
    taps_ref, bc_taps_ref, dt_par_ref,
    gzx_ref, gx_sum_ref, gbc_sum_ref, gdt_sum_ref,
    dstate, x_head, bc_head, from_state, grown_g, tailed, x_acc, bc_acc, dt_acc, rsum, dsum,
    dxd_all, gy_all, scores_all, dscores_all, held_all, x_taps, bc_taps_all, matrix_ref,
    back_matrix_ref,
):
    span = zx_ref.shape[1]
    inner = dstate.shape[0]
    size = inner // heads
    half = bc_ref.shape[0] // 2
    wide = zx_ref.shape[0]
    parts = range(span // PART)
    step = pl.program_id(0)
    count = pl.num_programs(0)
    first = step == count - 1

    @pl.when(step == 0)
    def _():
        dstate[...] = jnp.zeros_like(dstate)
        x_head[...] = jnp.zeros_like(x_head)
        bc_head[...] = jnp.zeros_like(bc_head)
        x_acc[...] = jnp.zeros_like(x_acc)
        bc_acc[...] = jnp.zeros_like(bc_acc)
        dt_acc[...] = jnp.zeros_like(dt_acc)
        rsum[...] = jnp.zeros_like(rsum)
        dsum[...] = jnp.zeros_like(dsum)
        held_all[...] = jnp.zeros_like(held_all)
        spread_taps(taps_ref, x_taps)
        spread_taps(bc_taps_ref, bc_taps_all)
        matrix_ref[...] = move_matrix(False)
        back_matrix_ref[...] = move_matrix(True)

    matrix, back_matrix = matrix_ref[...], back_matrix_ref[...]
    live = jnp.where(first, 0.0, 1.0)
    bc_tap = taps_at(bc_taps_all, slice(None), span)
    dt_raw = dt_ref[...]
    bc_now = bc_ref[...]
    (
        bc_pre, bc_sig, b_t, c_t, b_n, scores, causal, steps, rate, decay, decay_n, grown, left, kept
    ) = span_common(bc_before_ref[...] * live, bc_now, dt_raw, bc_tap, dt_par_ref[...], matrix)
    for q in parts:
        scores_all[q] = scores[q]
        dscores_all[q] = jnp.zeros((PART, PART), F32)
    coef = coef_ref[...]
    for h in range(heads):
        at = slice(h * size, (h + 1) * size)
        z = zx_ref[2 * h * size : (2 * h + 1) * size, :]
        tap = taps_at(x_taps, at, span)
        x = x_ref[at, :]
        xd = x * steps[h : h + 1, :]
        xd_low = xd.astype(BF)
        tailed[at, :] = (xd * left[h : h + 1, :]).astype(BF)
        ratios, mixings = [], []
        for q in parts:
            gap = decay[h : h + 1, lanes(q)] - decay_n[q][:, h : h + 1]
            ratios.append(jnp.exp2(jnp.minimum(gap, 0.0)))
            mixings.append((scores_all[q] * ratios[q]).astype(BF))
        grown_h = grown[h : h + 1, :]
        y_scan = y_ref[at, :]
        y = y_scan + tap(5) * x
        zsig = sigmoid(z)
        silu_z = z * zsig
        gated = y * silu_z
        gn = gn_ref[at, :].astype(F32)
        g_gated = tap(6) * gn - gated * coef
        gy = g_gated * silu_z
        gzx_ref[2 * h * size : (2 * h + 1) * size, :] = (
            g_gated * y * (zsig + silu_z * (1.0 - zsig))
        ).astype(BF)
        gy_low = gy.astype(BF)
        gy_all[at, :] = gy_low
        grown_g[at, :] = (gy * grown_h).astype(BF)
        rsum[h : h + 1, :] = jnp.sum(gy_low.astype(F32) * y_scan, axis=0, keepdims=True)
        x_acc[5, at, :] = x_acc[5, at, :] + fold(gy * x)
        x_acc[6, at, :] = x_acc[6, at, :] + fold(gn * gated)
        for q in parts:
            dxd_all[at, lanes(q)] = nt(gy_low[:, lanes(q)], mixings[q])
            dscores_all[q] = dscores_all[q] + tn(xd_low[:, lanes(q)], gy_low[:, lanes(q)]) * ratios[q]
    db, dc, flows = [], [], []
    for q in reversed(parts):
        entering = enter_ref[q * inner : (q + 1) * inner, :]
        leaving = dstate[...].astype(BF)
        from_state[:, lanes(q)] = nn(leaving, b_t[:, lanes(q)])
        low = jnp.where(causal, dscores_all[q], 0.0).astype(BF)
        dc.insert(0, nn(b_t[:, lanes(q)], low) + tn(entering, grown_g[:, lanes(q)]))
        db.insert(0, nt(c_t[:, lanes(q)], low) + tn(leaving, tailed[:, lanes(q)]))
        more = nt(grown_g[:, lanes(q)], c_t[:, lanes(q)])
        for h in range(heads):
            at = slice(h * size, (h + 1) * size)
            passed = dstate[at, :] * kept[q][h : h + 1, :]
            held_all[q, h : h + 1, :] = jnp.sum(passed * entering[at, :].astype(F32), axis=0, keepdims=True)
            dstate[at, :] = passed + more[at, :]
    for h in range(heads):
        at = slice(h * size, (h + 1) * size)
        x_raw = zx_ref[(2 * h + 1) * size : (2 * h + 2) * size, :]
        tap = taps_at(x_taps, at, span)
        x = x_ref[at, :]
        steps_h = steps[h : h + 1, :]
        dx_state = from_state[at, :] * left[h : h + 1, :]
        dxd = dxd_all[at, :] + dx_state
        xd_wide = (x * steps_h).astype(BF).astype(F32)
        rsum[h : h + 1, :] = rsum[h : h + 1, :] - jnp.sum(xd_wide * dxd, axis=0, keepdims=True)
        dsum[h : h + 1, :] = jnp.sum(x * dxd, axis=0, keepdims=True)
        held = jnp.sum(xd_wide * dx_state, axis=0, keepdims=True)
        for q in parts:
            held_all[q, h : h + 1, :] = held_all[q, h : h + 1, :] + held[:, lanes(q)]
        dx = dxd * steps_h + tap(5) * gy_all[at, :].astype(F32)
        gpre = dx * slope_ref[at, :]
        g_raw, later = conv_back(gpre, x_head[at, :], tap, back_matrix)
        x_head[at, :] = gpre[:, :EDGE]
        gzx_ref[(2 * h + 1) * size : (2 * h + 2) * size, :] = g_raw.astype(BF)
        for k, moved_g in enumerate((gpre, *later)):
            x_acc[3 - k, at, :] = x_acc[3 - k, at, :] + fold(moved_g * x_raw)
        x_acc[4, at, :] = x_acc[4, at, :] + fold(gpre)
    gbc = jnp.concatenate([jnp.concatenate(db, axis=1), jnp.concatenate(dc, axis=1)], axis=0)
    gbc = gbc * (bc_sig + bc_pre * bc_sig * (1.0 - bc_sig))
    g_raw, later = conv_back(gbc, bc_head[...], bc_tap, back_matrix)
    bc_head[...] = gbc[:, :EDGE]
    gzx_ref[wide : wide + 2 * half, :] = g_raw.astype(BF)
    for k, moved_g in enumerate((gbc, *later)):
        bc_acc[3 - k] = bc_acc[3 - k] + fold(moved_g * bc_now)
    bc_acc[4] = bc_acc[4] + fold(gbc)
    after = jnp.logical_or(
        jnp.logical_not(causal),
        lax.broadcasted_iota(jnp.int32, (PART, PART), 0) == lax.broadcasted_iota(jnp.int32, (PART, PART), 1),
    ).astype(F32)
    da = jnp.concatenate(
        [
            exact(rsum[:, lanes(q)], after) + jnp.sum(held_all[q], axis=1, keepdims=True)
            for q in parts
        ],
        axis=1,
    )
    g_steps = dsum[...] + rate * da
    g_dt = g_steps * sigmoid(dt_raw + dt_par_ref[:, 0:1])
    gzx_ref[wide + 2 * half :, :] = g_dt.astype(BF)
    dt_acc[:, 1:2] = dt_acc[:, 1:2] + jnp.sum(g_dt, axis=1, keepdims=True)
    dt_acc[:, 2:3] = dt_acc[:, 2:3] + jnp.sum(da * steps * rate, axis=1, keepdims=True)

    @pl.when(first)
    def _():
        for k in range(7):
            gx_sum_ref[:, k : k + 1] = jnp.sum(x_acc[k], axis=1, keepdims=True)
        for k in range(5):
            gbc_sum_ref[:, k : k + 1] = jnp.sum(bc_acc[k], axis=1, keepdims=True)
        gdt_sum_ref[...] = dt_acc[...]


def scan_forward(zx, taps, bc_taps, dt_par, heads, span=SPAN):
    inner = taps.shape[0]
    length = zx.shape[1]
    aux = bc_taps.shape[0]
    steps = dt_par.shape[0]
    states = aux // 2
    body = functools.partial(forward_kernel, heads)
    whole = lambda r, c: pl.BlockSpec((r, c), lambda i: (0, 0))
    return pl.pallas_call(
        body,
        grid=(length // span,),
        in_specs=[
            pl.BlockSpec((2 * inner, span), lambda i: (0, i)),
            pl.BlockSpec((aux, span), lambda i: (2 * inner // aux, i)),
            pl.BlockSpec((steps, span), lambda i: ((2 * inner + aux) // steps, i)),
            whole(inner, 8), whole(aux, 8), whole(steps, 8),
        ],
        out_specs=[
            pl.BlockSpec((inner, span), lambda i: (0, i)),
            pl.BlockSpec((1, span), lambda i: (0, i)),
            pl.BlockSpec((span // PART * inner, states), lambda i: (i, 0)),
        ]
        + [pl.BlockSpec((inner, span), lambda i: (0, i))] * 3,
        out_shape=[
            jax.ShapeDtypeStruct((inner, length), BF),
            jax.ShapeDtypeStruct((1, length), F32),
            jax.ShapeDtypeStruct((length // PART * inner, states), BF),
        ]
        + [jax.ShapeDtypeStruct((inner, length), F32)] * 3,
        scratch_shapes=[
            pltpu.VMEM((inner, states), F32),
            pltpu.VMEM((inner, EDGE), F32),
            pltpu.VMEM((aux, EDGE), F32),
            pltpu.VMEM((inner, span), F32),
            pltpu.VMEM((inner, span), BF),
            pltpu.VMEM((inner, span), BF),
            pltpu.VMEM((span // PART, PART, PART), F32),
            pltpu.VMEM((7, inner, EDGE), F32),
            pltpu.VMEM((5, aux, EDGE), F32),
            pltpu.VMEM((2 * EDGE, 3 * EDGE), BF),
        ],
        compiler_params=pltpu.CompilerParams(vmem_limit_bytes=56 * 2**20),
        name="scan_forward",
    )(zx, zx, zx, taps, bc_taps, dt_par)


def scan_backward(zx, kept, entering, gn, coef, taps, bc_taps, dt_par, heads, span=SPAN):
    inner = taps.shape[0]
    length = zx.shape[1]
    aux = bc_taps.shape[0]
    steps = dt_par.shape[0]
    states = aux // 2
    count = length // span
    ratio = span // EDGE
    body = functools.partial(backward_kernel, heads)
    whole = lambda r, c: pl.BlockSpec((r, c), lambda i: (0, 0))
    rev = lambda i: count - 1 - i
    before = lambda i: jnp.maximum((count - 1 - i) * ratio - 1, 0)
    return pl.pallas_call(
        body,
        grid=(count,),
        in_specs=[
            pl.BlockSpec((2 * inner, span), lambda i: (0, rev(i))),
            pl.BlockSpec((inner, span), lambda i: (0, rev(i))),
            pl.BlockSpec((inner, span), lambda i: (0, rev(i))),
            pl.BlockSpec((inner, span), lambda i: (0, rev(i))),
            pl.BlockSpec((aux, span), lambda i: (2 * inner // aux, rev(i))),
            pl.BlockSpec((aux, EDGE), lambda i: (2 * inner // aux, before(i))),
            pl.BlockSpec((steps, span), lambda i: ((2 * inner + aux) // steps, rev(i))),
            pl.BlockSpec((span // PART * inner, states), lambda i: (rev(i), 0)),
            pl.BlockSpec((inner, span), lambda i: (0, rev(i))),
            pl.BlockSpec((1, span), lambda i: (0, rev(i))),
            whole(inner, 8), whole(aux, 8), whole(steps, 8),
        ],
        out_specs=[
            pl.BlockSpec((2 * inner + aux + steps, span), lambda i: (0, rev(i))),
            whole(inner, 8), whole(aux, 8), whole(steps, EDGE),
        ],
        out_shape=[
            jax.ShapeDtypeStruct((2 * inner + aux + steps, length), BF),
            jax.ShapeDtypeStruct((inner, 8), F32),
            jax.ShapeDtypeStruct((aux, 8), F32),
            jax.ShapeDtypeStruct((steps, EDGE), F32),
        ],
        scratch_shapes=[
            pltpu.VMEM((inner, states), F32),
            pltpu.VMEM((inner, EDGE), F32),
            pltpu.VMEM((aux, EDGE), F32),
            pltpu.VMEM((inner, span), F32),
            pltpu.VMEM((inner, span), BF),
            pltpu.VMEM((inner, span), BF),
            pltpu.VMEM((7, inner, EDGE), F32),
            pltpu.VMEM((5, aux, EDGE), F32),
            pltpu.VMEM((steps, EDGE), F32),
            pltpu.VMEM((steps, span), F32),
            pltpu.VMEM((steps, span), F32),
            pltpu.VMEM((inner, span), F32),
            pltpu.VMEM((inner, span), BF),
            pltpu.VMEM((span // PART, PART, PART), F32),
            pltpu.VMEM((span // PART, PART, PART), F32),
            pltpu.VMEM((span // PART, steps, PART), F32),
            pltpu.VMEM((7, inner, EDGE), F32),
            pltpu.VMEM((5, aux, EDGE), F32),
            pltpu.VMEM((2 * EDGE, 3 * EDGE), BF),
            pltpu.VMEM((2 * EDGE, 3 * EDGE), BF),
        ],
        compiler_params=pltpu.CompilerParams(vmem_limit_bytes=56 * 2**20),
        name="scan_backward",
    )(zx, *kept, zx, zx, zx, entering, gn, coef, taps, bc_taps, dt_par)


def product_kernel(form, count, added, *refs):
    out_ref = refs[-1]
    total = refs[2 * count][...].astype(F32) if added else None
    for i in range(count):
        a, b = refs[2 * i][...], refs[2 * i + 1][...]
        if form == "tt":
            a = a.T
        over = 0 if form == "nn" else 1
        term = lax.dot_general(a, b, (((1,), (over,)), ((), ())), preferred_element_type=F32)
        total = term if total is None else total + term
    out_ref[...] = total.astype(out_ref.dtype)


def product(form, pairs, tile, added=None, dtype=BF, start=0, columns=None, wide=None):
    first, other = pairs[0]
    rows = columns or first.shape[1 if form == "tt" else 0]
    cols = wide or other.shape[1 if form == "nn" else 0]
    operands, specs = [], []
    for a, b in pairs:
        operands += [a, b]
        if form == "tt":
            specs.append(pl.BlockSpec((a.shape[0], tile), lambda i: (0, start // tile + i)))
        else:
            specs.append(pl.BlockSpec((tile, a.shape[1]), lambda i: (i, 0)))
        block = b.shape if form == "nn" else (cols, b.shape[1])
        specs.append(pl.BlockSpec(block, lambda i: (0, 0), pipeline_mode=pl.Buffered(1)))
    if added is not None:
        operands.append(added)
        specs.append(pl.BlockSpec((tile, cols), lambda i: (i, 0)))
    return pl.pallas_call(
        functools.partial(product_kernel, form, len(pairs), added is not None),
        grid=(rows // tile,),
        in_specs=specs,
        out_specs=pl.BlockSpec((tile, cols), lambda i: (i, 0)),
        out_shape=jax.ShapeDtypeStruct((rows, cols), dtype),
        compiler_params=pltpu.CompilerParams(vmem_limit_bytes=56 * 2**20),
        name="product_" + form,
    )(*operands)


def late_kernel(count, wide, first, *refs):
    scaled, g_all, g_tile = refs[:count], refs[count : 2 * count], refs[2 * count]
    weights, outs = refs[2 * count + 1 : 2 * count + 3], refs[2 * count + 3 : 2 * count + 6]
    held, sems = refs[2 * count + 6 : 2 * count + 8], refs[2 * count + 8]
    step = pl.program_id(0)
    copies = [pltpu.make_async_copy(weights[k], held[k], sems.at[k]) for k in range(2)]

    @pl.when(step == 0)
    def _():
        for copy in copies:
            copy.start()

    @pl.when(step < first)
    def _():
        total = None
        for s, g in zip(scaled, g_all):
            term = nt(s[...].T, g[:wide, :])
            total = term if total is None else total + term
        outs[0][...] = total.astype(BF)

    @pl.when(step == first)
    def _():
        for copy in copies:
            copy.wait()

    @pl.when(step >= first)
    def _():
        rows = g_tile[...].T
        for k in range(2):
            outs[1 + k][...] = nn(rows, held[k][...]).astype(BF)


def late_products(scaled, g_in, own, other, wide):
    depth, width = own.shape
    length = scaled[0].shape[0]
    first = width // TILE
    count = len(scaled)
    at = lambda i: jnp.maximum(i - first, 0)
    until = lambda i: jnp.minimum(i, first - 1)
    return pl.pallas_call(
        functools.partial(late_kernel, count, wide, first),
        grid=(first + length // TILE,),
        in_specs=[pl.BlockSpec((length, TILE), lambda i: (0, first + until(i))) for _ in scaled]
        + [pl.BlockSpec(g.shape, lambda i: (0, 0), pipeline_mode=pl.Buffered(1)) for g in g_in]
        + [pl.BlockSpec((depth, TILE), lambda i: (0, at(i)))]
        + [pl.BlockSpec(memory_space=pl.ANY)] * 2,
        out_specs=[
            pl.BlockSpec((TILE, wide), lambda i: (until(i), 0)),
            pl.BlockSpec((TILE, width), lambda i: (at(i), 0)),
            pl.BlockSpec((TILE, width), lambda i: (at(i), 0)),
        ],
        out_shape=[
            jax.ShapeDtypeStruct((width, wide), BF),
            jax.ShapeDtypeStruct((length, width), BF),
            jax.ShapeDtypeStruct((length, width), BF),
        ],
        scratch_shapes=[
            pltpu.VMEM(own.shape, BF),
            pltpu.VMEM(own.shape, BF),
            pltpu.SemaphoreType.DMA((2,)),
        ],
        compiler_params=pltpu.CompilerParams(vmem_limit_bytes=56 * 2**20),
        name="late_products",
    )(*scaled, *g_in, g_in[-1], own, other)


def tie(value, *before):
    return lax.optimization_barrier((value, *before))[0]


def split(v, width):
    rows = []
    rest = v
    for _ in range(3):
        part = lax.reduce_precision(rest, 8, 7)
        rows.append(part.astype(BF))
        rest = rest - part
    return jnp.pad(jnp.stack(rows), ((0, 13), (0, width - v.shape[0])))


def joined(rows, size):
    return jnp.sum(rows[:3, :size].astype(F32), axis=0)


def flip(v, bit):
    return lax.ppermute(v, "row", [(i, i ^ bit) for i in range(4)])


class Gather:
    def __init__(self, x, small=None):
        self.count = lax.axis_size("row")
        self.x, self.small, self.size = x, small, x.shape[0]
        self.sent = x
        if self.count == 4 and small is not None:
            self.sent = jnp.concatenate([x, split(small, x.shape[1])], axis=0)

    def first(self):
        self.got = self.cross = (self.sent,)
        if self.count == 4:
            self.got = (flip(self.sent, 1), flip(self.sent, 2))

    def second(self, *before):
        self.cross = self.passing = self.got
        if self.count == 4:
            from_x, from_y = tie(self.got, *before)
            self.passing = tie((from_y[: self.size // 2], from_x[self.size // 2 :]))
            self.cross = (flip(self.passing[0], 1), flip(self.passing[1], 2))

    def last(self, *before):
        count, x, small, size = self.count, self.x, self.small, self.size
        me = lax.axis_index("row")
        if count != 4:
            if small is not None:
                placed = jnp.zeros((count * size,), F32)
                placed = lax.dynamic_update_slice_in_dim(placed, small, me * size, 0)
                small = butterfly(placed[None, :], "row")
            return lax.all_gather(x, "row", axis=0, tiled=True), small
        from_x, from_y = self.got
        cross_a, cross_b = tie(self.cross, *before)
        out = jnp.zeros((4 * size, x.shape[1]), x.dtype)
        put = lambda o, v, bit, off: lax.dynamic_update_slice(o, v, ((me ^ bit) * size + off, 0))
        out = put(out, x, 0, 0)
        out = put(out, from_x[:size], 1, 0)
        out = put(out, from_y[:size], 2, 0)
        out = put(out, cross_a, 3, 0)
        out = put(out, cross_b[: size // 2], 3, size // 2)
        if small is not None:
            whole = jnp.zeros((1, 4 * size), F32)
            tails = (
                small,
                joined(from_x[size:], size),
                joined(from_y[size:], size),
                joined(cross_b[size // 2 :], size),
            )
            for bit, v in enumerate(tails):
                whole = lax.dynamic_update_slice(whole, v[None, :], (0, (me ^ bit) * size))
            small = whole
        return out, small


class Scatter:
    def __init__(self, left, right, small=None):
        self.count = lax.axis_size("row")
        self.small = small
        if self.count != 4:
            self.sent = (jnp.concatenate([left, right], axis=1),)
            return
        me = lax.axis_index("row")
        self.size, half = left.shape[0] // 4, left.shape[1]
        self.half = half
        self.my_y, self.my_x = me // 2, me % 2
        left = left.reshape(2, 2, self.size, half)
        right = right.reshape(2, 2, self.size, half)
        self.at_x = lambda i: lax.dynamic_index_in_dim(left, i, 1, keepdims=False)
        self.at_y = lambda i: lax.dynamic_index_in_dim(right, i, 0, keepdims=False)
        send_x = self.at_x(1 - self.my_x)
        if small is not None:
            pieces = small.reshape(2, 2, self.size)
            there = lax.dynamic_index_in_dim(pieces, 1 - self.my_x, 1, keepdims=False)
            self.here = lax.dynamic_index_in_dim(pieces, self.my_x, 1, keepdims=False)
            send_x = jnp.concatenate(
                [send_x, jnp.stack([split(there[0], half), split(there[1], half)])], axis=1
            )
        self.sent = (send_x, self.at_y(1 - self.my_y))

    def first(self):
        self.got = self.sent
        if self.count == 4:
            self.got = (flip(self.sent[0], 1), flip(self.sent[1], 2))

    def second(self, *before):
        if self.count != 4:
            self.passed = self.ended = self.sent
            return
        got_x, got_y = tie(self.got, *before)
        pick = lambda v, i: lax.dynamic_index_in_dim(v, i, 0, keepdims=False).astype(F32)
        size = self.size
        both_x = lambda i: pick(self.at_x(self.my_x), i) + pick(got_x[:, :size], i)
        both_y = lambda i: pick(self.at_y(self.my_y), i) + pick(got_y, i)
        pass_x = both_x(1 - self.my_y).astype(BF)
        if self.small is not None:
            little = lambda i: pick(self.here, i) + joined(
                lax.dynamic_index_in_dim(got_x[:, size:], i, 0, keepdims=False), size
            )
            pass_x = jnp.concatenate([pass_x, split(little(1 - self.my_y), self.half)], axis=0)
            self.little = little(self.my_y)
        self.passed = (pass_x, both_y(1 - self.my_x).astype(BF))
        self.left = both_x(self.my_y)
        self.right = both_y(self.my_x)
        self.ended = (flip(self.passed[0], 2), flip(self.passed[1], 1))

    def last(self, *before):
        if self.count != 4:
            total = lax.psum_scatter(self.passed[0], "row", scatter_dimension=0, tiled=True).astype(F32)
            little = None
            if self.small is not None:
                size = total.shape[0]
                little = butterfly(self.small, "row")[0]
                little = lax.dynamic_slice_in_dim(little, lax.axis_index("row") * size, size, 0)
            return total, little
        end_x, end_y = tie(self.ended, *before)
        size = self.size
        left = self.left + end_x[:size].astype(F32)
        right = self.right + end_y.astype(F32)
        little = None
        if self.small is not None:
            little = self.little + joined(end_x[size:], size)
        return jnp.concatenate([left, right], axis=1), little


def butterfly(v, axis):
    count = lax.axis_size(axis)
    bit = 1
    while bit < count:
        v = v + lax.ppermute(v, axis, [(i, i ^ bit) for i in range(count)])
        bit *= 2
    return v


def sum_over_row_dp(v, *before):
    if lax.axis_size("row") != 4:
        return lax.psum(butterfly(v, "row"), "dp")
    me = lax.axis_index("row")
    for bit in (1, 2):
        size = v.shape[0] // 2
        side = me // bit % 2
        away = lax.dynamic_slice_in_dim(v, (1 - side) * size, size, 0)
        keep = lax.dynamic_slice_in_dim(v, side * size, size, 0)
        v = keep + flip(away, bit)
    v = butterfly(tie(v, *before), "dp")
    for bit in (2, 1):
        other = flip(v, bit)
        first = me // bit % 2 == 0
        v = jnp.concatenate([jnp.where(first, v, other), jnp.where(first, other, v)], axis=0)
    return v


def sum_over_row(v):
    if lax.axis_size("row") != 4:
        return butterfly(v, "row")
    return v + flip(v, 1) + flip(v, 2) + flip(v, 3)


def other_col(v):
    return lax.ppermute(v, "col", [(0, 1), (1, 0)])


def dealt_rows(rows):
    half = rows[0].shape[1] // 2
    own = jnp.stack([r[:, :half] for r in rows])
    got = other_col(jnp.stack([r[:, half:] for r in rows]))
    at_start = lax.axis_index("col") == 0
    return jnp.concatenate([jnp.where(at_start, own, got), jnp.where(at_start, got, own)], axis=0)


def sent_back(dealt):
    groups = lax.axis_size("dp")
    me = lax.axis_index("dp")
    parts = []
    for hop in range(groups):
        piece = lax.dynamic_index_in_dim(dealt, (me + hop) % groups, 0, keepdims=False)
        if hop:
            piece = lax.ppermute(piece, "dp", [(i, (i + hop) % groups) for i in range(groups)])
        parts.append(piece)
    return parts


def in_given_order(parts, dest_group):
    groups = lax.axis_size("dp")
    hops = ((lax.axis_index("dp") - dest_group) % groups)[:, None, None]
    out = jnp.where(hops == 0, parts[0][None], jnp.zeros((), BF))
    for hop in range(1, groups):
        out = jnp.where(hops == hop, parts[hop][None], out)
    return out


def matmul(a, b, over_a, over_b):
    return lax.dot_general(a, b, (((over_a,), (over_b,)), ((), ())), preferred_element_type=F32)


def per_device(
    hidden, targets, lengths, dest_group, norm_gain, gate_input_weight, auxiliary_weight,
    conv_x, conv_x_bias, conv_bc, conv_bc_bias, dt_bias, a_log, d_skip, out_gain, output_weight,
):
    row_count = lax.axis_size("row")
    col_count = lax.axis_size("col")
    row_index = lax.axis_index("row")
    col_index = lax.axis_index("col")
    group_index = lax.axis_index("dp")
    seq_group, local_len, width_col = hidden.shape
    heads = gate_input_weight.shape[1]
    pair = gate_input_weight.shape[2]
    head_dim = pair // 2
    inner = heads * head_dim
    wide = heads * pair
    aux = conv_bc.shape[1]
    head_total = auxiliary_weight.shape[1] - aux
    steps = -(-heads // 16) * 16
    seq_col = seq_group // col_count
    model_width = width_col * col_count
    inner_width = inner * row_count
    all_tokens = lengths.shape[0] * local_len * row_count
    valid_count = jnp.sum(lengths).astype(F32)
    group_lengths = lax.dynamic_slice_in_dim(lengths, group_index * seq_group, seq_group, 0)
    own_lengths = lax.dynamic_slice_in_dim(group_lengths, col_index * seq_col, seq_col, 0)

    def widened(v):
        mine = lax.dynamic_slice_in_dim(v, col_index * seq_col, seq_col, 0)
        theirs = lax.dynamic_slice_in_dim(v, (1 - col_index) * seq_col, seq_col, 0)
        return jnp.concatenate([mine, other_col(theirs)], axis=2)

    u_low = widened(hidden)
    gain = jnp.concatenate([norm_gain, other_col(norm_gain)])
    u = [u_low[k].astype(F32) for k in range(seq_col)]
    inv_rms = [lax.rsqrt(jnp.mean(v * v, axis=1, keepdims=True) + EPSILON) for v in u]
    spread = lambda v: lax.all_gather(v, "row", axis=0, tiled=True)
    normed = [(v * r * gain[None, :]).astype(BF) for v, r in zip(u, inv_rms, strict=True)]
    scaled = [spread(normed[0])]
    for v in normed[1:]:
        scaled.append(spread(tie(v, scaled[-1])))
    in_own = tie(
        jnp.concatenate(
            [
                gate_input_weight.reshape(width_col, wide),
                auxiliary_weight[:, :aux],
                lax.dynamic_slice_in_dim(auxiliary_weight, aux + row_index * heads, heads, 1),
                jnp.zeros((width_col, steps - heads), BF),
            ],
            axis=1,
        )
    )
    out_own = output_weight.reshape(inner, width_col)
    column = lambda v: v.reshape(-1, 1)
    taps = jnp.concatenate(
        [
            conv_x.reshape(-1, inner).T,
            column(conv_x_bias),
            column(jnp.repeat(d_skip, head_dim)),
            column(out_gain),
            jnp.zeros((inner, 1), F32),
        ],
        axis=1,
    )
    bc_taps = jnp.concatenate([conv_bc.T, column(conv_bc_bias), jnp.zeros((aux, 3), F32)], axis=1)
    dt_par = jnp.pad(jnp.stack([dt_bias, a_log], axis=1), ((0, steps - heads), (0, 6)))
    targets_there = lax.dynamic_slice_in_dim(targets, (1 - col_index) * seq_col, seq_col, 0)
    in_own, taps, bc_taps, dt_par, targets_there = tie(
        (in_own, taps, bc_taps, dt_par, targets_there)
    )
    in_other, out_other = other_col(in_own), other_col(out_own)

    targets_own = jnp.concatenate(
        [
            lax.dynamic_slice_in_dim(targets, col_index * seq_col, seq_col, 0),
            other_col(targets_there),
        ],
        axis=2,
    )
    positions = row_index * local_len + jnp.arange(local_len, dtype=jnp.int32)

    zx, gated, entering, kept_rows, scatters, gathers = [], [], [], [], [], []
    result, g_result, g_rows, coef = [], [], [], []
    loss_part = jnp.zeros((), F32)

    def finish(k, *before):
        nonlocal loss_part
        summed, total_square = scatters[k].last(*before)
        gate_inv = lax.rsqrt(total_square / inner_width + EPSILON)[:, None]
        branch = summed * gate_inv
        full = u[k] + branch
        valid = (positions < own_lengths[k]).astype(F32)[:, None]
        difference = (full - targets_own[k].astype(F32)) * valid
        loss_part = loss_part + jnp.sum(difference * difference)
        grad = difference * (all_tokens / valid_count)
        result.append(full.astype(BF))
        g_result.append(grad)
        share = gate_inv[:, 0] * gate_inv[:, 0] * jnp.sum(grad * branch, axis=1) / inner_width
        placed = lax.dynamic_update_slice_in_dim(
            jnp.zeros((local_len * row_count,), F32), share, row_index * local_len, 0
        )
        sent = (grad * gate_inv).astype(BF)
        if k < seq_col - 1:
            gathers.append(Gather(sent, share))
            gathers[-1].first()
            return gathers[-1].sent
        coef.append(sum_over_row(placed[None, :]))
        g_rows.append(spread(tie(sent, *g_rows[-1:])))
        return sent

    for k in range(seq_col):
        source = scaled[k] if k == 0 else tie(scaled[k], *scatters[-1].sent)
        projected = matmul(in_own, source[:, :width_col], 0, 1) + matmul(
            in_other, source[:, width_col:], 0, 1
        )
        if k > 0:
            scatters[-1].second(projected)
            projected = tie(projected, *scatters[-1].passed)
            projected = tie(projected, finish(k - 1, projected))
        zx.append(projected)
        g, square, e, *kept = scan_forward(projected, taps, bc_taps, dt_par, heads)
        kept_rows.append(kept)
        gated.append(g)
        entering.append(e)
        left, right = (matmul(g, w, 0, 0).astype(BF) for w in (out_own, out_other))
        scatters.append(Scatter(left, right, square))
        if k > 0:
            gathers[-1].second(left, right)
            scatters[-1].sent = tie(scatters[-1].sent, *gathers[-1].passing)
        scatters[-1].first()
    out_weight = tie(jnp.concatenate(tie((out_own, out_other), *scatters[-1].sent), axis=1))
    scatters[-1].second(out_weight)
    for spread_k in gathers:
        whole, c = spread_k.last()
        g_rows.append(whole)
        coef.append(c)
    early = []
    if seq_col > 1:
        early = [matmul(out_weight, g_rows[0], 1, 1), matmul(gated[0], g_rows[0], 1, 0)]
    finish(seq_col - 1, *early)

    to_rows = lambda g: Scatter(*(matmul(g, w, 0, 1).astype(BF) for w in (in_own, in_other)))
    g_in, scatters = [], []
    sums = [0.0, 0.0, 0.0]
    w_out_part = 0.0
    for k in range(seq_col):
        final = k == seq_col - 1
        whole = g_rows[k] if k == 0 else tie(g_rows[k], g_in[-1], coef[k])
        if k == 0 and early:
            gn, w_out_part = early
        else:
            w_out_part = w_out_part + matmul(gated[k], whole, 1, 0)
            gn = matmul(out_weight, tie(whole, w_out_part) if final else whole, 1, 1)
        before = (w_out_part,)
        if k == 0:
            dealt_output = dealt_rows(result)
            output_parts = sent_back(dealt_output)
        if final:
            received = other_col(w_out_part[:, width_col:].astype(BF))
            w_out_low = (w_out_part[:, :width_col] + received.astype(F32)).astype(BF)
            w_out_sum = lax.psum(w_out_low, "dp")
            before = (w_out_low,)
        if k > 0:
            scatters.append(to_rows(tie(g_in[-1], *before)))
            scatters[-1].first()
            before = scatters[-1].sent
        gn = tie(gn, *before)
        g, gx, gbc, gdt = scan_backward(
            zx[k], kept_rows[k], entering[k], gn, coef[k], taps, bc_taps, dt_par, heads
        )
        sums = [a + b for a, b in zip(sums, (gx, gbc, gdt), strict=True)]
        if k == 0:
            g = tie(g, *output_parts)
        if k > 0:
            scatters[-1].second(g)
            g = tie(g, *scatters[-1].passed)
        g_in.append(g)

    there, left, right = late_products(scaled, g_in, in_own.T, in_other.T, wide)
    there, left, right, g_in[-1] = tie(
        (there, left, right, g_in[-1]), w_out_sum, *(v for s in scatters for v in s.ended)
    )
    scatters.append(Scatter(left, right))
    scatters[-1].first()
    g_late = g_in[:-1] + [tie(g_in[-1], *scatters[-1].sent)]
    in_low = product(
        "tt", list(zip(scaled, g_late)), TILE, added=other_col(there), columns=width_col, wide=wide
    )
    w_zx = lax.psum(in_low, "dp")
    g_aux = [g[wide:] for g in g_in]
    g_aux[-1] = tie(g_aux[-1], in_low)
    aux_part = sum(matmul(scaled[i], g_aux[i], 0, 1) for i in range(seq_col))
    scatters[-1].second(aux_part)
    aux_half = aux_part[:width_col] + other_col(aux_part[width_col:])
    aux_half = jnp.concatenate(
        [
            aux_half[:, :aux],
            lax.dynamic_update_slice_in_dim(
                jnp.zeros((width_col, head_total), F32),
                aux_half[:, aux : aux + heads],
                row_index * heads,
                1,
            ),
        ],
        axis=1,
    )
    gain_part = jnp.zeros((model_width,), F32)
    g_u = []
    for k in range(seq_col):
        g_scaled, _ = scatters[k].last(*((in_low,) if k < seq_col - 1 else ()))
        gain_part = gain_part + jnp.sum(g_scaled * u[k] * inv_rms[k], axis=0)
        weighted = g_scaled * gain[None, :]
        dot = jnp.sum(weighted * u[k], axis=1, keepdims=True) / model_width
        cube = inv_rms[k] * inv_rms[k] * inv_rms[k]
        g_u.append((g_result[k] + inv_rms[k] * weighted - u[k] * (cube * dot)).astype(BF))
    hidden_parts = sent_back(tie(dealt_rows(g_u), w_zx))
    w_aux = sum_over_row_dp(aux_half)

    gx, gbc, gdt = sums
    flat = jnp.concatenate(
        [gx.reshape(-1), gdt[:, 1:3].reshape(-1), gbc.reshape(-1), loss_part[None]]
    )
    vector = jnp.concatenate([flat, gain_part[:width_col]]) + other_col(
        jnp.concatenate([flat, gain_part[width_col:]])
    )
    own_size = inner * 8 + steps * 2
    vector = jnp.concatenate([vector[:own_size], butterfly(vector[own_size:], "row")])
    vector = butterfly(vector, "dp")
    gx = vector[: inner * 8].reshape(inner, 8)
    gdt = vector[inner * 8 : own_size].reshape(steps, 2)
    shared = vector[own_size:]
    gbc = shared[: aux * 8].reshape(aux, 8)
    loss = shared[aux * 8] * 0.5 / valid_count
    gain_sum = shared[aux * 8 + 1 :]
    return (
        loss,
        in_given_order(output_parts, dest_group),
        in_given_order(hidden_parts, dest_group),
        gain_sum,
        w_zx.astype(F32).reshape(width_col, heads, pair),
        w_aux.astype(F32),
        gx[:, :4].T.reshape(4, heads, head_dim),
        gx[:, 4].reshape(heads, head_dim),
        gbc[:, :4].T,
        gbc[:, 4],
        gdt[:heads, 0],
        gdt[:heads, 1],
        gx[:, 5].reshape(heads, head_dim).sum(axis=1),
        gx[:, 6].reshape(heads, head_dim),
        w_out_sum.astype(F32).reshape(heads, head_dim, width_col),
    )


def solution(mesh):
    placed = (
        P("dp", "row", "col"),
        P("dp", "row", "col"),
        P(),
        P("dp"),
        P("col"),
        P("col", "row", None),
        P("col", None),
        P(None, "row", None),
        P("row", None),
        P(),
        P(),
        P("row"),
        P("row"),
        P("row"),
        P("row", None),
        P("row", None, "col"),
    )
    return jax.shard_map(
        per_device,
        mesh=mesh,
        in_specs=placed,
        out_specs=(
            P(),
            P("dp", "row", "col"),
            P("dp", "row", "col"),
            P("col"),
            P("col", "row", None),
            P("col", None),
            P(None, "row", None),
            P("row", None),
            P(),
            P(),
            P("row"),
            P("row"),
            P("row"),
            P("row", None),
            P("row", None, "col"),
        ),
        check_vma=False,
    )
```

```python
import functools
import jax
import jax.numpy as jnp
from jax import lax
from jax.experimental import pallas as pl
from jax.experimental.pallas import tpu as pltpu
from jax.sharding import PartitionSpec as P

BF = jnp.bfloat16
F32 = jnp.float32
SPAN = 512
PART = 128
TILE = 256
LOG2E = 1.4426950408889634
EDGE = 128
EPSILON = 1e-05


def nn(a, b):
    return lax.dot_general(a, b, (((1,), (0,)), ((), ())), preferred_element_type=F32)


def nt(a, b):
    return lax.dot_general(a, b, (((1,), (1,)), ((), ())), preferred_element_type=F32)


def tn(a, b):
    return lax.dot_general(a, b, (((0,), (0,)), ((), ())), preferred_element_type=F32)


def exact(a, b):
    return lax.dot_general(
        a, b, (((1,), (0,)), ((), ())), precision=lax.Precision.HIGHEST, preferred_element_type=F32
    )


def sigmoid(v):
    return 0.5 * jnp.tanh(0.5 * v) + 0.5


def softplus(v):
    return jnp.maximum(v, 0.0) + jnp.log1p(jnp.exp(-jnp.abs(v)))


def wide(v, span):
    return jnp.concatenate([v] * (span // v.shape[1]), axis=1)


def taps_at(taps_ref, at, span):
    return lambda k: wide(taps_ref[k, at, :], span)


def spread_taps(from_ref, to_ref):
    for k in range(to_ref.shape[0]):
        to_ref[k] = jnp.broadcast_to(from_ref[:, k : k + 1], to_ref.shape[1:])


def move_matrix(ahead):
    rows = lax.broadcasted_iota(jnp.int32, (2 * EDGE, EDGE), 0)
    cols = lax.broadcasted_iota(jnp.int32, (2 * EDGE, EDGE), 1)
    moves = [rows == (cols + k if ahead else cols + EDGE - k) for k in (1, 2, 3)]
    return jnp.concatenate([m.astype(F32).astype(BF) for m in moves], axis=1)


def moved(joined, matrix):
    size = joined.shape[0]
    parts = range(joined.shape[1] // EDGE - 1)
    low = joined.astype(BF)
    stacked = jnp.concatenate([low[:, q * EDGE : (q + 2) * EDGE] for q in parts], axis=0)
    out = nn(stacked, matrix)
    return [
        jnp.concatenate(
            [out[q * size : (q + 1) * size, k * EDGE : (k + 1) * EDGE] for q in parts], axis=1
        )
        for k in range(3)
    ]


def conv_of(before, now, tap, matrix):
    one, two, three = moved(jnp.concatenate([before, now], axis=1), matrix)
    return tap(4) + tap(3) * now + tap(2) * one + tap(1) * two + tap(0) * three


def conv_back(now, after, tap, matrix):
    one, two, three = moved(jnp.concatenate([now, after], axis=1), matrix)
    return tap(3) * now + tap(2) * one + tap(1) * two + tap(0) * three, (one, two, three)


def fold(v):
    total = v[:, :EDGE]
    for k in range(1, v.shape[1] // EDGE):
        total = total + v[:, k * EDGE : (k + 1) * EDGE]
    return total


def lanes(q):
    return slice(q * PART, (q + 1) * PART)


def span_common(bc_before, bc_now, dt_raw, bc_tap, dt_par, matrix):
    pre = conv_of(bc_before, bc_now, bc_tap, matrix)
    sig = sigmoid(pre)
    act = pre * sig
    half = act.shape[0] // 2
    b_t = act[:half].astype(BF)
    c_t = act[half:].astype(BF)
    parts = range(bc_now.shape[1] // PART)
    rows = lax.broadcasted_iota(jnp.int32, (PART, PART), 0)
    cols = lax.broadcasted_iota(jnp.int32, (PART, PART), 1)
    causal = rows <= cols
    steps = softplus(dt_raw + dt_par[:, 0:1])
    rate = -jnp.exp(dt_par[:, 1:2])
    gone = steps * (rate * LOG2E)
    decay = [exact(gone[:, lanes(q)], causal.astype(F32)) for q in parts]
    last = [d[:, PART - 1 :] for d in decay]
    decay_n = [d.T for d in decay]
    left = jnp.concatenate([jnp.exp2(e - d) for e, d in zip(last, decay)], axis=1)
    kept = [jnp.exp2(e) for e in last]
    decay = jnp.concatenate(decay, axis=1)
    grown = jnp.exp2(decay)
    b_n = [b_t[:, lanes(q)].astype(F32).T.astype(BF) for q in parts]
    scores = [jnp.where(causal, nn(b_n[q], c_t[:, lanes(q)]), 0.0) for q in parts]
    return pre, sig, b_t, c_t, b_n, scores, causal, steps, rate, decay, decay_n, grown, left, kept


def forward_kernel(
    heads, zx_ref, bc_ref, dt_ref, taps_ref, bc_taps_ref, dt_par_ref,
    gated_ref, square_ref, enter_ref, x_ref, slope_ref, y_ref,
    state, x_tail, bc_tail, carry, xd_all, tailed, scores_all, x_taps, bc_taps, matrix_ref,
):
    span = zx_ref.shape[1]
    inner = state.shape[0]
    size = inner // heads
    parts = range(span // PART)

    @pl.when(pl.program_id(0) == 0)
    def _():
        state[...] = jnp.zeros_like(state)
        x_tail[...] = jnp.zeros_like(x_tail)
        bc_tail[...] = jnp.zeros_like(bc_tail)
        spread_taps(taps_ref, x_taps)
        spread_taps(bc_taps_ref, bc_taps)
        matrix_ref[...] = move_matrix(False)

    matrix = matrix_ref[...]
    bc_now = bc_ref[...]
    _, _, _, c_t, b_n, scores, _, steps, _, decay, decay_n, grown, left, kept = span_common(
        bc_tail[...], bc_now, dt_ref[...], taps_at(bc_taps, slice(None), span), dt_par_ref[...], matrix
    )
    bc_tail[...] = bc_now[:, span - EDGE :]
    for q in parts:
        scores_all[q] = scores[q]
    for h in range(heads):
        at = slice(h * size, (h + 1) * size)
        x_raw = zx_ref[(2 * h + 1) * size : (2 * h + 2) * size, :]
        pre = conv_of(x_tail[at, :], x_raw, taps_at(x_taps, at, span), matrix)
        x_tail[at, :] = x_raw[:, span - EDGE :]
        sig = sigmoid(pre)
        x = pre * sig
        xd = x * steps[h : h + 1, :]
        x_ref[at, :] = x
        slope_ref[at, :] = sig + x * (1.0 - sig)
        xd_all[at, :] = xd.astype(BF)
        tailed[at, :] = (xd * left[h : h + 1, :]).astype(BF)
    for q in parts:
        entering = state[...].astype(BF)
        enter_ref[q * inner : (q + 1) * inner, :] = entering
        carry[:, lanes(q)] = nn(entering, c_t[:, lanes(q)])
        more = nn(tailed[:, lanes(q)], b_n[q])
        for h in range(heads):
            at = slice(h * size, (h + 1) * size)
            state[at, :] = state[at, :] * kept[q][h : h + 1, :] + more[at, :]
    square = jnp.zeros((size, span), F32)
    for h in range(heads):
        at = slice(h * size, (h + 1) * size)
        z = zx_ref[2 * h * size : (2 * h + 1) * size, :]
        tap = taps_at(x_taps, at, span)
        mixed = []
        for q in parts:
            gap = decay[h : h + 1, lanes(q)] - decay_n[q][:, h : h + 1]
            mixing = scores_all[q] * jnp.exp2(jnp.minimum(gap, 0.0))
            mixed.append(nn(xd_all[at, lanes(q)], mixing.astype(BF)))
        y = jnp.concatenate(mixed, axis=1) + carry[at, :] * grown[h : h + 1, :]
        y_ref[at, :] = y
        y = y + tap(5) * x_ref[at, :]
        gated = y * (z * sigmoid(z))
        square = square + gated * gated
        gated_ref[at, :] = (gated * tap(6)).astype(BF)
    square_ref[...] = jnp.sum(square, axis=0, keepdims=True)


def backward_kernel(
    heads, zx_ref, x_ref, slope_ref, y_ref, bc_ref, bc_before_ref, dt_ref, enter_ref, gn_ref, coef_ref,
    taps_ref, bc_taps_ref, dt_par_ref,
    gzx_ref, gx_sum_ref, gbc_sum_ref, gdt_sum_ref,
    dstate, x_head, bc_head, from_state, grown_g, tailed, x_acc, bc_acc, dt_acc, rsum, dsum,
    dxd_all, gy_all, scores_all, dscores_all, held_all, x_taps, bc_taps_all, matrix_ref,
    back_matrix_ref,
):
    span = zx_ref.shape[1]
    inner = dstate.shape[0]
    size = inner // heads
    half = bc_ref.shape[0] // 2
    wide = zx_ref.shape[0]
    parts = range(span // PART)
    step = pl.program_id(0)
    count = pl.num_programs(0)
    first = step == count - 1

    @pl.when(step == 0)
    def _():
        dstate[...] = jnp.zeros_like(dstate)
        x_head[...] = jnp.zeros_like(x_head)
        bc_head[...] = jnp.zeros_like(bc_head)
        x_acc[...] = jnp.zeros_like(x_acc)
        bc_acc[...] = jnp.zeros_like(bc_acc)
        dt_acc[...] = jnp.zeros_like(dt_acc)
        rsum[...] = jnp.zeros_like(rsum)
        dsum[...] = jnp.zeros_like(dsum)
        held_all[...] = jnp.zeros_like(held_all)
        spread_taps(taps_ref, x_taps)
        spread_taps(bc_taps_ref, bc_taps_all)
        matrix_ref[...] = move_matrix(False)
        back_matrix_ref[...] = move_matrix(True)

    matrix, back_matrix = matrix_ref[...], back_matrix_ref[...]
    live = jnp.where(first, 0.0, 1.0)
    bc_tap = taps_at(bc_taps_all, slice(None), span)
    dt_raw = dt_ref[...]
    bc_now = bc_ref[...]
    (
        bc_pre, bc_sig, b_t, c_t, b_n, scores, causal, steps, rate, decay, decay_n, grown, left, kept
    ) = span_common(bc_before_ref[...] * live, bc_now, dt_raw, bc_tap, dt_par_ref[...], matrix)
    for q in parts:
        scores_all[q] = scores[q]
        dscores_all[q] = jnp.zeros((PART, PART), F32)
    coef = coef_ref[...]
    for h in range(heads):
        at = slice(h * size, (h + 1) * size)
        z = zx_ref[2 * h * size : (2 * h + 1) * size, :]
        tap = taps_at(x_taps, at, span)
        x = x_ref[at, :]
        xd = x * steps[h : h + 1, :]
        xd_low = xd.astype(BF)
        tailed[at, :] = (xd * left[h : h + 1, :]).astype(BF)
        ratios, mixings = [], []
        for q in parts:
            gap = decay[h : h + 1, lanes(q)] - decay_n[q][:, h : h + 1]
            ratios.append(jnp.exp2(jnp.minimum(gap, 0.0)))
            mixings.append((scores_all[q] * ratios[q]).astype(BF))
        grown_h = grown[h : h + 1, :]
        y_scan = y_ref[at, :]
        y = y_scan + tap(5) * x
        zsig = sigmoid(z)
        silu_z = z * zsig
        gated = y * silu_z
        gn = gn_ref[at, :].astype(F32)
        g_gated = tap(6) * gn - gated * coef
        gy = g_gated * silu_z
        gzx_ref[2 * h * size : (2 * h + 1) * size, :] = (
            g_gated * y * (zsig + silu_z * (1.0 - zsig))
        ).astype(BF)
        gy_low = gy.astype(BF)
        gy_all[at, :] = gy_low
        grown_g[at, :] = (gy * grown_h).astype(BF)
        rsum[h : h + 1, :] = jnp.sum(gy_low.astype(F32) * y_scan, axis=0, keepdims=True)
        x_acc[5, at, :] = x_acc[5, at, :] + fold(gy * x)
        x_acc[6, at, :] = x_acc[6, at, :] + fold(gn * gated)
        for q in parts:
            dxd_all[at, lanes(q)] = nt(gy_low[:, lanes(q)], mixings[q])
            dscores_all[q] = dscores_all[q] + tn(xd_low[:, lanes(q)], gy_low[:, lanes(q)]) * ratios[q]
    db, dc, flows = [], [], []
    for q in reversed(parts):
        entering = enter_ref[q * inner : (q + 1) * inner, :]
        leaving = dstate[...].astype(BF)
        from_state[:, lanes(q)] = nn(leaving, b_t[:, lanes(q)])
        low = jnp.where(causal, dscores_all[q], 0.0).astype(BF)
        dc.insert(0, nn(b_t[:, lanes(q)], low) + tn(entering, grown_g[:, lanes(q)]))
        db.insert(0, nt(c_t[:, lanes(q)], low) + tn(leaving, tailed[:, lanes(q)]))
        more = nt(grown_g[:, lanes(q)], c_t[:, lanes(q)])
        for h in range(heads):
            at = slice(h * size, (h + 1) * size)
            passed = dstate[at, :] * kept[q][h : h + 1, :]
            held_all[q, h : h + 1, :] = jnp.sum(passed * entering[at, :].astype(F32), axis=0, keepdims=True)
            dstate[at, :] = passed + more[at, :]
    for h in range(heads):
        at = slice(h * size, (h + 1) * size)
        x_raw = zx_ref[(2 * h + 1) * size : (2 * h + 2) * size, :]
        tap = taps_at(x_taps, at, span)
        x = x_ref[at, :]
        steps_h = steps[h : h + 1, :]
        dx_state = from_state[at, :] * left[h : h + 1, :]
        dxd = dxd_all[at, :] + dx_state
        xd_wide = (x * steps_h).astype(BF).astype(F32)
        rsum[h : h + 1, :] = rsum[h : h + 1, :] - jnp.sum(xd_wide * dxd, axis=0, keepdims=True)
        dsum[h : h + 1, :] = jnp.sum(x * dxd, axis=0, keepdims=True)
        held = jnp.sum(xd_wide * dx_state, axis=0, keepdims=True)
        for q in parts:
            held_all[q, h : h + 1, :] = held_all[q, h : h + 1, :] + held[:, lanes(q)]
        dx = dxd * steps_h + tap(5) * gy_all[at, :].astype(F32)
        gpre = dx * slope_ref[at, :]
        g_raw, later = conv_back(gpre, x_head[at, :], tap, back_matrix)
        x_head[at, :] = gpre[:, :EDGE]
        gzx_ref[(2 * h + 1) * size : (2 * h + 2) * size, :] = g_raw.astype(BF)
        for k, moved_g in enumerate((gpre, *later)):
            x_acc[3 - k, at, :] = x_acc[3 - k, at, :] + fold(moved_g * x_raw)
        x_acc[4, at, :] = x_acc[4, at, :] + fold(gpre)
    gbc = jnp.concatenate([jnp.concatenate(db, axis=1), jnp.concatenate(dc, axis=1)], axis=0)
    gbc = gbc * (bc_sig + bc_pre * bc_sig * (1.0 - bc_sig))
    g_raw, later = conv_back(gbc, bc_head[...], bc_tap, back_matrix)
    bc_head[...] = gbc[:, :EDGE]
    gzx_ref[wide : wide + 2 * half, :] = g_raw.astype(BF)
    for k, moved_g in enumerate((gbc, *later)):
        bc_acc[3 - k] = bc_acc[3 - k] + fold(moved_g * bc_now)
    bc_acc[4] = bc_acc[4] + fold(gbc)
    after = jnp.logical_or(
        jnp.logical_not(causal),
        lax.broadcasted_iota(jnp.int32, (PART, PART), 0) == lax.broadcasted_iota(jnp.int32, (PART, PART), 1),
    ).astype(F32)
    da = jnp.concatenate(
        [
            exact(rsum[:, lanes(q)], after) + jnp.sum(held_all[q], axis=1, keepdims=True)
            for q in parts
        ],
        axis=1,
    )
    g_steps = dsum[...] + rate * da
    g_dt = g_steps * sigmoid(dt_raw + dt_par_ref[:, 0:1])
    gzx_ref[wide + 2 * half :, :] = g_dt.astype(BF)
    dt_acc[:, 1:2] = dt_acc[:, 1:2] + jnp.sum(g_dt, axis=1, keepdims=True)
    dt_acc[:, 2:3] = dt_acc[:, 2:3] + jnp.sum(da * steps * rate, axis=1, keepdims=True)

    @pl.when(first)
    def _():
        for k in range(7):
            gx_sum_ref[:, k : k + 1] = jnp.sum(x_acc[k], axis=1, keepdims=True)
        for k in range(5):
            gbc_sum_ref[:, k : k + 1] = jnp.sum(bc_acc[k], axis=1, keepdims=True)
        gdt_sum_ref[...] = dt_acc[...]


def scan_forward(zx, taps, bc_taps, dt_par, heads, span=SPAN):
    inner = taps.shape[0]
    length = zx.shape[1]
    aux = bc_taps.shape[0]
    steps = dt_par.shape[0]
    states = aux // 2
    body = functools.partial(forward_kernel, heads)
    whole = lambda r, c: pl.BlockSpec((r, c), lambda i: (0, 0))
    return pl.pallas_call(
        body,
        grid=(length // span,),
        in_specs=[
            pl.BlockSpec((2 * inner, span), lambda i: (0, i)),
            pl.BlockSpec((aux, span), lambda i: (2 * inner // aux, i)),
            pl.BlockSpec((steps, span), lambda i: ((2 * inner + aux) // steps, i)),
            whole(inner, 8), whole(aux, 8), whole(steps, 8),
        ],
        out_specs=[
            pl.BlockSpec((inner, span), lambda i: (0, i)),
            pl.BlockSpec((1, span), lambda i: (0, i)),
            pl.BlockSpec((span // PART * inner, states), lambda i: (i, 0)),
        ]
        + [pl.BlockSpec((inner, span), lambda i: (0, i))] * 3,
        out_shape=[
            jax.ShapeDtypeStruct((inner, length), BF),
            jax.ShapeDtypeStruct((1, length), F32),
            jax.ShapeDtypeStruct((length // PART * inner, states), BF),
        ]
        + [jax.ShapeDtypeStruct((inner, length), F32)] * 3,
        scratch_shapes=[
            pltpu.VMEM((inner, states), F32),
            pltpu.VMEM((inner, EDGE), F32),
            pltpu.VMEM((aux, EDGE), F32),
            pltpu.VMEM((inner, span), F32),
            pltpu.VMEM((inner, span), BF),
            pltpu.VMEM((inner, span), BF),
            pltpu.VMEM((span // PART, PART, PART), F32),
            pltpu.VMEM((7, inner, EDGE), F32),
            pltpu.VMEM((5, aux, EDGE), F32),
            pltpu.VMEM((2 * EDGE, 3 * EDGE), BF),
        ],
        compiler_params=pltpu.CompilerParams(vmem_limit_bytes=56 * 2**20),
        name="scan_forward",
    )(zx, zx, zx, taps, bc_taps, dt_par)


def scan_backward(zx, kept, entering, gn, coef, taps, bc_taps, dt_par, heads, span=SPAN):
    inner = taps.shape[0]
    length = zx.shape[1]
    aux = bc_taps.shape[0]
    steps = dt_par.shape[0]
    states = aux // 2
    count = length // span
    ratio = span // EDGE
    body = functools.partial(backward_kernel, heads)
    whole = lambda r, c: pl.BlockSpec((r, c), lambda i: (0, 0))
    rev = lambda i: count - 1 - i
    before = lambda i: jnp.maximum((count - 1 - i) * ratio - 1, 0)
    return pl.pallas_call(
        body,
        grid=(count,),
        in_specs=[
            pl.BlockSpec((2 * inner, span), lambda i: (0, rev(i))),
            pl.BlockSpec((inner, span), lambda i: (0, rev(i))),
            pl.BlockSpec((inner, span), lambda i: (0, rev(i))),
            pl.BlockSpec((inner, span), lambda i: (0, rev(i))),
            pl.BlockSpec((aux, span), lambda i: (2 * inner // aux, rev(i))),
            pl.BlockSpec((aux, EDGE), lambda i: (2 * inner // aux, before(i))),
            pl.BlockSpec((steps, span), lambda i: ((2 * inner + aux) // steps, rev(i))),
            pl.BlockSpec((span // PART * inner, states), lambda i: (rev(i), 0)),
            pl.BlockSpec((inner, span), lambda i: (0, rev(i))),
            pl.BlockSpec((1, span), lambda i: (0, rev(i))),
            whole(inner, 8), whole(aux, 8), whole(steps, 8),
        ],
        out_specs=[
            pl.BlockSpec((2 * inner + aux + steps, span), lambda i: (0, rev(i))),
            whole(inner, 8), whole(aux, 8), whole(steps, EDGE),
        ],
        out_shape=[
            jax.ShapeDtypeStruct((2 * inner + aux + steps, length), BF),
            jax.ShapeDtypeStruct((inner, 8), F32),
            jax.ShapeDtypeStruct((aux, 8), F32),
            jax.ShapeDtypeStruct((steps, EDGE), F32),
        ],
        scratch_shapes=[
            pltpu.VMEM((inner, states), F32),
            pltpu.VMEM((inner, EDGE), F32),
            pltpu.VMEM((aux, EDGE), F32),
            pltpu.VMEM((inner, span), F32),
            pltpu.VMEM((inner, span), BF),
            pltpu.VMEM((inner, span), BF),
            pltpu.VMEM((7, inner, EDGE), F32),
            pltpu.VMEM((5, aux, EDGE), F32),
            pltpu.VMEM((steps, EDGE), F32),
            pltpu.VMEM((steps, span), F32),
            pltpu.VMEM((steps, span), F32),
            pltpu.VMEM((inner, span), F32),
            pltpu.VMEM((inner, span), BF),
            pltpu.VMEM((span // PART, PART, PART), F32),
            pltpu.VMEM((span // PART, PART, PART), F32),
            pltpu.VMEM((span // PART, steps, PART), F32),
            pltpu.VMEM((7, inner, EDGE), F32),
            pltpu.VMEM((5, aux, EDGE), F32),
            pltpu.VMEM((2 * EDGE, 3 * EDGE), BF),
            pltpu.VMEM((2 * EDGE, 3 * EDGE), BF),
        ],
        compiler_params=pltpu.CompilerParams(vmem_limit_bytes=56 * 2**20),
        name="scan_backward",
    )(zx, *kept, zx, zx, zx, entering, gn, coef, taps, bc_taps, dt_par)


def product_kernel(form, count, added, *refs):
    out_ref = refs[-1]
    total = refs[2 * count][...].astype(F32) if added else None
    for i in range(count):
        a, b = refs[2 * i][...], refs[2 * i + 1][...]
        if form == "tt":
            a = a.T
        over = 0 if form == "nn" else 1
        term = lax.dot_general(a, b, (((1,), (over,)), ((), ())), preferred_element_type=F32)
        total = term if total is None else total + term
    out_ref[...] = total.astype(out_ref.dtype)


def product(form, pairs, tile, added=None, dtype=BF, start=0, columns=None, wide=None):
    first, other = pairs[0]
    rows = columns or first.shape[1 if form == "tt" else 0]
    cols = wide or other.shape[1 if form == "nn" else 0]
    operands, specs = [], []
    for a, b in pairs:
        operands += [a, b]
        if form == "tt":
            specs.append(pl.BlockSpec((a.shape[0], tile), lambda i: (0, start // tile + i)))
        else:
            specs.append(pl.BlockSpec((tile, a.shape[1]), lambda i: (i, 0)))
        block = b.shape if form == "nn" else (cols, b.shape[1])
        specs.append(pl.BlockSpec(block, lambda i: (0, 0), pipeline_mode=pl.Buffered(1)))
    if added is not None:
        operands.append(added)
        specs.append(pl.BlockSpec((tile, cols), lambda i: (i, 0)))
    return pl.pallas_call(
        functools.partial(product_kernel, form, len(pairs), added is not None),
        grid=(rows // tile,),
        in_specs=specs,
        out_specs=pl.BlockSpec((tile, cols), lambda i: (i, 0)),
        out_shape=jax.ShapeDtypeStruct((rows, cols), dtype),
        compiler_params=pltpu.CompilerParams(vmem_limit_bytes=56 * 2**20),
        name="product_" + form,
    )(*operands)


def late_kernel(count, wide, first, *refs):
    scaled, g_all, g_tile = refs[:count], refs[count : 2 * count], refs[2 * count]
    weights, outs = refs[2 * count + 1 : 2 * count + 3], refs[2 * count + 3 : 2 * count + 6]
    held, sems = refs[2 * count + 6 : 2 * count + 8], refs[2 * count + 8]
    step = pl.program_id(0)
    copies = [pltpu.make_async_copy(weights[k], held[k], sems.at[k]) for k in range(2)]

    @pl.when(step == 0)
    def _():
        for copy in copies:
            copy.start()

    @pl.when(step < first)
    def _():
        total = None
        for s, g in zip(scaled, g_all):
            term = nt(s[...].T, g[:wide, :])
            total = term if total is None else total + term
        outs[0][...] = total.astype(BF)

    @pl.when(step == first)
    def _():
        for copy in copies:
            copy.wait()

    @pl.when(step >= first)
    def _():
        rows = g_tile[...].T
        for k in range(2):
            outs[1 + k][...] = nn(rows, held[k][...]).astype(BF)


def late_products(scaled, g_in, own, other, wide):
    depth, width = own.shape
    length = scaled[0].shape[0]
    first = width // TILE
    count = len(scaled)
    at = lambda i: jnp.maximum(i - first, 0)
    until = lambda i: jnp.minimum(i, first - 1)
    return pl.pallas_call(
        functools.partial(late_kernel, count, wide, first),
        grid=(first + length // TILE,),
        in_specs=[pl.BlockSpec((length, TILE), lambda i: (0, first + until(i))) for _ in scaled]
        + [pl.BlockSpec(g.shape, lambda i: (0, 0), pipeline_mode=pl.Buffered(1)) for g in g_in]
        + [pl.BlockSpec((depth, TILE), lambda i: (0, at(i)))]
        + [pl.BlockSpec(memory_space=pl.ANY)] * 2,
        out_specs=[
            pl.BlockSpec((TILE, wide), lambda i: (until(i), 0)),
            pl.BlockSpec((TILE, width), lambda i: (at(i), 0)),
            pl.BlockSpec((TILE, width), lambda i: (at(i), 0)),
        ],
        out_shape=[
            jax.ShapeDtypeStruct((width, wide), BF),
            jax.ShapeDtypeStruct((length, width), BF),
            jax.ShapeDtypeStruct((length, width), BF),
        ],
        scratch_shapes=[
            pltpu.VMEM(own.shape, BF),
            pltpu.VMEM(own.shape, BF),
            pltpu.SemaphoreType.DMA((2,)),
        ],
        compiler_params=pltpu.CompilerParams(vmem_limit_bytes=56 * 2**20),
        name="late_products",
    )(*scaled, *g_in, g_in[-1], own, other)


def tie(value, *before):
    return lax.optimization_barrier((value, *before))[0]


def split(v, width):
    rows = []
    rest = v
    for _ in range(3):
        part = lax.reduce_precision(rest, 8, 7)
        rows.append(part.astype(BF))
        rest = rest - part
    return jnp.pad(jnp.stack(rows), ((0, 13), (0, width - v.shape[0])))


def joined(rows, size):
    return jnp.sum(rows[:3, :size].astype(F32), axis=0)


def flip(v, bit):
    return lax.ppermute(v, "row", [(i, i ^ bit) for i in range(4)])


class Gather:
    def __init__(self, x, small=None):
        self.count = lax.axis_size("row")
        self.x, self.small, self.size = x, small, x.shape[0]
        self.sent = x
        if self.count == 4 and small is not None:
            self.sent = jnp.concatenate([x, split(small, x.shape[1])], axis=0)

    def first(self):
        self.got = self.cross = (self.sent,)
        if self.count == 4:
            self.got = (flip(self.sent, 1), flip(self.sent, 2))

    def second(self, *before):
        self.cross = self.passing = self.got
        if self.count == 4:
            from_x, from_y = tie(self.got, *before)
            self.passing = tie((from_y[: self.size // 2], from_x[self.size // 2 :]))
            self.cross = (flip(self.passing[0], 1), flip(self.passing[1], 2))

    def last(self, *before):
        count, x, small, size = self.count, self.x, self.small, self.size
        me = lax.axis_index("row")
        if count != 4:
            if small is not None:
                placed = jnp.zeros((count * size,), F32)
                placed = lax.dynamic_update_slice_in_dim(placed, small, me * size, 0)
                small = butterfly(placed[None, :], "row")
            return lax.all_gather(x, "row", axis=0, tiled=True), small
        from_x, from_y = self.got
        cross_a, cross_b = tie(self.cross, *before)
        out = jnp.zeros((4 * size, x.shape[1]), x.dtype)
        put = lambda o, v, bit, off: lax.dynamic_update_slice(o, v, ((me ^ bit) * size + off, 0))
        out = put(out, x, 0, 0)
        out = put(out, from_x[:size], 1, 0)
        out = put(out, from_y[:size], 2, 0)
        out = put(out, cross_a, 3, 0)
        out = put(out, cross_b[: size // 2], 3, size // 2)
        if small is not None:
            whole = jnp.zeros((1, 4 * size), F32)
            tails = (
                small,
                joined(from_x[size:], size),
                joined(from_y[size:], size),
                joined(cross_b[size // 2 :], size),
            )
            for bit, v in enumerate(tails):
                whole = lax.dynamic_update_slice(whole, v[None, :], (0, (me ^ bit) * size))
            small = whole
        return out, small


class Scatter:
    def __init__(self, left, right, small=None):
        self.count = lax.axis_size("row")
        self.small = small
        if self.count != 4:
            self.sent = (jnp.concatenate([left, right], axis=1),)
            return
        me = lax.axis_index("row")
        self.size, half = left.shape[0] // 4, left.shape[1]
        self.half = half
        self.my_y, self.my_x = me // 2, me % 2
        left = left.reshape(2, 2, self.size, half)
        right = right.reshape(2, 2, self.size, half)
        self.at_x = lambda i: lax.dynamic_index_in_dim(left, i, 1, keepdims=False)
        self.at_y = lambda i: lax.dynamic_index_in_dim(right, i, 0, keepdims=False)
        send_x = self.at_x(1 - self.my_x)
        if small is not None:
            pieces = small.reshape(2, 2, self.size)
            there = lax.dynamic_index_in_dim(pieces, 1 - self.my_x, 1, keepdims=False)
            self.here = lax.dynamic_index_in_dim(pieces, self.my_x, 1, keepdims=False)
            send_x = jnp.concatenate(
                [send_x, jnp.stack([split(there[0], half), split(there[1], half)])], axis=1
            )
        self.sent = (send_x, self.at_y(1 - self.my_y))

    def first(self):
        self.got = self.sent
        if self.count == 4:
            self.got = (flip(self.sent[0], 1), flip(self.sent[1], 2))

    def second(self, *before):
        if self.count != 4:
            self.passed = self.ended = self.sent
            return
        got_x, got_y = tie(self.got, *before)
        pick = lambda v, i: lax.dynamic_index_in_dim(v, i, 0, keepdims=False).astype(F32)
        size = self.size
        both_x = lambda i: pick(self.at_x(self.my_x), i) + pick(got_x[:, :size], i)
        both_y = lambda i: pick(self.at_y(self.my_y), i) + pick(got_y, i)
        pass_x = both_x(1 - self.my_y).astype(BF)
        if self.small is not None:
            little = lambda i: pick(self.here, i) + joined(
                lax.dynamic_index_in_dim(got_x[:, size:], i, 0, keepdims=False), size
            )
            pass_x = jnp.concatenate([pass_x, split(little(1 - self.my_y), self.half)], axis=0)
            self.little = little(self.my_y)
        self.passed = (pass_x, both_y(1 - self.my_x).astype(BF))
        self.left = both_x(self.my_y)
        self.right = both_y(self.my_x)
        self.ended = (flip(self.passed[0], 2), flip(self.passed[1], 1))

    def last(self, *before):
        if self.count != 4:
            total = lax.psum_scatter(self.passed[0], "row", scatter_dimension=0, tiled=True).astype(F32)
            little = None
            if self.small is not None:
                size = total.shape[0]
                little = butterfly(self.small, "row")[0]
                little = lax.dynamic_slice_in_dim(little, lax.axis_index("row") * size, size, 0)
            return total, little
        end_x, end_y = tie(self.ended, *before)
        size = self.size
        left = self.left + end_x[:size].astype(F32)
        right = self.right + end_y.astype(F32)
        little = None
        if self.small is not None:
            little = self.little + joined(end_x[size:], size)
        return jnp.concatenate([left, right], axis=1), little


def butterfly(v, axis):
    count = lax.axis_size(axis)
    bit = 1
    while bit < count:
        v = v + lax.ppermute(v, axis, [(i, i ^ bit) for i in range(count)])
        bit *= 2
    return v


def sum_over_row_dp(v, *before):
    if lax.axis_size("row") != 4:
        return lax.psum(butterfly(v, "row"), "dp")
    me = lax.axis_index("row")
    for bit in (1, 2):
        size = v.shape[0] // 2
        side = me // bit % 2
        away = lax.dynamic_slice_in_dim(v, (1 - side) * size, size, 0)
        keep = lax.dynamic_slice_in_dim(v, side * size, size, 0)
        v = keep + flip(away, bit)
    v = butterfly(tie(v, *before), "dp")
    for bit in (2, 1):
        other = flip(v, bit)
        first = me // bit % 2 == 0
        v = jnp.concatenate([jnp.where(first, v, other), jnp.where(first, other, v)], axis=0)
    return v


def sum_over_row(v):
    if lax.axis_size("row") != 4:
        return butterfly(v, "row")
    return v + flip(v, 1) + flip(v, 2) + flip(v, 3)


def other_col(v):
    return lax.ppermute(v, "col", [(0, 1), (1, 0)])


def dealt_rows(rows):
    half = rows[0].shape[1] // 2
    own = jnp.stack([r[:, :half] for r in rows])
    got = other_col(jnp.stack([r[:, half:] for r in rows]))
    at_start = lax.axis_index("col") == 0
    return jnp.concatenate([jnp.where(at_start, own, got), jnp.where(at_start, got, own)], axis=0)


def sent_back(dealt):
    groups = lax.axis_size("dp")
    me = lax.axis_index("dp")
    parts = []
    for hop in range(groups):
        piece = lax.dynamic_index_in_dim(dealt, (me + hop) % groups, 0, keepdims=False)
        if hop:
            piece = lax.ppermute(piece, "dp", [(i, (i + hop) % groups) for i in range(groups)])
        parts.append(piece)
    return parts


def in_given_order(parts, dest_group):
    groups = lax.axis_size("dp")
    hops = ((lax.axis_index("dp") - dest_group) % groups)[:, None, None]
    out = jnp.where(hops == 0, parts[0][None], jnp.zeros((), BF))
    for hop in range(1, groups):
        out = jnp.where(hops == hop, parts[hop][None], out)
    return out


def matmul(a, b, over_a, over_b):
    return lax.dot_general(a, b, (((over_a,), (over_b,)), ((), ())), preferred_element_type=F32)


def per_device(
    hidden, targets, lengths, dest_group, norm_gain, gate_input_weight, auxiliary_weight,
    conv_x, conv_x_bias, conv_bc, conv_bc_bias, dt_bias, a_log, d_skip, out_gain, output_weight,
):
    row_count = lax.axis_size("row")
    col_count = lax.axis_size("col")
    row_index = lax.axis_index("row")
    col_index = lax.axis_index("col")
    group_index = lax.axis_index("dp")
    seq_group, local_len, width_col = hidden.shape
    heads = gate_input_weight.shape[1]
    pair = gate_input_weight.shape[2]
    head_dim = pair // 2
    inner = heads * head_dim
    wide = heads * pair
    aux = conv_bc.shape[1]
    head_total = auxiliary_weight.shape[1] - aux
    steps = -(-heads // 16) * 16
    seq_col = seq_group // col_count
    model_width = width_col * col_count
    inner_width = inner * row_count
    all_tokens = lengths.shape[0] * local_len * row_count
    valid_count = jnp.sum(lengths).astype(F32)
    group_lengths = lax.dynamic_slice_in_dim(lengths, group_index * seq_group, seq_group, 0)
    own_lengths = lax.dynamic_slice_in_dim(group_lengths, col_index * seq_col, seq_col, 0)

    def widened(v):
        mine = lax.dynamic_slice_in_dim(v, col_index * seq_col, seq_col, 0)
        theirs = lax.dynamic_slice_in_dim(v, (1 - col_index) * seq_col, seq_col, 0)
        return jnp.concatenate([mine, other_col(theirs)], axis=2)

    u_low = widened(hidden)
    gain = jnp.concatenate([norm_gain, other_col(norm_gain)])
    u = [u_low[k].astype(F32) for k in range(seq_col)]
    inv_rms = [lax.rsqrt(jnp.mean(v * v, axis=1, keepdims=True) + EPSILON) for v in u]
    spread = lambda v: lax.all_gather(v, "row", axis=0, tiled=True)
    normed = [(v * r * gain[None, :]).astype(BF) for v, r in zip(u, inv_rms, strict=True)]
    scaled = [spread(normed[0])]
    for v in normed[1:]:
        scaled.append(spread(tie(v, scaled[-1])))
    in_own = tie(
        jnp.concatenate(
            [
                gate_input_weight.reshape(width_col, wide),
                auxiliary_weight[:, :aux],
                lax.dynamic_slice_in_dim(auxiliary_weight, aux + row_index * heads, heads, 1),
                jnp.zeros((width_col, steps - heads), BF),
            ],
            axis=1,
        )
    )
    out_own = output_weight.reshape(inner, width_col)
    column = lambda v: v.reshape(-1, 1)
    taps = jnp.concatenate(
        [
            conv_x.reshape(-1, inner).T,
            column(conv_x_bias),
            column(jnp.repeat(d_skip, head_dim)),
            column(out_gain),
            jnp.zeros((inner, 1), F32),
        ],
        axis=1,
    )
    bc_taps = jnp.concatenate([conv_bc.T, column(conv_bc_bias), jnp.zeros((aux, 3), F32)], axis=1)
    dt_par = jnp.pad(jnp.stack([dt_bias, a_log], axis=1), ((0, steps - heads), (0, 6)))
    targets_there = lax.dynamic_slice_in_dim(targets, (1 - col_index) * seq_col, seq_col, 0)
    in_own, taps, bc_taps, dt_par, targets_there = tie(
        (in_own, taps, bc_taps, dt_par, targets_there)
    )
    in_other, out_other = other_col(in_own), other_col(out_own)

    targets_own = jnp.concatenate(
        [
            lax.dynamic_slice_in_dim(targets, col_index * seq_col, seq_col, 0),
            other_col(targets_there),
        ],
        axis=2,
    )
    positions = row_index * local_len + jnp.arange(local_len, dtype=jnp.int32)

    zx, gated, entering, kept_rows, scatters, gathers = [], [], [], [], [], []
    result, g_result, g_rows, coef = [], [], [], []
    loss_part = jnp.zeros((), F32)

    def finish(k, *before):
        nonlocal loss_part
        summed, total_square = scatters[k].last(*before)
        gate_inv = lax.rsqrt(total_square / inner_width + EPSILON)[:, None]
        branch = summed * gate_inv
        full = u[k] + branch
        valid = (positions < own_lengths[k]).astype(F32)[:, None]
        difference = (full - targets_own[k].astype(F32)) * valid
        loss_part = loss_part + jnp.sum(difference * difference)
        grad = difference * (all_tokens / valid_count)
        result.append(full.astype(BF))
        g_result.append(grad)
        share = gate_inv[:, 0] * gate_inv[:, 0] * jnp.sum(grad * branch, axis=1) / inner_width
        placed = lax.dynamic_update_slice_in_dim(
            jnp.zeros((local_len * row_count,), F32), share, row_index * local_len, 0
        )
        sent = (grad * gate_inv).astype(BF)
        if k < seq_col - 1:
            gathers.append(Gather(sent, share))
            gathers[-1].first()
            return gathers[-1].sent
        coef.append(sum_over_row(placed[None, :]))
        g_rows.append(spread(tie(sent, *g_rows[-1:])))
        return sent

    for k in range(seq_col):
        source = scaled[k] if k == 0 else tie(scaled[k], *scatters[-1].sent)
        projected = matmul(in_own, source[:, :width_col], 0, 1) + matmul(
            in_other, source[:, width_col:], 0, 1
        )
        if k > 0:
            scatters[-1].second(projected)
            projected = tie(projected, *scatters[-1].passed)
            projected = tie(projected, finish(k - 1, projected))
        zx.append(projected)
        g, square, e, *kept = scan_forward(projected, taps, bc_taps, dt_par, heads)
        kept_rows.append(kept)
        gated.append(g)
        entering.append(e)
        left, right = (matmul(g, w, 0, 0).astype(BF) for w in (out_own, out_other))
        scatters.append(Scatter(left, right, square))
        if k > 0:
            gathers[-1].second(left, right)
            scatters[-1].sent = tie(scatters[-1].sent, *gathers[-1].passing)
        scatters[-1].first()
    out_weight = tie(jnp.concatenate(tie((out_own, out_other), *scatters[-1].sent), axis=1))
    scatters[-1].second(out_weight)
    for spread_k in gathers:
        whole, c = spread_k.last()
        g_rows.append(whole)
        coef.append(c)
    early = []
    if seq_col > 1:
        early = [matmul(out_weight, g_rows[0], 1, 1).astype(BF), matmul(gated[0], g_rows[0], 1, 0)]
    finish(seq_col - 1, *early)

    to_rows = lambda g: Scatter(*(matmul(g, w, 0, 1).astype(BF) for w in (in_own, in_other)))
    g_in, scatters = [], []
    sums = [0.0, 0.0, 0.0]
    w_out_part = 0.0
    for k in range(seq_col):
        final = k == seq_col - 1
        whole = g_rows[k] if k == 0 else tie(g_rows[k], g_in[-1], coef[k])
        if k == 0 and early:
            gn, w_out_part = early
        else:
            w_out_part = w_out_part + matmul(gated[k], whole, 1, 0)
            gn = matmul(out_weight, tie(whole, w_out_part) if final else whole, 1, 1).astype(BF)
        before = (w_out_part,)
        if k == 0:
            dealt_output = dealt_rows(result)
            output_parts = sent_back(dealt_output)
        if final:
            received = other_col(w_out_part[:, width_col:].astype(BF))
            w_out_low = (w_out_part[:, :width_col] + received.astype(F32)).astype(BF)
            w_out_sum = lax.psum(w_out_low, "dp")
            before = (w_out_low,)
        if k > 0:
            scatters.append(to_rows(tie(g_in[-1], *before)))
            scatters[-1].first()
            before = scatters[-1].sent
        gn = tie(gn, *before)
        g, gx, gbc, gdt = scan_backward(
            zx[k], kept_rows[k], entering[k], gn, coef[k], taps, bc_taps, dt_par, heads
        )
        sums = [a + b for a, b in zip(sums, (gx, gbc, gdt), strict=True)]
        if k == 0:
            g = tie(g, *output_parts)
        if k > 0:
            scatters[-1].second(g)
            g = tie(g, *scatters[-1].passed)
        g_in.append(g)

    there, left, right = late_products(scaled, g_in, in_own.T, in_other.T, wide)
    there, left, right, g_in[-1] = tie(
        (there, left, right, g_in[-1]), w_out_sum, *(v for s in scatters for v in s.ended)
    )
    scatters.append(Scatter(left, right))
    scatters[-1].first()
    g_late = g_in[:-1] + [tie(g_in[-1], *scatters[-1].sent)]
    in_low = product(
        "tt", list(zip(scaled, g_late)), TILE, added=other_col(there), columns=width_col, wide=wide
    )
    w_zx = lax.psum(in_low, "dp")
    g_aux = [g[wide:] for g in g_in]
    g_aux[-1] = tie(g_aux[-1], in_low)
    aux_part = sum(matmul(scaled[i], g_aux[i], 0, 1) for i in range(seq_col))
    scatters[-1].second(aux_part)
    aux_half = aux_part[:width_col] + other_col(aux_part[width_col:])
    aux_half = jnp.concatenate(
        [
            aux_half[:, :aux],
            lax.dynamic_update_slice_in_dim(
                jnp.zeros((width_col, head_total), F32),
                aux_half[:, aux : aux + heads],
                row_index * heads,
                1,
            ),
        ],
        axis=1,
    )
    gain_part = jnp.zeros((model_width,), F32)
    g_u = []
    for k in range(seq_col):
        g_scaled, _ = scatters[k].last(*((in_low,) if k < seq_col - 1 else ()))
        gain_part = gain_part + jnp.sum(g_scaled * u[k] * inv_rms[k], axis=0)
        weighted = g_scaled * gain[None, :]
        dot = jnp.sum(weighted * u[k], axis=1, keepdims=True) / model_width
        cube = inv_rms[k] * inv_rms[k] * inv_rms[k]
        g_u.append((g_result[k] + inv_rms[k] * weighted - u[k] * (cube * dot)).astype(BF))
    hidden_parts = sent_back(tie(dealt_rows(g_u), w_zx))
    w_aux = sum_over_row_dp(aux_half)

    gx, gbc, gdt = sums
    flat = jnp.concatenate(
        [gx.reshape(-1), gdt[:, 1:3].reshape(-1), gbc.reshape(-1), loss_part[None]]
    )
    vector = jnp.concatenate([flat, gain_part[:width_col]]) + other_col(
        jnp.concatenate([flat, gain_part[width_col:]])
    )
    own_size = inner * 8 + steps * 2
    vector = jnp.concatenate([vector[:own_size], butterfly(vector[own_size:], "row")])
    vector = butterfly(vector, "dp")
    gx = vector[: inner * 8].reshape(inner, 8)
    gdt = vector[inner * 8 : own_size].reshape(steps, 2)
    shared = vector[own_size:]
    gbc = shared[: aux * 8].reshape(aux, 8)
    loss = shared[aux * 8] * 0.5 / valid_count
    gain_sum = shared[aux * 8 + 1 :]
    return (
        loss,
        in_given_order(output_parts, dest_group),
        in_given_order(hidden_parts, dest_group),
        gain_sum,
        w_zx.astype(F32).reshape(width_col, heads, pair),
        w_aux.astype(F32),
        gx[:, :4].T.reshape(4, heads, head_dim),
        gx[:, 4].reshape(heads, head_dim),
        gbc[:, :4].T,
        gbc[:, 4],
        gdt[:heads, 0],
        gdt[:heads, 1],
        gx[:, 5].reshape(heads, head_dim).sum(axis=1),
        gx[:, 6].reshape(heads, head_dim),
        w_out_sum.astype(F32).reshape(heads, head_dim, width_col),
    )


def solution(mesh):
    placed = (
        P("dp", "row", "col"),
        P("dp", "row", "col"),
        P(),
        P("dp"),
        P("col"),
        P("col", "row", None),
        P("col", None),
        P(None, "row", None),
        P("row", None),
        P(),
        P(),
        P("row"),
        P("row"),
        P("row"),
        P("row", None),
        P("row", None, "col"),
    )
    return jax.shard_map(
        per_device,
        mesh=mesh,
        in_specs=placed,
        out_specs=(
            P(),
            P("dp", "row", "col"),
            P("dp", "row", "col"),
            P("col"),
            P("col", "row", None),
            P("col", None),
            P(None, "row", None),
            P("row", None),
            P(),
            P(),
            P("row"),
            P("row"),
            P("row"),
            P("row", None),
            P("row", None, "col"),
        ),
        check_vma=False,
    )
```
